32 devices in a mesh: dp: 4 (over y, x), seq: 2 (over core), tensor: 4 (over z).
Axes of the slice: x: 2, y: 2, z: 4, core: 2. Of those that a mesh axis runs over, the one named last changes fastest.
Arguments:
- tokens: bfloat16 [4, 2048, 1536], P('dp', 'seq'), may hold values from -6 to 6
- positions: int32 [3, 4, 2048], P(None, 'dp', 'seq'), may hold values from 0 to 100, as said below
- time_emb: float32 [4, 6, 1536], P('dp'), may hold values from -4 to 4
- modulation: float32 [6, 1536], replicated, may hold values from -4 to 4
- context: bfloat16 [512, 1536], replicated, may hold values from -6 to 6
- adapter_index: int32 [4], P('dp'), may hold values from 0 to 7
- self_qkv: bfloat16 [3, 1536, 1536], P(None, None, 'tensor'), may hold values from -0.15625 to 0.15625
- self_bias: bfloat16 [3, 1536], P(None, 'tensor'), may hold values from -2 to 2
- self_gain: bfloat16 [2, 1536], P(None, 'tensor'), may hold values from 0.25 to 1.75
- self_out: bfloat16 [1536, 1536], P('tensor'), may hold values from -2.5 to 2.5
- cross_qkv: bfloat16 [3, 1536, 1536], P(None, None, 'tensor'), may hold values from -0.15625 to 0.15625
- cross_bias: bfloat16 [3, 1536], P(None, 'tensor'), may hold values from -2 to 2
- cross_gain: bfloat16 [2, 1536], P(None, 'tensor'), may hold values from 0.25 to 1.75
- cross_out: bfloat16 [1536, 1536], P('tensor'), may hold values from -2.5 to 2.5
- cross_norm_gain: float32 [1536], replicated, may hold values from 0.25 to 1.75
- cross_norm_bias: float32 [1536], replicated, may hold values from -2 to 2
- ffn_in: bfloat16 [1536, 8960], P(None, 'tensor'), may hold values from -0.15625 to 0.15625
- ffn_bias: bfloat16 [8960], P('tensor'), may hold values from -2 to 2
- ffn_out: bfloat16 [8960, 1536], P('tensor'), may hold values from -0.0625 to 0.0625
- out_bias: bfloat16 [3, 1536], replicated, may hold values from -2 to 2
- col_down: bfloat16 [8, 6, 1536, 16], replicated, may hold values from -0.15625 to 0.15625
- col_up: bfloat16 [8, 6, 16, 1536], P(None, None, None, 'tensor'), may hold values from -0.75 to 0.75
- ffn1_down: bfloat16 [8, 1536, 16], replicated, may hold values from -0.15625 to 0.15625
- ffn1_up: bfloat16 [8, 16, 8960], P(None, None, 'tensor'), may hold values from -0.75 to 0.75
- row_down: bfloat16 [8, 2, 1536, 16], P(None, None, 'tensor'), may hold values from -1.25 to 1.25
- row_up: bfloat16 [8, 2, 16, 1536], replicated, may hold values from -0.75 to 0.75
- ffn2_down: bfloat16 [8, 8960, 16], P(None, 'tensor'), may hold values from -0.0625 to 0.0625
- ffn2_up: bfloat16 [8, 16, 1536], replicated, may hold values from -0.75 to 0.75
- out_grad: bfloat16 [4, 2048, 1536], P('dp', 'seq'), may hold values from -6 to 6
Outputs:
- output: bfloat16 [4, 2048, 1536], P('dp', 'seq')
- input_grad: bfloat16 [4, 2048, 1536], P('dp', 'seq')
- context_grad: float32 [512, 1536], replicated
- col_down_grad: float32 [8, 6, 1536, 16], replicated
- col_up_grad: float32 [8, 6, 16, 1536], P(None, None, None, 'tensor')
- ffn1_down_grad: float32 [8, 1536, 16], replicated
- ffn1_up_grad: float32 [8, 16, 8960], P(None, None, 'tensor')
- row_down_grad: float32 [8, 2, 1536, 16], P(None, None, 'tensor')
- row_up_grad: float32 [8, 2, 16, 1536], replicated
- ffn2_down_grad: float32 [8, 8960, 16], P(None, 'tensor')
- ffn2_up_grad: float32 [8, 16, 1536], replicated
The draws below stay inside these ranges and needn't reach their ends.
Inputs may be any that keep to these rules, and one draw needn't show every extreme that they name: positions[0], positions[1], positions[2] are a token's frame, row and column in its latent's grid of 2 x 32 x 32 (tokens in the order frame, row, column), each times a stride of 1 to 3 plus an offset of 0 to 7, stride and offset fixed for a latent and a component.
All inputs are finite; a program needn't handle non-finite values.
Results may differ from the reference program's by a relative error of at most 0.025.
Values may be sent and summed in bfloat16 or wider, within the bound.
No kernel may reach another device: no remote copies, remote signals or barrier semaphores. Data moves between devices by JAX's collectives and lax.ppermute only.
A program may use at most 256 MiB of HBM per device.

```python
import jax
import jax.numpy as jnp
from jax import lax

D = 1536
HEADS = 12
HEAD_DIM = 128
FF = 8960
CTX = 512
RANK = 16
ADAPTERS = 8
GH = 32
GW = 32
SEQLEN = 2048
LATENTS = 4
N_TENSOR = 4


def draw_positions(key, part):
    key = jax.random.fold_in(key, 11)
    offsets = jax.random.randint(key, (3, LATENTS), 0, 8)
    strides = jax.random.randint(jax.random.fold_in(key, 2), (3, LATENTS), 1, 4)
    chosen = jax.random.randint(jax.random.fold_in(key, 1), (), 0, LATENTS)
    lanes = jnp.arange(LATENTS)
    offsets = jnp.where(lanes[None, :] == chosen, 7, offsets)
    strides = jnp.where(lanes[None, :] == chosen, 3, strides)
    offsets = jnp.where(lanes[None, :] == (chosen + 1) % LATENTS, 0, offsets)
    token_ids = jnp.arange(SEQLEN)
    grid = jnp.stack([token_ids // (GH * GW), token_ids // GW % GH, token_ids % GW])
    return (grid[:, None, :] * strides[:, :, None] + offsets[:, :, None]).astype(jnp.int32)


def touch_ends(array, key, low, top_value):
    longest = array.shape.index(max(array.shape))
    spots = []
    for shift in (0, 1):
        where = [jax.random.randint(jax.random.fold_in(key, axis), (), 0, length) for axis, length in enumerate(array.shape)]
        where[longest] = (where[longest] + shift) % array.shape[longest]
        spots.append(tuple(where))
    return array.at[spots[0]].set(low).at[spots[1]].set(top_value)


def level_of(rng, shape, shards, low, high):
    loudness, own = 1.0, jax.random.fold_in(rng, 6)
    for axis_at, blocks in shards:
        heights = jnp.exp(jax.random.uniform(jax.random.fold_in(own, axis_at), (blocks,), jnp.float32, low / len(shards), high / len(shards)))
        loudness = loudness * jnp.repeat(heights, shape[axis_at] // blocks).reshape([-1 if axis == axis_at else 1 for axis in range(len(shape))])
    return loudness


def noise(own_key, extent, deviation, reach, cuts=(), held_as=jnp.bfloat16):
    values = jax.random.normal(own_key, extent, jnp.float32) * deviation
    if len(cuts) > 0:
        values = level_of(own_key, extent, cuts, -0.22, 0.18) * values
    return jnp.clip(values, min=-reach, max=reach).astype(held_as)


def setup_inputs(seed: int = 0) -> dict:
    keys = jax.random.split(jax.random.key(seed), 30)
    return {
        "tokens": noise(keys[0], (LATENTS, SEQLEN, D), 1.0, 6.0, ((0, 4), (1, 2))),
        "positions": draw_positions(jax.random.fold_in(keys[29], 71), 0),
        "time_emb": noise(keys[2], (LATENTS, 6, D), 0.5, 4.0, ((0, 4),), jnp.float32),
        "modulation": noise(keys[3], (6, D), 0.5, 4.0, (), jnp.float32),
        "context": noise(keys[4], (CTX, D), 1.0, 6.0),
        "adapter_index": touch_ends(jax.random.randint(keys[5], (LATENTS,), 0, ADAPTERS), jax.random.fold_in(keys[5], 1), 0, ADAPTERS - 1).astype(jnp.int32),
        "self_qkv": noise(keys[6], (3, D, D), D ** -0.5, 0.15625, ((2, 4),)),
        "self_bias": noise(keys[7], (3, D), 0.3, 2.0, ((1, 4),)),
        "self_gain": jnp.clip(1.0 + 0.15 * jax.random.normal(keys[8], (2, D), jnp.float32), 0.25, 1.75).astype(jnp.bfloat16),
        "self_out": noise(keys[9], (D, D), (max(D // 256, 1)) ** -0.5, 2.5, ((0, 4),)),
        "cross_qkv": noise(keys[10], (3, D, D), D ** -0.5, 0.15625, ((2, 4),)),
        "cross_bias": noise(keys[11], (3, D), 0.3, 2.0, ((1, 4),)),
        "cross_gain": jnp.clip(1.0 + 0.15 * jax.random.normal(keys[12], (2, D), jnp.float32), 0.25, 1.75).astype(jnp.bfloat16),
        "cross_out": noise(keys[13], (D, D), (max(D // 256, 1)) ** -0.5, 2.5, ((0, 4),)),
        "cross_norm_gain": jnp.clip(1.0 + 0.15 * jax.random.normal(keys[14], (D,), jnp.float32), 0.25, 1.75),
        "cross_norm_bias": noise(keys[15], (D,), 0.3, 2.0, (), jnp.float32),
        "ffn_in": noise(keys[16], (D, FF), D ** -0.5, 0.15625, ((1, 4),)),
        "ffn_bias": noise(keys[17], (FF,), 0.3, 2.0, ((0, 4),)),
        "ffn_out": noise(keys[18], (FF, D), FF ** -0.5, 0.0625, ((0, 4),)),
        "out_bias": noise(keys[19], (3, D), 0.3, 2.0),
        "col_down": noise(keys[20], (ADAPTERS, 6, D, RANK), D ** -0.5, 0.15625),
        "col_up": noise(keys[21], (ADAPTERS, 6, RANK, D), 64 ** -0.5, 0.75, ((3, 4),)),
        "ffn1_down": noise(keys[22], (ADAPTERS, D, RANK), D ** -0.5, 0.15625),
        "ffn1_up": noise(keys[23], (ADAPTERS, RANK, FF), 64 ** -0.5, 0.75, ((2, 4),)),
        "row_down": noise(keys[24], (ADAPTERS, 2, D, RANK), (max(D // 64, 1)) ** -0.5, 1.25, ((2, 4),)),
        "row_up": noise(keys[25], (ADAPTERS, 2, RANK, D), 64 ** -0.5, 0.75),
        "ffn2_down": noise(keys[26], (ADAPTERS, FF, RANK), FF ** -0.5, 0.0625, ((1, 4),)),
        "ffn2_up": noise(keys[27], (ADAPTERS, RANK, D), 64 ** -0.5, 0.75),
        "out_grad": noise(keys[28], (LATENTS, SEQLEN, D), 1.0, 6.0, ((0, 4), (1, 2))),
    }


@jax.custom_vjp
def low(v):
    return lax.optimization_barrier(v.astype(jnp.bfloat16)).astype(jnp.float32)

@jax.custom_vjp
def low_back(v):
    return v

def low_keep(v):
    return (low(v), None)

def low_pass(kept, grad):
    return (grad,)

def back_keep(v):
    return (v, None)

def back_low(kept, grad):
    return (low(grad),)
low.defvjp(low_keep, low_pass)
low_back.defvjp(back_keep, back_low)
epsilon = 1e-06
highest = lax.Precision.HIGHEST

def rounded_both(values):
    return low(low_back(values))

def matmul(left, right):
    return jnp.dot(left, right, precision=highest)

def layer_norm(values):
    centered = values - lax.optimization_barrier(jnp.mean(values, axis=-1, keepdims=True))
    return centered * lax.rsqrt(lax.optimization_barrier(jnp.mean(centered * centered, axis=-1, keepdims=True)) + epsilon)

def rms_norm(values, gain_row):
    return values * lax.rsqrt(lax.optimization_barrier(jnp.mean(values * values, axis=-1, keepdims=True)) + epsilon) * gain_row

def rope_angles(grid_pos, head_width):
    one_sixth = head_width // 6
    pair_counts = [(head_width - 4 * one_sixth) // 2, one_sixth, one_sixth]
    pieces = []
    for component in range(3):
        pair_count = pair_counts[component]
        frequency = 1.0 / 10000.0 ** (jnp.arange(pair_count, dtype=jnp.float32) / pair_count)
        pieces.append(grid_pos[component].astype(jnp.float32)[:, None] * frequency[None, :])
    return jnp.concatenate(pieces, axis=1)

def rotate(values, angles):
    full_shape = values.shape
    paired = values.reshape(full_shape[0], full_shape[1], full_shape[2] // 2, 2)
    cosine = jnp.cos(angles)[:, None, :]
    sine_part = jnp.sin(angles)[:, None, :]
    even_part = paired[..., 0]
    odd_part = paired[..., 1]
    turned = jnp.stack([even_part * cosine - odd_part * sine_part, even_part * sine_part + odd_part * cosine], axis=-1)
    return turned.reshape(full_shape)

def attend(queries, key_rows, value_rows):
    score_scale = HEAD_DIM ** (-0.5)
    length = queries.shape[0]
    stride = min(512, length)

    def one_block(query_block):
        scores = low_back(jnp.einsum('qhd,khd->hqk', query_block, key_rows, precision=highest) * score_scale)
        weights = jax.nn.softmax(scores, axis=-1)
        return jnp.einsum('hqk,khd->qhd', low(weights), value_rows, precision=highest)
    blocks = queries.reshape(length // stride, stride, queries.shape[1], queries.shape[2])
    return lax.map(jax.checkpoint(one_block), blocks).reshape(queries.shape)

def columns(held_inputs, weight, bias_row, down, up):
    width = weight.shape[1] // N_TENSOR
    outputs = []
    for member in range(N_TENSOR):
        latent = rounded_both(matmul(held_inputs[member], down))
        start = member * width
        outputs.append(matmul(held_inputs[member], weight[:, start:start + width]) + matmul(latent, up[:, start:start + width]) + bias_row[start:start + width])
    return jnp.concatenate(outputs, axis=1)

def rows_out(inputs, weight, down, up):
    width = weight.shape[0] // N_TENSOR
    summed = jnp.zeros((inputs.shape[0], weight.shape[1]), jnp.float32)
    for member in range(N_TENSOR):
        start = member * width
        piece = inputs[:, start:start + width]
        latent = rounded_both(matmul(piece, down[start:start + width]))
        summed = summed + low(matmul(piece, weight[start:start + width]) + matmul(latent, up))
    return low_back(summed)

def block(latent_x, latent_e, index, grid_pos, context_values, frozen, adapters):
    modulation, self_qkv, self_bias, self_gain, self_out, cross_qkv, cross_bias, cross_gain, cross_out, norm_gain, norm_bias, ffn_in, ffn_bias, ffn_out, out_bias = frozen
    col_down, col_up, ffn1_down, ffn1_up, row_down, row_up, ffn2_down, ffn2_up = adapters
    length = latent_x.shape[0]
    modes = modulation + latent_e
    downs = col_down[index]
    ups = col_up[index]
    row_downs = row_down[index]
    row_ups = row_up[index]
    angles = rope_angles(grid_pos, HEAD_DIM)
    hidden_one = low(layer_norm(latent_x) * (1.0 + modes[1]) + modes[0])
    held = [low_back(hidden_one) for member in range(N_TENSOR)]
    query_pre = low_back(columns(held, self_qkv[0], self_bias[0], downs[0], ups[0]))
    key_pre = low_back(columns(held, self_qkv[1], self_bias[1], downs[1], ups[1]))
    value_self = rounded_both(columns(held, self_qkv[2], self_bias[2], downs[2], ups[2]))
    query_rot = low(rotate(rms_norm(query_pre, self_gain[0]).reshape(length, HEADS, HEAD_DIM), angles))
    key_rot = low(rotate(rms_norm(key_pre, self_gain[1]).reshape(length, HEADS, HEAD_DIM), angles))
    mixed_self = rounded_both(attend(query_rot, key_rot, value_self.reshape(length, HEADS, HEAD_DIM)).reshape(length, D))
    after_self = latent_x + (rows_out(mixed_self, self_out, row_downs[0], row_ups[0]) + out_bias[0]) * modes[2]
    hidden_three = low(layer_norm(after_self) * norm_gain + norm_bias)
    held = [low_back(hidden_three) for member in range(N_TENSOR)]
    context_held = [context_values for member in range(N_TENSOR)]
    query_cross = low(rms_norm(low_back(columns(held, cross_qkv[0], cross_bias[0], downs[3], ups[3])), cross_gain[0]))
    key_cross = low(rms_norm(low_back(columns(context_held, cross_qkv[1], cross_bias[1], downs[4], ups[4])), cross_gain[1]))
    value_cross = rounded_both(columns(context_held, cross_qkv[2], cross_bias[2], downs[5], ups[5]))
    mixed_cross = rounded_both(attend(query_cross.reshape(length, HEADS, HEAD_DIM), key_cross.reshape(CTX, HEADS, HEAD_DIM), value_cross.reshape(CTX, HEADS, HEAD_DIM)).reshape(length, D))
    after_cross = after_self + rows_out(mixed_cross, cross_out, row_downs[1], row_ups[1]) + out_bias[1]
    hidden_two = low(layer_norm(after_cross) * (1.0 + modes[4]) + modes[3])
    held = [low_back(hidden_two) for member in range(N_TENSOR)]
    gated = low(jax.nn.gelu(low_back(columns(held, ffn_in, ffn_bias, ffn1_down[index], ffn1_up[index])), approximate=True))
    feed = rows_out(gated, ffn_out, ffn2_down[index], ffn2_up[index]) + out_bias[2]
    return after_cross + feed * modes[5]

def reference(tokens, positions, time_emb, modulation, context, adapter_index, self_qkv, self_bias, self_gain, self_out, cross_qkv, cross_bias, cross_gain, cross_out, cross_norm_gain, cross_norm_bias, ffn_in, ffn_bias, ffn_out, out_bias, col_down, col_up, ffn1_down, ffn1_up, row_down, row_up, ffn2_down, ffn2_up, out_grad):
    frozen = tuple((weight.astype(jnp.float32) for weight in (modulation, self_qkv, self_bias, self_gain, self_out, cross_qkv, cross_bias, cross_gain, cross_out, cross_norm_gain, cross_norm_bias, ffn_in, ffn_bias, ffn_out, out_bias)))
    adapter_set = tuple((table.astype(jnp.float32) for table in (col_down, col_up, ffn1_down, ffn1_up, row_down, row_up, ffn2_down, ffn2_up)))
    grid_all = jnp.transpose(positions, (1, 0, 2))
    emb_all = time_emb.astype(jnp.float32)

    def forward(inputs, context_values, adapters):

        def per_latent(entry):
            latent_x, latent_e, index, grid_pos = entry
            return block(latent_x, latent_e, index, grid_pos, context_values, frozen, adapters)
        return lax.map(per_latent, (inputs, emb_all, adapter_index, grid_all))
    outputs, pullback = jax.vjp(forward, tokens.astype(jnp.float32), context.astype(jnp.float32), adapter_set)
    grad_inputs, grad_context, grad_tables = pullback(out_grad.astype(jnp.float32))
    return (outputs.astype(jnp.bfloat16), grad_inputs.astype(jnp.bfloat16), grad_context, grad_tables[0], grad_tables[1], grad_tables[2], grad_tables[3], grad_tables[4], grad_tables[5], grad_tables[6], grad_tables[7])
```

```python
import functools
import math

import jax
import jax.numpy as jnp
import numpy as np
from jax import lax
from jax.experimental import pallas as pl
from jax.experimental.pallas import tpu as pltpu
from jax.sharding import PartitionSpec as P

F32 = jnp.float32
BF16 = jnp.bfloat16
HEAD_DIM = 128
EPS = 1e-06
LOG2E = 1.4426950408889634
SCALE = HEAD_DIM ** (-0.5)
VMEM_LIMIT = 58 * 1024 * 1024
GELU_C = math.sqrt(2.0 / math.pi)
M0, M1, M2, M3, M4, M5, B0, B1, B2, CG, CB = range(11)
AT_T, AT_S, ADAPTER, PART, SLOTS = range(5)


def nn(left, right):
    return jnp.dot(left, right, preferred_element_type=F32)


def nt(left, right):
    return lax.dot_general(left, right, (((1,), (1,)), ((), ())), preferred_element_type=F32)


def row_total(values):
    ones = jnp.ones((8, values.shape[1]), BF16)
    high = values.astype(BF16)
    return nt(ones, high) + nt(ones, (values - high.astype(F32)).astype(BF16))


def mean(values):
    return jnp.mean(values, axis=-1, keepdims=True)


def normalize(values):
    centered = values - mean(values)
    inverse = lax.rsqrt(mean(centered * centered) + EPS)
    return centered * inverse, inverse


def normalize_back(normed, inverse, upstream):
    return inverse * (upstream - mean(upstream) - normed * mean(upstream * normed))


def pair_swap(values):
    width = values.shape[1]
    lane = lax.broadcasted_iota(jnp.int32, values.shape, 1)
    return jnp.where(lane % 2 == 0, pltpu.roll(values, width - 1, 1), pltpu.roll(values, 1, 1))


def rope(values, cosine, sine):
    return values * cosine + pair_swap(values) * sine


def rope_back(values, cosine, sine):
    return values * cosine - pair_swap(values) * sine


def heads_of(array, count):
    return [array[:, h * HEAD_DIM : (h + 1) * HEAD_DIM] for h in range(count)]


def whole(shape):
    return pl.BlockSpec(shape, lambda *_: (0,) * len(shape))


def run_kernel(body, meta, ins, outs, grid=(1,), scratch=(), us=1.0, aliases=None, after=()):
    count = len(ins)
    ins = list(ins) + [(a, pl.BlockSpec(memory_space=pl.ANY)) for a in after]
    arrays = [a for a, _ in ins]
    moved = sum(math.prod(a.shape) * a.dtype.itemsize for a in arrays[:count]) + sum(
        math.prod(s.shape) * s.dtype.itemsize for s, _ in outs
    )

    def reading(meta_ref, *refs):
        return body(meta_ref, *refs[:count], *refs[len(arrays) :])

    return pl.pallas_call(
        reading,
        grid_spec=pltpu.PrefetchScalarGridSpec(
            num_scalar_prefetch=1,
            grid=grid,
            in_specs=[s for _, s in ins],
            out_specs=[s for _, s in outs],
            scratch_shapes=list(scratch),
        ),
        out_shape=[s for s, _ in outs],
        input_output_aliases=aliases or {},
        compiler_params=pltpu.CompilerParams(vmem_limit_bytes=VMEM_LIMIT),
        cost_estimate=pl.CostEstimate(
            flops=int(us * 1.15e9), bytes_accessed=int(min(moved, us * 2e6)), transcendentals=0
        ),
    )(meta, *arrays)


def sds(shape, dtype):
    return jax.ShapeDtypeStruct(shape, dtype)


def qkv_kernel(head_count, meta, tok, mod, emb, b_out, cg, cb, w, up, dn, bias, gain, cos, sin, ctx_ssq, *outs):
    y1, lat_t, pre_q, pre_k, raw_q, kv, ssq, vec, up_s = outs
    width = head_count * HEAD_DIM
    rank = up.shape[2]
    modes = mod[...] + emb[...]

    @pl.when(pl.program_id(0) == 0)
    def _():
        row = lax.broadcasted_iota(jnp.int32, modes.shape, 0)
        rows = [modes + jnp.where((row == 1) | (row == 4), 1.0, 0.0), b_out[...].astype(F32), cg[...], cb[...]]
        vec[...] = jnp.concatenate(rows + [jnp.zeros((5, modes.shape[1]), F32)], axis=0)
        up_s[...] = jnp.zeros_like(up_s)
        for j in range(3):
            up_s[j * rank : (j + 1) * rank, j * width : (j + 1) * width] = up[0, j]

    normed, _ = normalize(tok[...].astype(F32))
    y = (normed * (1.0 + modes[1:2, :]) + modes[0:1, :]).astype(BF16)
    y1[...] = y
    down = jnp.concatenate([dn[0, j] for j in range(3)], axis=0)
    lat = nt(y, down).astype(BF16)
    lat_t[...] = nt(down, y).astype(BF16)
    totals = []
    for j in range(3):
        lanes = slice(j * width, (j + 1) * width)
        u = nn(y, w[j]) + nn(lat, up_s[:, lanes]) + bias[j : j + 1, :].astype(F32)
        if j == 2:
            kv[:, width:] = u.astype(BF16)
            continue
        (pre_q, pre_k)[j][...] = u.astype(BF16)
        totals.append(row_total(u * u))
        scaled = u * gain[j : j + 1, :].astype(F32)
        for h in range(head_count):
            lanes = slice(h * HEAD_DIM, (h + 1) * HEAD_DIM)
            (raw_q, kv)[j][:, lanes] = rope(scaled[:, lanes], cos[...], sin[...]).astype(BF16)
    row = lax.broadcasted_iota(jnp.int32, totals[0].shape, 0)
    ssq[...] = jnp.where(row == 0, totals[0], jnp.where(row == 1, totals[1], ctx_ssq[...]))


def attention_kernel(groups, meta, raw_q, st, st_own, st_sib, k_own, k_sib, v_own, v_sib, *outs):
    blocks, out, lse, kn, vt = outs[:groups], outs[groups], outs[groups + 1], outs[groups + 2], outs[groups + 3]
    count = k_own.shape[0]
    step = pl.program_id(1)

    @pl.when(step == 0)
    def _():
        for at, (k, s, v) in enumerate(((k_own, st_own, v_own), (k_sib, st_sib, v_sib))):
            rows = slice(at * count, (at + 1) * count)
            kn[rows, :] = (k[...].astype(F32) * s[...].T[:, 1:2]).astype(BF16)
            vt[:, rows] = v[...].astype(F32).T.astype(BF16)

    q = (raw_q[...].astype(F32) * (st[...].T[:, 0:1] * (SCALE * LOG2E))).astype(BF16)
    scores = nt(kn[...], q)
    highest = jnp.max(scores, axis=0, keepdims=True)
    e = jnp.exp2(scores - highest)
    total = jnp.sum(e, axis=0, keepdims=True)
    mixed = (nn(vt[...], e.astype(BF16)) / total).T.astype(BF16)
    out[...] = mixed
    for r in range(groups):

        @pl.when(step == r)
        def _(r=r):
            blocks[r][...] = mixed

    lse[...] = jnp.broadcast_to(highest + jnp.log2(total), lse.shape)


def attention_back_kernel(groups, first, meta, raw_q, st, st_own, st_sib, k_own, k_sib, v_own, v_sib, out, lse, *rest):
    grads, rest = rest[:groups], rest[groups:]
    if not first:
        stat_in, cross_in = rest[:2]
        rest = rest[2:]
    dq, dkv_own, dkv_sib, stat, cross, kn, knt, vn, dk_acc, dv_acc, g_s = rest
    count = k_own.shape[0]
    size = raw_q.shape[0]
    step = pl.program_id(0)

    @pl.when(step == 0)
    def _():
        for at, (k, s, v) in enumerate(((k_own, st_own, v_own), (k_sib, st_sib, v_sib))):
            rows = slice(at * count, (at + 1) * count)
            scaled = k[...].astype(F32) * s[...].T[:, 1:2]
            kn[rows, :] = scaled.astype(BF16)
            knt[:, rows] = scaled.T.astype(BF16)
            vn[rows, :] = v[...]
        dk_acc[...] = jnp.zeros_like(dk_acc)
        dv_acc[...] = jnp.zeros_like(dv_acc)
        stat[...] = jnp.zeros_like(stat) if first else stat_in[...]
        cross[...] = jnp.zeros_like(cross) if first else cross_in[...]

    for r in range(groups):

        @pl.when(step == r)
        def _(r=r):
            g_s[...] = grads[r][...]

    raw = raw_q[...].astype(F32)
    q = (raw * (st[...].T[:, 0:1] * (SCALE * LOG2E))).astype(BF16)
    g = g_s[...]
    delta = row_total(g.astype(F32) * out[...].astype(F32))[0:1, :]
    p = jnp.exp2(nt(kn[...], q) - lse[0:1, :])
    dv_acc[...] += nn(p.astype(BF16), g)
    ds = (p * (nt(vn[...], g) - delta)).astype(BF16)
    dk_acc[...] += nn(ds, q)
    dqs = nn(knt[...], ds).T * SCALE
    dq[...] = dqs
    lanes = pl.ds(pl.multiple_of(lax.rem(meta[AT_T] + step, groups) * size, size), size)
    total = row_total(dqs * raw)
    stat[:, lanes] += jnp.where(lax.broadcasted_iota(jnp.int32, total.shape, 0) == 0, total, 0.0)

    @pl.when(step == pl.num_programs(0) - 1)
    def _():
        for at, (k, dkv, sums) in enumerate(((k_own, dkv_own, stat), (k_sib, dkv_sib, cross))):
            rows = slice(at * count, (at + 1) * count)
            dk = dk_acc[rows, :] * (1.0 / LOG2E)
            dkv[:, :HEAD_DIM] = dk.astype(dkv.dtype)
            dkv[:, HEAD_DIM:] = dv_acc[rows, :].astype(dkv.dtype)
            all_k = row_total(dk * k[...].astype(F32))
            sums[...] += jnp.where(lax.broadcasted_iota(jnp.int32, all_k.shape, 0) == 1, all_k, 0.0)


def qkv_back_kernel(head_count, at, meta, *refs):
    n = head_count
    dq, dkv, dkv_in = (refs[j * n : (j + 1) * n] for j in range(3))
    refs = refs[3 * n :]
    pre_q, pre_k, st, st_back, gain_in, cos, sin, w, up_in, dn_in, tok, vec, y1, lat_t, dx1 = refs[:15]
    packed_in = refs[15] if at else None
    part, packed, up = refs[-3:]
    inverse, cubed = st[...].T, st_back[...].T
    c, s = cos[...], sin[...]
    width = n * HEAD_DIM
    rank = up_in.shape[2]
    d = tok.shape[1]
    gain = gain_in[...].astype(F32)
    up[...] = jnp.zeros_like(up)
    for j in range(3):
        up[j * rank : (j + 1) * rank, j * width : (j + 1) * width] = up_in[0, j]
    dn = jnp.concatenate([dn_in[0, j] for j in range(3)], axis=0)
    dk = [a[:, :HEAD_DIM] + b[:, :HEAD_DIM].astype(F32) for a, b in zip(dkv, dkv_in)]
    dv = [a[:, HEAD_DIM:] + b[:, HEAD_DIM:].astype(F32) for a, b in zip(dkv, dkv_in)]
    grads = [
        jnp.concatenate([rope_back(ref[...], c, s) for ref in dq], axis=1),
        jnp.concatenate([rope_back(a, c, s) for a in dk], axis=1),
        jnp.concatenate(dv, axis=1).astype(BF16),
    ]
    for j, pre in enumerate((pre_q, pre_k)):
        grads[j] = (
            inverse[:, j : j + 1] * gain[j : j + 1, :] * grads[j] - pre[...].astype(F32) * cubed[:, j : j + 1]
        ).astype(BF16)
    joined = jnp.concatenate(grads, axis=1)
    d_lat = nt(joined, up[...]).astype(BF16)
    d_lat_t = nt(up[...], joined).astype(BF16)
    total = nn(d_lat, dn)
    for j in range(3):
        total = total + nt(grads[j], w[j])
    normed, inverse = normalize(tok[...].astype(F32))
    back = normalize_back(normed, inverse, total * vec[M1 : M1 + 1, :])
    own = (meta[0] == at).astype(F32)
    part[...] = (back + dx1[...] * own).astype(part.dtype)
    g_dn = nn(d_lat_t, y1[...])
    for j in range(3):
        rows = slice(j * rank, (j + 1) * rank)
        g_up = nn(lat_t[rows, :], grads[j])
        for start, g in ((j * d, g_dn[rows, :]), (3 * d + j * width, g_up)):
            lanes = slice(start, start + g.shape[1])
            packed[:, lanes] = g + packed_in[:, lanes] if at else g


def context_kernel(groups, meta, ctx, w, up, dn, bias, gain, up_q, down_row, pre, low, ssq, lat_t):
    key = meta[AT_S] == 0
    c = ctx[...]
    count = c.shape[0]
    rank, width = up.shape[2:]
    lat = nt(c, dn[0, 0]).astype(BF16)
    lat_t[...] = nt(dn[0, 0], c).astype(BF16)
    b, g = bias[...].astype(F32), gain[...].astype(F32)
    u = nn(c, w[0]) + nn(lat, up[0, 0]) + jnp.where(key, b[1:2, :], b[2:3, :])
    pre[...] = u
    low[:count, :] = (u * jnp.where(key, g[1:2, :], 1.0)).astype(BF16)
    low[count : count + rank, :] = up_q[0, 0]
    low[count + rank : count + 2 * rank, :] = down_row[0, 0]
    low[count + 2 * rank : count + 3 * rank, :] = down_row[0, 1]
    row = lax.broadcasted_iota(jnp.int32, (rank, width), 0)
    low[count + 3 * rank :, :] = jnp.where(row == 0, b[0:1, :], jnp.where(row == 1, g[0:1, :], 0.0)).astype(BF16)
    total = row_total(u * u)
    share, block = count // groups, ssq.shape[1] // groups
    ssq[...] = jnp.zeros_like(ssq)
    for j in range(groups):
        ssq[:, j * block : j * block + share] = total[:, j * share : (j + 1) * share]


def context_row(groups, count, rows):
    share, block = count // groups, rows.shape[1] // groups
    return jnp.concatenate([rows[2:3, j * block : j * block + share] for j in range(groups)], axis=1)


def context_back_kernel(meta, ctx, w, up_in, dn_in, lat_t, grad, out, g_up, g_dn):
    g = grad[...]
    up, dn = up_in[0, 0], dn_in[0, 0]
    d_lat = nt(g, up).astype(BF16)
    d_lat_t = nt(up, g).astype(BF16)
    out[...] = nt(g, w[0]) + nn(d_lat, dn)
    g_up[...] = nn(lat_t[...], g)
    g_dn[...] = nn(d_lat_t, ctx[...])


def pack_kernel(meta, wo, wq, wc, out):
    rows, width = wo.shape[0], wq.shape[2]
    out[:rows, :] = wo[...]
    for j in range(out.shape[1] // width):
        out[rows : 2 * rows, j * width : (j + 1) * width] = wq[0, j * rows : (j + 1) * rows, :]
    out[2 * rows :, :] = wc[...]


def stack_kernel(meta, *refs):
    for j, ref in enumerate(refs[:-1]):
        refs[-1][j] = ref[...]


def start_copies(meta, plan, refs, targets, sems):
    copies = [[] for _ in targets]
    at = 0
    for source, weight, first, rows, slot, inner, size in plan:
        target = targets[weight]
        width = target.shape[2]
        sides = refs[source].shape[2] // width
        for j in range(sides):
            start = pl.multiple_of(meta[slot] * (size * sides) + (j * size + inner), 16)
            copies[weight].append(
                pltpu.make_async_copy(
                    refs[source].at[:, pl.ds(first, rows), pl.ds(j * width, width)],
                    target.at[:, pl.ds(start, rows), :],
                    sems.at[at],
                )
            )
            at += 1
    for weight in copies:
        for copy in weight:
            copy.start()
    return copies


def finish(copies):
    for copy in copies:
        copy.wait()


def cross_kernel(groups, head_count, plan, meta, *refs):
    n = groups * head_count
    os_first, os_rest, refs = refs[:groups], refs[groups : 2 * groups], refs[2 * groups :]
    tok, vec, up, dn3 = refs[:4]
    ctx, refs = refs[4], refs[5:]
    st_own, st_sib, wo_own, wq_own, wc_own = refs[:5]
    k = 1 + max(entry[0] for entry in plan)
    sources, refs = refs[5 : 5 + k], refs[5 + k :]
    y2, x2, x1, y3, qn, qc, oc, os_all, lse, lats = refs[:10]
    wo, wq, wc, sems = refs[10:]
    copies = start_copies(meta, plan, sources, (wo, wq, wc), sems)
    dn3 = dn3[0, 0]
    rank = dn3.shape[0]
    ctx_len = ctx.shape[2] - 4 * rank
    group = [lax.rem(meta[AT_T] + groups - r, groups) for r in range(groups)]
    small = jnp.concatenate([ctx[0, group[r], ctx_len:, :] for r in range(groups)], axis=1)
    first = meta[AT_S] == 0
    key_row = context_row(groups, ctx_len, jnp.where(first, st_own[...], st_sib[...]))
    ctx_inverse = jnp.broadcast_to(key_row, (8, ctx_len)).T[:, 0:1]
    width = head_count * HEAD_DIM
    for r in range(groups):
        middle = r * width + os_first[r].shape[1]
        os_all[:, r * width : middle] = os_first[r][...]
        os_all[:, middle : (r + 1) * width] = os_rest[r][...]
    os_v = os_all[...]
    down0, down1 = small[rank : 2 * rank, :], small[2 * rank : 3 * rank, :]
    lat = nt(os_v, down0).astype(BF16)
    lats[0:rank, :] = nt(down0, os_v).astype(BF16)
    total = nn(lat, up[0, 0])
    finish(copies[0])
    for r in range(groups):
        total = total + nn(os_v[:, r * width : (r + 1) * width], wo[r - 1] if r else wo_own[...])
    x1_v = tok[...].astype(F32) + (total + vec[B0 : B0 + 1, :]) * vec[M2 : M2 + 1, :]
    x1[...] = x1_v
    normed, _ = normalize(x1_v)
    y3_v = (normed * vec[CG : CG + 1, :] + vec[CB : CB + 1, :]).astype(BF16)
    y3[...] = y3_v
    lat = nt(y3_v, dn3).astype(BF16)
    lats[2 * rank : 3 * rank, :] = nt(dn3, y3_v).astype(BF16)
    finish(copies[1])
    q = nn(lat, small[0:rank, :]) + small[3 * rank : 3 * rank + 1, :].astype(F32)
    q = q + jnp.concatenate([nn(y3_v, wq[r - 1] if r else wq_own[0]) for r in range(groups)], axis=1)
    qc[...] = q
    inverse = lax.rsqrt(mean(q * q) + EPS)
    gain = small[3 * rank + 1 : 3 * rank + 2, :].astype(F32)
    qn[...] = (q * (inverse * (SCALE * LOG2E)) * gain).astype(BF16)
    for j in range(n):
        r, lanes = j // head_count, slice((j % head_count) * HEAD_DIM, (j % head_count + 1) * HEAD_DIM)
        keys = (ctx[0, group[r], :ctx_len, lanes].astype(F32) * ctx_inverse).astype(BF16)
        values = ctx[1, group[r], :ctx_len, lanes]
        scores = nt(keys, qn[:, j * HEAD_DIM : (j + 1) * HEAD_DIM])
        highest = jnp.max(scores, axis=0, keepdims=True)
        e = jnp.exp2(scores - highest)
        sums = jnp.sum(e, axis=0, keepdims=True)
        mixed = nn(values.astype(F32).T.astype(BF16), e.astype(BF16)) / sums
        oc[:, j * HEAD_DIM : (j + 1) * HEAD_DIM] = mixed.T.astype(BF16)
        lse[j : j + 1, :] = highest + jnp.log2(sums)
    oc_v = oc[...]
    lat = nt(oc_v, down1).astype(BF16)
    lats[rank : 2 * rank, :] = nt(down1, oc_v).astype(BF16)
    total = nn(lat, up[0, 1])
    finish(copies[2])
    for r in range(groups):
        total = total + nn(oc_v[:, r * width : (r + 1) * width], wc[r - 1] if r else wc_own[...])
    x2_v = x1_v + total + vec[B1 : B1 + 1, :]
    x2[...] = x2_v
    normed, _ = normalize(x2_v)
    y2[...] = (normed * vec[M4 : M4 + 1, :] + vec[M3 : M3 + 1, :]).astype(BF16)


def cross_back_kernel(groups, head_count, plan, meta, *refs):
    n = groups * head_count
    dy_own, dy_in, og, x2, x1, y3, qn, qc, oc, os_all, lse, lats, vec, up, dn3 = refs[:15]
    ctx, refs = refs[15], refs[16:]
    st_own, st_sib, wo_own, wq_own, wc_own = refs[:5]
    k = 1 + max(entry[0] for entry in plan)
    sources, refs = refs[5 : 5 + k], refs[5 + k :]
    dos_first, dos_rest, refs = refs[:groups], refs[groups : 2 * groups], refs[2 * groups :]
    dx1, g_own, g_oth, g_up, g_split, g_dn, wo, wq, wc, dq_s, sems = refs
    copies = start_copies(meta, plan, sources, (wo, wq, wc), sems)
    dn3 = dn3[0, 0]
    rank = dn3.shape[0]
    ctx_len = ctx.shape[2] - 4 * rank
    group = [lax.rem(meta[AT_T] + groups - r, groups) for r in range(groups)]
    small = jnp.concatenate([ctx[0, group[r], ctx_len:, :] for r in range(groups)], axis=1)
    first = meta[AT_S] == 0
    key_row = context_row(groups, ctx_len, jnp.where(first, st_own[...], st_sib[...]))
    ctx_inverse = jnp.broadcast_to(key_row, (8, ctx_len)).T[:, 0:1]
    width = head_count * HEAD_DIM
    down0, down1 = small[rank : 2 * rank, :], small[2 * rank : 3 * rank, :]
    normed, inverse = normalize(x2[...])
    dn = (dy_own[...] + dy_in[...].astype(F32)) * vec[M4 : M4 + 1, :]
    dx2 = og[...].astype(F32) + normalize_back(normed, inverse, dn)
    grad = dx2.astype(BF16)
    d_lat = nt(grad, up[0, 1]).astype(BF16)
    d_lat_t = nt(up[0, 1], grad).astype(BF16)
    oc_v = oc[...]
    g_up[rank : 2 * rank, :] = nn(lats[rank : 2 * rank, :], grad)
    split = nn(d_lat_t, oc_v)
    for r in range(groups):
        g_split[r, 2 * rank : 3 * rank, :] = split[:, r * width : (r + 1) * width]
    finish(copies[2])
    d_oc = nn(d_lat, down1) + jnp.concatenate(
        [nt(grad, wc[r - 1] if r else wc_own[...]) for r in range(groups)], axis=1
    )
    d_oc = d_oc.astype(BF16)
    for j in range(n):
        r, lanes = j // head_count, slice((j % head_count) * HEAD_DIM, (j % head_count + 1) * HEAD_DIM)
        head = slice(j * HEAD_DIM, (j + 1) * HEAD_DIM)
        keys = (ctx[0, group[r], :ctx_len, lanes].astype(F32) * ctx_inverse).astype(BF16)
        values = ctx[1, group[r], :ctx_len, lanes]
        q, g = qn[:, head], d_oc[:, head]
        delta = row_total(g.astype(F32) * oc_v[:, head].astype(F32))[0:1, :]
        p = jnp.exp2(nt(keys, q) - lse[j : j + 1, :])
        dv = nn(p.astype(BF16), g)
        ds = (p * (nt(values, g) - delta)).astype(BF16)
        dk = nn(ds, q) * (1.0 / LOG2E)
        dq_s[:, head] = nn(keys.astype(F32).T.astype(BF16), ds).T * SCALE
        g_own[r, :, lanes] = jnp.where(first, dk, dv).astype(BF16)
        g_oth[r, :, lanes] = jnp.where(first, dv, dk).astype(BF16)
    q = qc[...]
    inverse = lax.rsqrt(mean(q * q) + EPS)
    gain = small[3 * rank + 1 : 3 * rank + 2, :].astype(F32)
    scaled = dq_s[...] * gain
    stat = mean(scaled * q)
    dqc = (inverse * scaled - q * (inverse * inverse * inverse * stat)).astype(BF16)
    up_q = small[0:rank, :]
    d_lat = nt(dqc, up_q).astype(BF16)
    d_lat_t = nt(up_q, dqc).astype(BF16)
    split = nn(lats[2 * rank : 3 * rank, :], dqc)
    for r in range(groups):
        g_split[r, 0:rank, :] = split[:, r * width : (r + 1) * width]
    g_dn[...] = nn(d_lat_t, y3[...])
    dy3 = nn(d_lat, dn3)
    finish(copies[1])
    for r in range(groups):
        part = dqc[:, r * width : (r + 1) * width]
        dy3 = dy3 + nt(part, wq[r - 1] if r else wq_own[0])
    normed, inverse = normalize(x1[...])
    dx1_v = dx2 + normalize_back(normed, inverse, dy3 * vec[CG : CG + 1, :])
    dx1[...] = dx1_v
    grad = (dx1_v * vec[M2 : M2 + 1, :]).astype(BF16)
    d_lat = nt(grad, up[0, 0]).astype(BF16)
    d_lat_t = nt(up[0, 0], grad).astype(BF16)
    g_up[0:rank, :] = nn(lats[0:rank, :], grad)
    split = nn(d_lat_t, os_all[...])
    for r in range(groups):
        g_split[r, rank : 2 * rank, :] = split[:, r * width : (r + 1) * width]
    finish(copies[0])
    low = nn(d_lat, down0)
    for r in range(groups):
        block = nt(grad, wo[r - 1] if r else wo_own[...]) + low[:, r * width : (r + 1) * width]
        dos_first[r][...] = block[:, :HEAD_DIM].astype(BF16)
        dos_rest[r][...] = block[:, HEAD_DIM:].astype(BF16)


def feed_kernel(tiles, first, meta, *refs):
    y2, og, vec, bias, dn1, up1, dn2, up2, w1_h, w2_h = refs[:10]
    if first:
        x2 = refs[10]
    else:
        acc = refs[10:14]
    refs = refs[11:] if first else refs[15:]
    dn1, up1, dn2, up2 = dn1.at[0], up1.at[0], dn2.at[0], up2.at[0]
    out, dy, g_up1, g_dn1, g_up2, g_dn2, w1, w2, sems = refs
    copies = []
    for at, (start, size) in enumerate(tiles):
        rows = pl.ds(start, size)
        pair = [
            pltpu.make_async_copy(h.at[rows, :], v.at[rows, :], sems.at[j, at])
            for j, (h, v) in enumerate(((w1_h, w1), (w2_h, w2)))
        ]
        for copy in pair:
            copy.start()
        copies.append(pair)
    y = y2[...]
    dff = (og[...].astype(F32) * vec[M5 : M5 + 1, :]).astype(BF16)
    lat = nt(y, dn1[...]).astype(BF16)
    lat_t = nt(dn1[...], y).astype(BF16)
    drl = nt(dff, up2[...]).astype(BF16)
    drl_t = nt(up2[...], dff).astype(BF16)
    part = grad = rl = rl_t = d_lat = d_lat_t = 0.0
    for (start, size), pair in zip(tiles, copies):
        cols = slice(start, start + size)
        finish(pair)
        h = nt(y, w1[cols, :]) + nn(lat, up1[:, cols]) + bias[:, cols]
        du = nt(dff, w2[cols, :]) + nn(drl, dn2[:, cols])
        sq = h * h
        t = jnp.tanh(GELU_C * h * (1.0 + 0.044715 * sq))
        act = (0.5 * h * (1.0 + t)).astype(BF16)
        slope = 0.5 * (1.0 + t) + (0.5 * GELU_C) * h * (1.0 - t * t) * (1.0 + (3.0 * 0.044715) * sq)
        dh = (du * slope).astype(BF16)
        part = part + nn(act, w2[cols, :])
        grad = grad + nn(dh, w1[cols, :])
        rl = rl + nt(act, dn2[:, cols])
        rl_t = rl_t + nt(dn2[:, cols], act)
        d_lat = d_lat + nt(dh, up1[:, cols])
        d_lat_t = d_lat_t + nt(up1[:, cols], dh)
        new_up1, new_dn2 = nn(lat_t, dh), nn(drl_t, act)
        g_up1[:, cols] = new_up1 if first else new_up1 + acc[0][:, cols]
        g_dn2[:, cols] = new_dn2 if first else new_dn2 + acc[3][:, cols]
    part = part + nn(rl.astype(BF16), up2[...])
    grad = grad + nn(d_lat.astype(BF16), dn1[...])
    new_dn1, new_up2 = nn(d_lat_t.astype(BF16), y), nn(rl_t.astype(BF16), dff)
    g_dn1[...] = new_dn1 if first else new_dn1 + acc[1][...]
    g_up2[...] = new_up2 if first else new_up2 + acc[2][...]
    part = part * vec[M5 : M5 + 1, :]
    if first:
        part = part + x2[...] + vec[B2 : B2 + 1, :] * vec[M5 : M5 + 1, :]
    out[...] = part.astype(out.dtype)
    dy[...] = grad.astype(dy.dtype)


def shift(count, step):
    return [(a, (a + step) % count) for a in range(count)]


def flip(count, step):
    return [(a, a ^ step) for a in range(count)]


def powers(count):
    return [1 << j for j in range(count.bit_length() - 1)]


def send(values, axis, pairs):
    return jax.tree.map(lambda v: lax.ppermute(v, axis, pairs), values)


def ring_pieces(own, axis):
    count = lax.axis_size(axis)
    pieces = [own]
    for _ in range(count - 1):
        pieces.append(send(pieces[-1], axis, shift(count, 1)))
    return pieces


def ring_total(parts, axis):
    count = lax.axis_size(axis)
    moving = parts[1]
    for r in range(2, count):
        moving = send(moving, axis, shift(count, 1))
        moving = (moving.astype(F32) + parts[r].astype(F32)).astype(BF16)
    return parts[0], send(moving, axis, shift(count, 1))


def gather_direct(own, axis):
    count = lax.axis_size(axis)
    return [own] + [send(own, axis, shift(count, r)) for r in range(1, count)]


def scatter_direct(parts, axis):
    count = lax.axis_size(axis)
    return parts[0].astype(F32) + sum(
        send(parts[r].astype(BF16), axis, shift(count, -r)).astype(F32) for r in range(1, count)
    )


def gather_flipped(own, axis):
    count = lax.axis_size(axis)
    return [own] + [send(own, axis, flip(count, j)) for j in range(1, count)]


def total_flipped(own, axis):
    terms = [v.astype(F32) for v in gather_flipped(own, axis)]
    while len(terms) > 1:
        terms = [terms[j] + terms[j + 1] for j in range(0, len(terms), 2)]
    return terms[0]


def halves(values, axis):
    half = values.shape[0] // 2
    low, high = values[:half], values[half:]
    upper = lax.axis_index(axis) == 1
    return jnp.where(upper, high, low), jnp.where(upper, low, high)


def pair_scatter(values):
    kept, sent = halves(values, "seq")
    return kept + send(sent.astype(BF16), "seq", flip(2, 1)).astype(F32)


def pair_gather(values, dim):
    other = send(values, "seq", flip(2, 1))
    upper = lax.axis_index("seq") == 1
    return jnp.concatenate([jnp.where(upper, other, values), jnp.where(upper, values, other)], axis=dim)


def place_blocks(blocks, axis):
    size = blocks[0].shape[0]
    out = jnp.zeros((size * len(blocks),) + blocks[0].shape[1:], blocks[0].dtype)
    index = lax.axis_index(axis)
    for j, block in enumerate(blocks):
        out = lax.dynamic_update_slice_in_dim(out, block, (index ^ j) * size, 0)
    return out


def total_twice(values, axis):
    for step in powers(lax.axis_size(axis)):
        values = values + send(values, axis, flip(lax.axis_size(axis), step))
    return values


class Chains:
    def __init__(self):
        self.chains, self.values, self.results = [], [], {}

    def add(self, chain):
        self.chains.append(chain)
        self.values.append(None)
        return len(self.chains) - 1

    def start(self, at):
        self.advance(at)

    def advance(self, at):
        try:
            self.values[at] = self.chains[at].send(self.values[at])
        except StopIteration as end:
            self.results[at] = end.value

    def step(self, skip=()):
        for at in range(len(self.chains)):
            if at not in self.results and at not in skip:
                self.advance(at)

    def live(self):
        return len(self.results) < len(self.chains)

    def done(self, at):
        return at in self.results

    def result(self, at):
        return self.results[at]

    def arrived(self):
        live = [self.values[at] for at in range(len(self.chains)) if at not in self.results]
        return jax.tree.leaves(live)

    def put(self, leaves):
        places = [at for at in range(len(self.chains)) if at not in self.results]
        structure = jax.tree.structure([self.values[at] for at in places])
        for at, value in zip(places, jax.tree.unflatten(structure, leaves)):
            self.values[at] = value


def seal(*values):
    return list(lax.optimization_barrier(values)) if values else []


def ring_steps(parts, axis):
    count = lax.axis_size(axis)
    moving = parts[1].astype(BF16)
    for r in range(2, count + 1):
        moving = yield send(moving, axis, shift(count, 1))
        if r < count:
            moving = (moving.astype(F32) + parts[r].astype(F32)).astype(BF16)
    return parts[0].astype(F32) + moving.astype(F32)


class Line:
    def __init__(self):
        self.parts, self.acc, self.total, self.out, self.at, self.moving = [], [], [], [], 0, []
        index = lax.axis_index("tensor")
        self.inner = (index == 1) | (index == 2)

    def add(self, part):
        self.parts.append(part)

    def send(self):
        inward = self.parts[self.at] if self.at < len(self.parts) else None
        outward = self.total[self.at - 2] if 0 <= self.at - 2 < len(self.total) else None
        across = self.acc[self.at - 1] if 0 <= self.at - 1 < len(self.acc) else None
        pairs = [(0, 1), (3, 2)] * (inward is not None) + [(1, 0), (2, 3)] * (outward is not None)
        if inward is None or outward is None:
            mine = outward if inward is None else inward
        else:
            mine = jnp.where(self.inner, outward, inward)
        self.moving = [send(mine, "tensor", pairs)] if pairs else []
        self.shape = (inward is not None, across is not None, outward is not None)
        if across is not None:
            self.moving.append(send(across, "tensor", [(1, 2), (2, 1)]))

    def receive(self, moving):
        inward, across, outward = self.shape
        moving = list(moving)
        add_low = lambda a, b: (a.astype(F32) + b.astype(F32)).astype(BF16)
        if inward or outward:
            first = moving.pop(0)
        if inward:
            self.acc.append(add_low(self.parts[self.at], first))
        if across:
            self.total.append(add_low(self.acc[self.at - 1], moving.pop(0)))
        if outward:
            self.out.append(jnp.where(self.inner, self.total[self.at - 2], first))
        self.at += 1
        self.moving = []

    def live(self):
        return len(self.out) < len(self.parts)


def adapter_steps(value, shared):
    groups, dp = lax.axis_size("tensor"), lax.axis_size("dp")
    pair, upper = flip(2, 1), lax.axis_index("seq") == 1
    kept, sent = halves(value, "seq")
    other = yield send(sent.astype(BF16), "seq", pair)
    value = kept + other.astype(F32)
    own, rest = value[:, :shared].astype(BF16), value[:, shared:].astype(BF16)
    for step in powers(groups):
        other = yield send(own, "tensor", flip(groups, step))
        own = (own.astype(F32) + other.astype(F32)).astype(BF16)
    value = jnp.concatenate([own, rest], axis=1)[None]
    for step in powers(dp):
        other = yield send(value, "dp", flip(dp, step))
        value = jnp.concatenate([value, other])
    other = yield send(value, "seq", pair)
    return jnp.concatenate([jnp.where(upper, other, value), jnp.where(upper, value, other)], axis=1)


def context_grad_steps(value):
    groups, dp = lax.axis_size("tensor"), lax.axis_size("dp")
    at_dp = lax.axis_index("dp")
    pair, second = flip(2, 1), lax.axis_index("seq") == 1
    kept, sent = halves(value, "seq")
    other = yield send(sent.astype(BF16), "seq", pair)
    value = kept + other.astype(F32)
    rows = value.shape[0] // dp
    parts = [lax.dynamic_slice_in_dim(value, (at_dp ^ j) * rows, rows, 0) for j in range(dp)]
    others = yield tuple(send(parts[j].astype(BF16), "dp", flip(dp, j)) for j in range(1, dp))
    value = (parts[0] + sum(other.astype(F32) for other in others)).astype(BF16)
    for step in powers(groups):
        other = yield send(value, "tensor", flip(groups, step))
        value = (value.astype(F32) + other.astype(F32)).astype(BF16)
    for step in powers(dp):
        other = yield send(value, "dp", flip(dp, step))
        upper = (at_dp & step) != 0
        value = jnp.concatenate([jnp.where(upper, other, value), jnp.where(upper, value, other)])
    other = yield send(value, "seq", pair)
    return jnp.concatenate([jnp.where(second, other, value), jnp.where(second, value, other)])


def weight_share():
    return 4 if lax.axis_size("dp") == 4 else 1


def weight_plan(rows, count):
    share, seq = weight_share(), lax.axis_size("seq")
    d, s = lax.axis_index("dp"), lax.axis_index("seq")
    slots = [(s ^ a) * share + ((d ^ b) if share > 1 else 0) for a in range(seq) for b in range(share)]
    total = rows * count
    cut = far_cut(total)
    half = [(0, 0, total, 0)]
    if share > 1:
        half += [(1, 0, total, 1), (2, 0, total, 2), (3, 0, cut, 3), (4, cut, total - cut, 3)]
    spans = half + [(len(half) + a, b, c, share + e) for a, b, c, e in half]
    plan = []
    for source, start, size, slot in spans:
        for weight in range(count):
            low, high = max(start, weight * rows), min(start + size, (weight + 1) * rows)
            if low < high:
                plan.append((source, weight, low - start, high - low, SLOTS + slot, low - weight * rows, rows))
    return plan, slots


def far_cut(total):
    return (total // 2 + 15) // 16 * 16


def rope_tables(grid_pos):
    sixth = HEAD_DIM // 6
    counts = [(HEAD_DIM - 4 * sixth) // 2, sixth, sixth]
    table = np.zeros((3, HEAD_DIM), np.float32)
    lane = 0
    for component, count in enumerate(counts):
        for pair in range(count):
            table[component, lane : lane + 2] = 10000.0 ** (-pair / count)
            lane += 2
    positions = grid_pos.astype(F32)
    angles = sum(positions[c][:, None] * table[c][None, :] for c in range(3))
    sign = np.where(np.arange(HEAD_DIM) % 2 == 0, -1.0, 1.0).astype(np.float32)
    return jnp.cos(angles), jnp.sin(angles) * sign[None, :]


def select_slot(table, index):
    return lax.dynamic_index_in_dim(table, index, 0, keepdims=False)


def spread(gradients, indices, slot_count):
    hits = (jnp.arange(slot_count)[:, None] == indices[None, :]).astype(F32)
    out = 0.0
    for latent in range(gradients.shape[0]):
        shape = (slot_count,) + (1,) * (gradients.ndim - 1)
        out = out + hits[:, latent].reshape(shape) * gradients[latent].astype(F32)[None]
    return out


def eight_rows(rows):
    return jnp.concatenate([jnp.stack(rows), jnp.zeros((8 - len(rows), rows[0].shape[0]), F32)])


def per_device(
    tokens,
    positions,
    time_emb,
    modulation,
    context,
    adapter_index,
    self_qkv,
    self_bias,
    self_gain,
    self_out,
    cross_qkv,
    cross_bias,
    cross_gain,
    cross_out,
    cross_norm_gain,
    cross_norm_bias,
    ffn_in,
    ffn_bias,
    ffn_out,
    out_bias,
    col_down,
    col_up,
    ffn1_down,
    ffn1_up,
    row_down,
    row_up,
    ffn2_down,
    ffn2_up,
    out_grad,
):
    groups = lax.axis_size("tensor")
    seq = lax.axis_size("seq")
    i, s = lax.axis_index("tensor"), lax.axis_index("seq")
    tl, d = tokens.shape[1:]
    tc = tl // groups
    ctx_len = context.shape[0]
    width = self_qkv.shape[2]
    hc = width // HEAD_DIM
    ff = ffn_in.shape[1]
    slots, rank = col_down.shape[0], col_down.shape[3]
    share = weight_share()
    slice_rows = width // (share * seq)
    plan, slot_list = weight_plan(slice_rows, 3)
    part_at = s * share + (lax.axis_index("dp") if share > 1 else 0)
    meta = jnp.stack([jnp.asarray(v, jnp.int32) for v in [i, s, adapter_index[0], part_at] + slot_list])
    tok, og = tokens[0], out_grad[0]
    block = pl.BlockSpec
    hbm = pl.BlockSpec(memory_space=pl.ANY)
    pair = flip(seq, 1)

    def table(array, *place, rows=1):
        if not place:
            return (array, block((1,) + array.shape[1:], lambda *a: (a[-1][ADAPTER],) + (0,) * (array.ndim - 1)))
        return (
            array,
            block(
                (1, rows) + array.shape[2:],
                lambda *a: (a[-1][ADAPTER], place[0](a[-1]) if callable(place[0]) else place[0], 0, 0),
            ),
        )

    col_dn, row_dn = jnp.swapaxes(col_down, 2, 3), jnp.swapaxes(row_down, 2, 3)
    feed_tables = [
        table(jnp.swapaxes(ffn1_down, 1, 2)),
        table(ffn1_up),
        table(jnp.swapaxes(ffn2_down, 1, 2)),
        table(ffn2_up),
    ]

    shard_at = lambda b, m: (m[PART], 0)
    (slices,) = run_kernel(
        pack_kernel,
        meta,
        [
            (self_out, block((slice_rows, d), shard_at)),
            (cross_qkv, block((1, slice_rows * groups, width), lambda b, m: (0, m[PART], 0))),
            (cross_out, block((slice_rows, d), shard_at)),
        ],
        [(sds((3 * slice_rows, d), BF16), whole((3 * slice_rows, d)))],
        us=1.5,
    )
    by_group = gather_direct(slices, "tensor")[1:]

    is_key = s == 0
    ctx_w = (cross_qkv, block((1, d, width), lambda b, m: (1 + m[AT_S], 0, 0)))
    ctx_up, ctx_dn = table(col_up, lambda m: 4 + m[AT_S]), table(col_dn, lambda m: 4 + m[AT_S])
    low_rows = ctx_len + 4 * rank
    ctx_pre, ctx_low, ctx_ssq, ctx_lat_t = run_kernel(
        functools.partial(context_kernel, groups),
        meta,
        [
            (context, whole(context.shape)),
            ctx_w,
            ctx_up,
            ctx_dn,
            (cross_bias, whole(cross_bias.shape)),
            (cross_gain, whole(cross_gain.shape)),
            table(col_up, 3),
            table(row_dn, 0, rows=2),
        ],
        [
            (sds((ctx_len, width), F32), whole((ctx_len, width))),
            (sds((low_rows, width), BF16), whole((low_rows, width))),
            (sds((8, tl), F32), whole((8, tl))),
            (sds((rank, ctx_len), BF16), whole((rank, ctx_len))),
        ],
        us=6,
        after=[slices],
    )
    cos, sin = rope_tables(positions[:, 0, :])
    rows_d = block((tc, d), lambda b, m: (b, 0))
    rows_w = block((tc, width), lambda b, m: (b, 0))
    rows_h = block((tc, HEAD_DIM), lambda b, m: (b, 0))
    lanes_8 = block((8, tc), lambda b, m: (0, b))
    self_tables = [table(col_up, 0, rows=3), table(col_dn, 0, rows=3)]
    y1, lat_t, pre_q, pre_k, raw_q, kv, ssq, vec = run_kernel(
        functools.partial(qkv_kernel, hc),
        meta,
        [
            (tok, rows_d),
            (modulation, whole(modulation.shape)),
            (time_emb[0], whole(modulation.shape)),
            (out_bias, whole(out_bias.shape)),
            (cross_norm_gain[None], whole((1, d))),
            (cross_norm_bias[None], whole((1, d))),
            (self_qkv, whole(self_qkv.shape)),
        ]
        + self_tables
        + [
            (self_bias, whole(self_bias.shape)),
            (self_gain, whole(self_gain.shape)),
            (cos, rows_h),
            (sin, rows_h),
            (ctx_ssq, lanes_8),
        ],
        [
            (sds((tl, d), BF16), rows_d),
            (sds((3 * rank, tl), BF16), block((3 * rank, tc), lambda b, m: (0, b))),
            (sds((tl, width), BF16), rows_w),
            (sds((tl, width), BF16), rows_w),
            (sds((tl, width), BF16), rows_w),
            (sds((tl, 2 * width), BF16), block((tc, 2 * width), lambda b, m: (b, 0))),
            (sds((8, tl), F32), lanes_8),
            (sds((16, d), F32), whole((16, d))),
        ],
        grid=(groups,),
        scratch=[pltpu.VMEM((3 * rank, 3 * width), BF16)],
        us=15,
    )
    kv_sib = send(kv, "seq", pair)
    *first_steps, last_step = powers(groups)
    for step in first_steps:
        ssq = ssq + send(ssq, "tensor", flip(groups, step))
    ssq, *by_group = seal(ssq, *by_group)
    (by_group,) = run_kernel(
        stack_kernel,
        meta,
        [(a, whole(a.shape)) for a in by_group],
        [(sds((groups - 1,) + slices.shape, BF16), whole((groups - 1,) + slices.shape))],
        us=2,
    )
    ssq, by_group = seal(ssq, by_group)
    along = [send(by_group, "dp", flip(share, 1)), send(by_group, "dp", flip(share, 2))] if share > 1 else []
    st_own = lax.rsqrt((ssq + send(ssq, "tensor", flip(groups, last_step))) / d + EPS)
    st_sib = send(st_own, "seq", pair)
    ctx_low, _ = seal(ctx_low, st_own)
    ctx_all = lax.all_gather(ctx_low, ("seq", "tensor"))
    ctx_all = ctx_all.reshape((seq, groups) + ctx_all.shape[1:])

    all_8 = whole((8, tl))
    turned = lambda r, m: lax.rem(m[AT_T] + r, groups)
    parts = [(0, hc - 1), (hc - 1, 1)]
    mixed, lses, os_pieces = [], [], []
    for first, count in parts:
        kv_at = lambda lane: block((tl, HEAD_DIM), lambda h, r, m: (0, lane + h))
        own_rows = block((tc, HEAD_DIM), lambda h, r, m: (0, h))
        *blocks, out, lse = run_kernel(
            functools.partial(attention_kernel, groups),
            meta,
            [
                (raw_q, block((tc, HEAD_DIM), lambda h, r, m, first=first: (turned(r, m), first + h))),
                (st_own, block((8, tc), lambda h, r, m: (0, turned(r, m)))),
                (st_own, all_8),
                (st_sib, all_8),
                (kv, kv_at(first)),
                (kv_sib, kv_at(first)),
                (kv, kv_at(hc + first)),
                (kv_sib, kv_at(hc + first)),
            ],
            [(sds((tc, count * HEAD_DIM), BF16), own_rows)] * groups
            + [
                (sds((tl, count * HEAD_DIM), BF16), block((tc, HEAD_DIM), lambda h, r, m: (r, h))),
                (sds((8 * count, tl), F32), block((8, tc), lambda h, r, m: (h, r))),
            ],
            grid=(count, groups),
            scratch=[pltpu.VMEM((2 * tl, HEAD_DIM), BF16), pltpu.VMEM((HEAD_DIM, 2 * tl), BF16)],
            us=9.5 * count,
            after=[by_group] if first == 0 else [out],
        )
        mixed.append(out)
        lses.append(lse)
        if first:
            blocks[0], *late = seal(blocks[0], *along, *os_pieces)
            along, os_pieces = late[: len(along)], late[len(along) :]
        os_pieces += [send(a, "tensor", shift(groups, r)) if r else a for r, a in enumerate(blocks)]
    weight_parts = [by_group] + along
    if share > 1:
        middle = far_cut(by_group.shape[1])
        weight_parts += [
            send(along[1][:, :middle], "dp", flip(share, 1)),
            send(along[0][:, middle:], "dp", flip(share, 2)),
        ]
    near = seal(*os_pieces[-groups + 1 :], *weight_parts)
    os_pieces[-groups + 1 :], weight_parts = near[: groups - 1], near[groups - 1 :]
    weight_parts = weight_parts + [send(p, "seq", pair) for p in weight_parts]

    vspec = whole(vec.shape)
    own_block = block((tc, d), lambda b, m: (m[AT_T], 0))
    weight_scratch = [
        pltpu.VMEM((groups - 1, width, d), BF16),
        pltpu.VMEM((groups - 1, d, width), BF16),
        pltpu.VMEM((groups - 1, width, d), BF16),
    ]
    sems = pltpu.SemaphoreType.DMA((len(plan) * groups,))
    shared = [
        table(row_up),
        table(col_dn, 3),
        (ctx_all, whole(ctx_all.shape)),
        (st_own, all_8),
        (st_sib, all_8),
        (self_out, whole(self_out.shape)),
        (cross_qkv, block((1, d, width), lambda b, m: (0, 0, 0))),
        (cross_out, whole(cross_out.shape)),
    ] + [(p, hbm) for p in weight_parts]
    whole_of = lambda shape, dtype: (sds(shape, dtype), whole(shape))
    y2, x2, x1, y3, qn, qc, oc, os_all, lse_c, lats = run_kernel(
        functools.partial(cross_kernel, groups, hc, plan),
        meta,
        [(p, whole(p.shape)) for p in os_pieces] + [(tok, own_block), (vec, vspec)] + shared,
        [
            whole_of((tc, d), BF16),
            whole_of((tc, d), F32),
            whole_of((tc, d), F32),
            whole_of((tc, d), BF16),
            whole_of((tc, d), BF16),
            whole_of((tc, d), F32),
            whole_of((tc, d), BF16),
            whole_of((tc, d), BF16),
            whole_of((16, tc), F32),
            whole_of((3 * rank, tc), BF16),
        ],
        scratch=weight_scratch + [sems],
        us=20,
    )

    tiles = [(a, min(768, ff - a)) for a in range(0, ff, 768)]
    w1t = ffn_in.T
    y2_pieces = ring_pieces(y2, "tensor")
    feed_bias = ffn_bias.astype(F32)[None]
    feed_out, dys, acc = None, [], None
    for r in range(groups):
        place = block((tc, d), lambda b, m, r=r: (lax.rem(m[AT_T] + groups - r, groups), 0))
        ins = [(y2_pieces[r], whole((tc, d))), (og, place), (vec, vspec), (feed_bias, whole(feed_bias.shape))]
        ins += feed_tables + [(w1t, hbm), (ffn_out, hbm)]
        if r == 0:
            ins += [(x2, whole((tc, d)))]
        else:
            ins += [(a, whole(a.shape)) for a in acc] + [(feed_out, hbm)]
        feed_out, dy, *acc = run_kernel(
            functools.partial(feed_kernel, tiles, r == 0),
            meta,
            ins,
            [(sds((tl, d), BF16), place), whole_of((tc, d), F32 if r == 0 else BF16)]
            + [whole_of((rank, n), F32) for n in (ff, d, d, ff)],
            scratch=[pltpu.VMEM((ff, d), BF16), pltpu.VMEM((ff, d), BF16), pltpu.SemaphoreType.DMA((2, len(tiles)))],
            us=18,
            aliases={15: 0} if r else None,
        )
        dys.append(dy)
    g_up1, g_dn1, g_up2, g_dn2 = acc

    dy_own, dy_in = ring_total(dys, "tensor")
    feed_out, dy_in = seal(feed_out, dy_in)
    line = Line() if groups == 4 else None
    if line:
        for r in range(groups):
            line.add(feed_out[r * tc : (r + 1) * tc])
        line.send()
    else:
        result = lax.psum(feed_out, "tensor")
    *dos, dx1, g_own, g_oth, g_rup, g_split, g_cqdn = run_kernel(
        functools.partial(cross_back_kernel, groups, hc, plan),
        meta,
        [(dy_own, whole((tc, d))), (dy_in, whole((tc, d))), (og, own_block)]
        + [(a, whole(a.shape)) for a in (x2, x1, y3, qn, qc, oc, os_all, lse_c, lats)]
        + [(vec, vspec)]
        + shared,
        [whole_of((tc, HEAD_DIM), BF16)] * groups
        + [whole_of((tc, width - HEAD_DIM), BF16)] * groups
        + [
            whole_of((tc, d), F32),
            whole_of((groups, ctx_len, width), BF16),
            whole_of((groups, ctx_len, width), BF16),
            whole_of((2 * rank, d), F32),
            whole_of((groups, 3 * rank, width), F32),
            whole_of((rank, d), F32),
        ],
        scratch=weight_scratch + [pltpu.VMEM((tc, d), F32), sems],
        us=26,
    )

    back_shift = lambda arrays: [send(a, "tensor", shift(groups, -r)) if r else a for r, a in enumerate(arrays)]
    moving = lambda: line.moving if line else []
    chains = Chains()
    dos[0], g_oth, g_cqdn, *tied = seal(dos[0], g_oth, g_cqdn, *moving())
    if line:
        line.receive(tied)
    dos_first = back_shift(dos[:groups])
    packed = jnp.concatenate([g_cqdn, g_dn1, g_rup[:rank], g_rup[rank:], g_up2, g_up1, g_dn2], axis=1)
    early_at = chains.add(adapter_steps(packed, 5 * d))
    g_oth = send(g_oth, "seq", pair)
    chains.step()
    g_oth, *dos_first = seal(g_oth, *dos_first)
    to_group = jnp.concatenate([g_own.astype(F32) + g_oth.astype(F32), g_split], axis=1)
    dos_rest = back_shift(dos[groups:])
    group_at = chains.add(ring_steps([to_group[r] for r in range(groups)], "tensor"))
    chains.step()

    back, dkv_in = [], []
    for h in range(hc):
        of, at = (0, h) if h < parts[1][0] else (1, h - parts[1][0])
        grads = dos_first if h == 0 else dos_rest
        lane = 0 if h == 0 else h - 1
        kv_at = lambda lane: block((tl, HEAD_DIM), lambda r, m: (0, lane))
        if h:
            tied = seal(*dos_rest, *chains.arrived(), *back[-1][:1])
            dos_rest = tied[: len(dos_rest)]
            chains.put(tied[len(dos_rest) : -1])
            dkv_in.append(send(back[-1][2], "seq", pair))
            if h == 1:
                chains.step([early_at])
                if line:
                    line.send()
            else:
                chains.step()
            grads = dos_rest
        back.append(
            run_kernel(
                functools.partial(attention_back_kernel, groups, h == 0),
                meta,
                [
                    (raw_q, block((tc, HEAD_DIM), lambda r, m, h=h: (turned(r, m), h))),
                    (st_own, block((8, tc), lambda r, m: (0, turned(r, m)))),
                    (st_own, all_8),
                    (st_sib, all_8),
                    (kv, kv_at(h)),
                    (kv_sib, kv_at(h)),
                    (kv, kv_at(hc + h)),
                    (kv_sib, kv_at(hc + h)),
                    (mixed[of], block((tc, HEAD_DIM), lambda r, m, at=at: (r, at))),
                    (lses[of], block((8, tc), lambda r, m, at=at: (at, r))),
                ]
                + [(g, block((tc, HEAD_DIM), lambda r, m, lane=lane: (0, lane))) for g in grads]
                + ([(a, all_8) for a in back[-1][3:]] if h else []),
                [
                    (sds((tl, HEAD_DIM), F32), block((tc, HEAD_DIM), lambda r, m: (turned(r, m), 0))),
                    whole_of((tl, 2 * HEAD_DIM), F32),
                    whole_of((tl, 2 * HEAD_DIM), BF16),
                    whole_of((8, tl), F32),
                    whole_of((8, tl), F32),
                ],
                grid=(groups,),
                scratch=[
                    pltpu.VMEM((2 * tl, HEAD_DIM), BF16),
                    pltpu.VMEM((HEAD_DIM, 2 * tl), BF16),
                    pltpu.VMEM((2 * tl, HEAD_DIM), BF16),
                    pltpu.VMEM((2 * tl, HEAD_DIM), F32),
                    pltpu.VMEM((2 * tl, HEAD_DIM), F32),
                    pltpu.VMEM((tc, HEAD_DIM), BF16),
                ],
                us=12.5,
                after=list(tied[-1:]) if h else [],
            )
        )
    dq, dkv, dkv_out = zip(*[b[:3] for b in back])
    stat, cross = back[-1][3:]
    stat, cross, *tied = seal(stat, cross, *chains.arrived(), *moving())
    count = len(chains.arrived())
    chains.put(tied[:count])
    if line:
        line.receive(tied[count:])
    cross = send(cross, "seq", pair)
    dkv_in.append(send(dkv_out[-1], "seq", pair))
    chains.step([early_at])
    to_group = chains.result(group_at)
    g_ctx, split = to_group[:ctx_len], to_group[ctx_len:]
    ctx_gain = jnp.where(is_key, cross_gain[1:2].astype(F32), 1.0)
    ctx_stat = jnp.sum(g_ctx * ctx_gain * ctx_pre, axis=1)
    stat = stat + cross
    for step in powers(groups):
        other, ctx_other, *tied = seal(*send((stat, ctx_stat), "tensor", flip(groups, step)), *chains.arrived())
        chains.put(tied)
        stat, ctx_stat = stat + other, ctx_stat + ctx_other
    if line:
        line.send()
    chains.step()
    st_back = st_own * st_own * st_own * stat / d

    ctx_inverse = jnp.concatenate([st_own[2, j * tc : j * tc + ctx_len // groups] for j in range(groups)])
    ctx_cubed = ctx_inverse * ctx_inverse * ctx_inverse * ctx_stat / d
    d_key = ctx_inverse[:, None] * ctx_gain * g_ctx - ctx_pre * ctx_cubed[:, None]
    d_ctx = jnp.where(is_key, d_key, g_ctx).astype(BF16)
    ctx_part, g_ctx_up, g_ctx_dn = run_kernel(
        context_back_kernel,
        meta,
        [
            (context, whole(context.shape)),
            ctx_w,
            ctx_up,
            ctx_dn,
            (ctx_lat_t, whole(ctx_lat_t.shape)),
            (d_ctx, whole(d_ctx.shape)),
        ],
        [whole_of((ctx_len, d), F32), whole_of((rank, width), F32), whole_of((rank, d), F32)],
        us=6,
    )

    q_parts, late = [], None
    for r in range(groups):
        in_d = block((tc, d), lambda b, m, r=r: (r, 0))
        in_w = block((tc, width), lambda b, m, r=r: (r, 0))
        in_h = block((tc, HEAD_DIM), lambda b, m, r=r: (r, 0))
        in_2h = block((tc, 2 * HEAD_DIM), lambda b, m, r=r: (r, 0))
        in_8 = block((8, tc), lambda b, m, r=r: (0, r))
        size = (rank, 3 * (d + width))
        part, late = run_kernel(
            functools.partial(qkv_back_kernel, hc, r),
            meta,
            [(a, in_h) for a in dq]
            + [(a, in_2h) for a in list(dkv) + dkv_in]
            + [
                (pre_q, in_w),
                (pre_k, in_w),
                (st_own, in_8),
                (st_back, in_8),
                (self_gain, whole(self_gain.shape)),
                (cos, in_h),
                (sin, in_h),
                (self_qkv, whole(self_qkv.shape)),
            ]
            + self_tables
            + [
                (tok, in_d),
                (vec, vspec),
                (y1, in_d),
                (lat_t, block((3 * rank, tc), lambda b, m, r=r: (0, r))),
                (dx1, whole((tc, d))),
            ]
            + ([(late, whole(size))] if r else []),
            [whole_of((tc, d), BF16), whole_of(size, F32)],
            scratch=[pltpu.VMEM((3 * rank, 3 * width), BF16)],
            us=8.5,
        )
        q_parts.append(part)
        if line:
            line.add(part)
        if r != 1:
            late, *tied = seal(late, *chains.arrived(), *moving())
            count = len(chains.arrived())
            chains.put(tied[:count])
            if r == 0:
                ctx_at = chains.add(context_grad_steps(ctx_part))
            chains.step()
            if line:
                line.receive(tied[count:])
                line.send()
    pick = lambda g: [jnp.where(is_key, g, 0.0), jnp.where(is_key, 0.0, g)]
    late = jnp.concatenate(
        [late[:, : 3 * d]]
        + pick(g_ctx_dn)
        + [late[:, 3 * d :], split[:rank]]
        + pick(g_ctx_up)
        + [split[rank : 2 * rank], split[2 * rank :]]
        + [jnp.broadcast_to(adapter_index[0].astype(F32) / seq, (rank, HEAD_DIM))],
        axis=1,
    )
    late_at = chains.add(adapter_steps(late, 5 * d))
    chains.start(late_at)
    while chains.live() or (line and line.live()):
        tied = seal(*chains.arrived(), *(line.moving if line else []))
        count = len(chains.arrived())
        chains.put(tied[:count])
        chains.step()
        if line and line.moving:
            line.receive(tied[count:])
            if line.live():
                line.send()
    early, late, context_grad = chains.result(early_at), chains.result(late_at), chains.result(ctx_at).astype(F32)
    if line:
        result, input_grad = jnp.concatenate(line.out[:groups]), jnp.concatenate(line.out[groups:])
    else:
        input_grad = lax.psum(jnp.concatenate(q_parts), "tensor")

    indices = jnp.round(late[:, 0, -1].astype(F32)).astype(jnp.int32)
    early, late = spread(early, indices, slots), spread(late[:, :, :-HEAD_DIM], indices, slots)
    cut = lambda grads, start, size, count: [
        grads[:, :, start + j * size : start + (j + 1) * size] for j in range(count)
    ]
    wide, feed = cut(early, 0, d, 5), cut(early, 5 * d, ff, 2)
    wide_late, narrow = cut(late, 0, d, 5), cut(late, 5 * d, width, 8)
    swap = lambda a: jnp.swapaxes(a, -1, -2)
    return (
        result[None],
        input_grad[None],
        context_grad,
        swap(jnp.stack(wide_late[:3] + wide[:1] + wide_late[3:], axis=1)),
        jnp.stack(narrow[:6], axis=1),
        swap(wide[1]),
        feed[0],
        swap(jnp.stack(narrow[6:], axis=1)),
        jnp.stack(wide[2:4], axis=1),
        swap(feed[1]),
        wide[4],
    )


def solution(mesh):
    placed = (
        P("dp", "seq", None),
        P(None, "dp", "seq"),
        P("dp", None, None),
        P(),
        P(),
        P("dp"),
        P(None, None, "tensor"),
        P(None, "tensor"),
        P(None, "tensor"),
        P("tensor", None),
        P(None, None, "tensor"),
        P(None, "tensor"),
        P(None, "tensor"),
        P("tensor", None),
        P(),
        P(),
        P(None, "tensor"),
        P("tensor"),
        P("tensor", None),
        P(),
        P(),
        P(None, None, None, "tensor"),
        P(),
        P(None, None, "tensor"),
        P(None, None, "tensor", None),
        P(),
        P(None, "tensor", None),
        P(),
        P("dp", "seq", None),
    )
    return jax.shard_map(
        per_device,
        mesh=mesh,
        in_specs=placed,
        out_specs=(
            P("dp", "seq", None),
            P("dp", "seq", None),
            P(),
            P(),
            P(None, None, None, "tensor"),
            P(),
            P(None, None, "tensor"),
            P(None, None, "tensor", None),
            P(),
            P(None, "tensor", None),
            P(),
        ),
        check_vma=False,
    )
```

```python
import functools
import math

import jax
import jax.numpy as jnp
import numpy as np
from jax import lax
from jax.experimental import pallas as pl
from jax.experimental.pallas import tpu as pltpu
from jax.sharding import PartitionSpec as P

F32 = jnp.float32
BF16 = jnp.bfloat16
HEAD_DIM = 128
EPS = 1e-06
LOG2E = 1.4426950408889634
SCALE = HEAD_DIM ** (-0.5)
VMEM_LIMIT = 58 * 1024 * 1024
GELU_C = math.sqrt(2.0 / math.pi)
M0, M1, M2, M3, M4, M5, B0, B1, B2, CG, CB = range(11)
AT_T, AT_S, ADAPTER, PART, SLOTS = range(5)


def nn(left, right):
    return jnp.dot(left, right, preferred_element_type=F32)


def nt(left, right):
    return lax.dot_general(left, right, (((1,), (1,)), ((), ())), preferred_element_type=F32)


def row_total(values):
    ones = jnp.ones((8, values.shape[1]), BF16)
    high = values.astype(BF16)
    return nt(ones, high) + nt(ones, (values - high.astype(F32)).astype(BF16))


def mean(values):
    return jnp.mean(values, axis=-1, keepdims=True)


def normalize(values):
    centered = values - mean(values)
    inverse = lax.rsqrt(mean(centered * centered) + EPS)
    return centered * inverse, inverse


def normalize_back(normed, inverse, upstream):
    return inverse * (upstream - mean(upstream) - normed * mean(upstream * normed))


def pair_swap(values):
    width = values.shape[1]
    lane = lax.broadcasted_iota(jnp.int32, values.shape, 1)
    return jnp.where(lane % 2 == 0, pltpu.roll(values, width - 1, 1), pltpu.roll(values, 1, 1))


def rope(values, cosine, sine):
    return values * cosine + pair_swap(values) * sine


def rope_back(values, cosine, sine):
    return values * cosine - pair_swap(values) * sine


def heads_of(array, count):
    return [array[:, h * HEAD_DIM : (h + 1) * HEAD_DIM] for h in range(count)]


def whole(shape):
    return pl.BlockSpec(shape, lambda *_: (0,) * len(shape))


def run_kernel(body, meta, ins, outs, grid=(1,), scratch=(), us=1.0, aliases=None, after=()):
    count = len(ins)
    ins = list(ins) + [(a, pl.BlockSpec(memory_space=pl.ANY)) for a in after]
    arrays = [a for a, _ in ins]
    moved = sum(math.prod(a.shape) * a.dtype.itemsize for a in arrays[:count]) + sum(
        math.prod(s.shape) * s.dtype.itemsize for s, _ in outs
    )

    def reading(meta_ref, *refs):
        return body(meta_ref, *refs[:count], *refs[len(arrays) :])

    return pl.pallas_call(
        reading,
        grid_spec=pltpu.PrefetchScalarGridSpec(
            num_scalar_prefetch=1,
            grid=grid,
            in_specs=[s for _, s in ins],
            out_specs=[s for _, s in outs],
            scratch_shapes=list(scratch),
        ),
        out_shape=[s for s, _ in outs],
        input_output_aliases=aliases or {},
        compiler_params=pltpu.CompilerParams(vmem_limit_bytes=VMEM_LIMIT),
        cost_estimate=pl.CostEstimate(
            flops=int(us * 1.15e9), bytes_accessed=int(min(moved, us * 2e6)), transcendentals=0
        ),
    )(meta, *arrays)


def sds(shape, dtype):
    return jax.ShapeDtypeStruct(shape, dtype)


def qkv_kernel(head_count, meta, tok, mod, emb, b_out, cg, cb, w, up, dn, bias, gain, cos, sin, ctx_ssq, *outs):
    y1, lat_t, pre_q, pre_k, raw_q, kv, ssq, vec, up_s = outs
    width = head_count * HEAD_DIM
    rank = up.shape[2]
    modes = mod[...] + emb[...]

    @pl.when(pl.program_id(0) == 0)
    def _():
        row = lax.broadcasted_iota(jnp.int32, modes.shape, 0)
        rows = [modes + jnp.where((row == 1) | (row == 4), 1.0, 0.0), b_out[...].astype(F32), cg[...], cb[...]]
        vec[...] = jnp.concatenate(rows + [jnp.zeros((5, modes.shape[1]), F32)], axis=0)
        up_s[...] = jnp.zeros_like(up_s)
        for j in range(3):
            up_s[j * rank : (j + 1) * rank, j * width : (j + 1) * width] = up[0, j]

    normed, _ = normalize(tok[...].astype(F32))
    y = (normed * (1.0 + modes[1:2, :]) + modes[0:1, :]).astype(BF16)
    y1[...] = y
    down = jnp.concatenate([dn[0, j] for j in range(3)], axis=0)
    lat = nt(y, down).astype(BF16)
    lat_t[...] = nt(down, y).astype(BF16)
    totals = []
    for j in range(3):
        lanes = slice(j * width, (j + 1) * width)
        u = nn(y, w[j]) + nn(lat, up_s[:, lanes]) + bias[j : j + 1, :].astype(F32)
        if j == 2:
            kv[:, width:] = u.astype(BF16)
            continue
        (pre_q, pre_k)[j][...] = u.astype(BF16)
        totals.append(row_total(u * u))
        scaled = u * gain[j : j + 1, :].astype(F32)
        for h in range(head_count):
            lanes = slice(h * HEAD_DIM, (h + 1) * HEAD_DIM)
            (raw_q, kv)[j][:, lanes] = rope(scaled[:, lanes], cos[...], sin[...]).astype(BF16)
    row = lax.broadcasted_iota(jnp.int32, totals[0].shape, 0)
    ssq[...] = jnp.where(row == 0, totals[0], jnp.where(row == 1, totals[1], ctx_ssq[...]))


def attention_kernel(groups, meta, raw_q, st, st_own, st_sib, k_own, k_sib, v_own, v_sib, *outs):
    blocks, out, lse, kn, vt = outs[:groups], outs[groups], outs[groups + 1], outs[groups + 2], outs[groups + 3]
    count = k_own.shape[0]
    step = pl.program_id(1)

    @pl.when(step == 0)
    def _():
        for at, (k, s, v) in enumerate(((k_own, st_own, v_own), (k_sib, st_sib, v_sib))):
            rows = slice(at * count, (at + 1) * count)
            kn[rows, :] = (k[...].astype(F32) * s[...].T[:, 1:2]).astype(BF16)
            vt[:, rows] = v[...].astype(F32).T.astype(BF16)

    q = (raw_q[...].astype(F32) * (st[...].T[:, 0:1] * (SCALE * LOG2E))).astype(BF16)
    scores = nt(kn[...], q)
    highest = jnp.max(scores, axis=0, keepdims=True)
    e = jnp.exp2(scores - highest)
    total = jnp.sum(e, axis=0, keepdims=True)
    mixed = (nn(vt[...], e.astype(BF16)) / total).T.astype(BF16)
    out[...] = mixed
    for r in range(groups):

        @pl.when(step == r)
        def _(r=r):
            blocks[r][...] = mixed

    lse[...] = jnp.broadcast_to(highest + jnp.log2(total), lse.shape)


def attention_back_kernel(groups, first, meta, raw_q, st, st_own, st_sib, k_own, k_sib, v_own, v_sib, out, lse, *rest):
    grads, rest = rest[:groups], rest[groups:]
    if not first:
        stat_in, cross_in = rest[:2]
        rest = rest[2:]
    dq, dkv_own, dkv_sib, stat, cross, kn, knt, vn, dk_acc, dv_acc, g_s = rest
    count = k_own.shape[0]
    size = raw_q.shape[0]
    step = pl.program_id(0)

    @pl.when(step == 0)
    def _():
        for at, (k, s, v) in enumerate(((k_own, st_own, v_own), (k_sib, st_sib, v_sib))):
            rows = slice(at * count, (at + 1) * count)
            scaled = k[...].astype(F32) * s[...].T[:, 1:2]
            kn[rows, :] = scaled.astype(BF16)
            knt[:, rows] = scaled.T.astype(BF16)
            vn[rows, :] = v[...]
        dk_acc[...] = jnp.zeros_like(dk_acc)
        dv_acc[...] = jnp.zeros_like(dv_acc)
        stat[...] = jnp.zeros_like(stat) if first else stat_in[...]
        cross[...] = jnp.zeros_like(cross) if first else cross_in[...]

    for r in range(groups):

        @pl.when(step == r)
        def _(r=r):
            g_s[...] = grads[r][...]

    raw = raw_q[...].astype(F32)
    q = (raw * (st[...].T[:, 0:1] * (SCALE * LOG2E))).astype(BF16)
    g = g_s[...]
    delta = row_total(g.astype(F32) * out[...].astype(F32))[0:1, :]
    p = jnp.exp2(nt(kn[...], q) - lse[0:1, :])
    dv_acc[...] += nn(p.astype(BF16), g)
    ds = (p * (nt(vn[...], g) - delta)).astype(BF16)
    dk_acc[...] += nn(ds, q)
    dqs = nn(knt[...], ds).T * SCALE
    dq[...] = dqs
    lanes = pl.ds(pl.multiple_of(lax.rem(meta[AT_T] + step, groups) * size, size), size)
    total = row_total(dqs * raw)
    stat[:, lanes] += jnp.where(lax.broadcasted_iota(jnp.int32, total.shape, 0) == 0, total, 0.0)

    @pl.when(step == pl.num_programs(0) - 1)
    def _():
        for at, (k, dkv, sums) in enumerate(((k_own, dkv_own, stat), (k_sib, dkv_sib, cross))):
            rows = slice(at * count, (at + 1) * count)
            dk = dk_acc[rows, :] * (1.0 / LOG2E)
            dkv[:, :HEAD_DIM] = dk.astype(dkv.dtype)
            dkv[:, HEAD_DIM:] = dv_acc[rows, :].astype(dkv.dtype)
            all_k = row_total(dk * k[...].astype(F32))
            sums[...] += jnp.where(lax.broadcasted_iota(jnp.int32, all_k.shape, 0) == 1, all_k, 0.0)


def qkv_back_kernel(head_count, call, meta, *refs):
    n = head_count
    dq, dkv, dkv_in = (refs[j * n : (j + 1) * n] for j in range(3))
    refs = refs[3 * n :]
    pre_q, pre_k, st, st_back, gain_in, cos, sin, w, up_in, dn_in, tok, vec, y1, lat_t, dx1 = refs[:15]
    packed_in = refs[15] if call else None
    part, packed, up, w_s, sem = refs[-5:]
    step = pl.program_id(0)
    fetch = pltpu.make_async_copy(w, w_s, sem)

    @pl.when(step == 0)
    def _():
        fetch.start()
        packed[...] = packed_in[...] if call else jnp.zeros_like(packed)

    inverse, cubed = st[...].T, st_back[...].T
    c, s = cos[...], sin[...]
    width = n * HEAD_DIM
    rank = up_in.shape[2]
    d = tok.shape[1]
    gain = gain_in[...].astype(F32)
    up[...] = jnp.zeros_like(up)
    for j in range(3):
        up[j * rank : (j + 1) * rank, j * width : (j + 1) * width] = up_in[0, j]
    dn = jnp.concatenate([dn_in[0, j] for j in range(3)], axis=0)
    dk = [a[:, :HEAD_DIM] + b[:, :HEAD_DIM].astype(F32) for a, b in zip(dkv, dkv_in)]
    dv = [a[:, HEAD_DIM:] + b[:, HEAD_DIM:].astype(F32) for a, b in zip(dkv, dkv_in)]
    grads = [
        jnp.concatenate([rope_back(ref[...], c, s) for ref in dq], axis=1),
        jnp.concatenate([rope_back(a, c, s) for a in dk], axis=1),
        jnp.concatenate(dv, axis=1).astype(BF16),
    ]
    for j, pre in enumerate((pre_q, pre_k)):
        grads[j] = (
            inverse[:, j : j + 1] * gain[j : j + 1, :] * grads[j] - pre[...].astype(F32) * cubed[:, j : j + 1]
        ).astype(BF16)
    joined = jnp.concatenate(grads, axis=1)
    d_lat = nt(joined, up[...]).astype(BF16)
    d_lat_t = nt(up[...], joined).astype(BF16)
    total = nn(d_lat, dn)

    @pl.when(step == 0)
    def _():
        fetch.wait()

    for j in range(3):
        total = total + nt(grads[j], w_s[j])
    normed, inverse = normalize(tok[...].astype(F32))
    back = normalize_back(normed, inverse, total * vec[M1 : M1 + 1, :])
    own = (meta[AT_T] == call * pl.num_programs(0) + step).astype(F32)
    part[...] = (back + dx1[...] * own).astype(part.dtype)
    g_dn = nn(d_lat_t, y1[...])
    for j in range(3):
        rows = slice(j * rank, (j + 1) * rank)
        g_up = nn(lat_t[rows, :], grads[j])
        for start, g in ((j * d, g_dn[rows, :]), (3 * d + j * width, g_up)):
            lanes = slice(start, start + g.shape[1])
            packed[:, lanes] += g


def context_kernel(groups, meta, ctx, w, up, dn, bias, gain, up_q, down_row, pre, low, ssq, lat_t):
    key = meta[AT_S] == 0
    c = ctx[...]
    count = c.shape[0]
    rank, width = up.shape[2:]
    lat = nt(c, dn[0, 0]).astype(BF16)
    lat_t[...] = nt(dn[0, 0], c).astype(BF16)
    b, g = bias[...].astype(F32), gain[...].astype(F32)
    u = nn(c, w[0]) + nn(lat, up[0, 0]) + jnp.where(key, b[1:2, :], b[2:3, :])
    pre[...] = u
    low[:count, :] = (u * jnp.where(key, g[1:2, :], 1.0)).astype(BF16)
    low[count : count + rank, :] = up_q[0, 0]
    low[count + rank : count + 2 * rank, :] = down_row[0, 0]
    low[count + 2 * rank : count + 3 * rank, :] = down_row[0, 1]
    row = lax.broadcasted_iota(jnp.int32, (rank, width), 0)
    low[count + 3 * rank :, :] = jnp.where(row == 0, b[0:1, :], jnp.where(row == 1, g[0:1, :], 0.0)).astype(BF16)
    total = row_total(u * u)
    share, block = count // groups, ssq.shape[1] // groups
    ssq[...] = jnp.zeros_like(ssq)
    for j in range(groups):
        ssq[:, j * block : j * block + share] = total[:, j * share : (j + 1) * share]


def context_row(groups, count, rows):
    share, block = count // groups, rows.shape[1] // groups
    return jnp.concatenate([rows[2:3, j * block : j * block + share] for j in range(groups)], axis=1)


def context_back_kernel(meta, ctx, w, up_in, dn_in, lat_t, grad, out, g_up, g_dn):
    g = grad[...]
    up, dn = up_in[0, 0], dn_in[0, 0]
    d_lat = nt(g, up).astype(BF16)
    d_lat_t = nt(up, g).astype(BF16)
    out[...] = nt(g, w[0]) + nn(d_lat, dn)
    g_up[...] = nn(lat_t[...], g)
    g_dn[...] = nn(d_lat_t, ctx[...])


def pack_kernel(meta, wo, wq, wc, out):
    rows, width = wo.shape[0], wq.shape[2]
    out[:rows, :] = wo[...]
    for j in range(out.shape[1] // width):
        out[rows : 2 * rows, j * width : (j + 1) * width] = wq[0, j * rows : (j + 1) * rows, :]
    out[2 * rows :, :] = wc[...]


def stack_kernel(meta, *refs):
    for j, ref in enumerate(refs[:-1]):
        refs[-1][j] = ref[...]


def start_copies(meta, plan, refs, targets, sems, own):
    copies = [[] for _ in targets]
    at = 0
    for source, weight, first, rows, slot, inner, size in plan:
        target = targets[weight]
        width = target.shape[2]
        sides = refs[source].shape[2] // width
        for j in range(sides):
            start = pl.multiple_of(meta[slot] * (size * sides) + (j * size + inner), 16)
            copies[weight].append(
                pltpu.make_async_copy(
                    refs[source].at[:, pl.ds(first, rows), pl.ds(j * width, width)],
                    target.at[pl.ds(target.shape[0] - refs[source].shape[0], refs[source].shape[0]), pl.ds(start, rows), :],
                    sems.at[at],
                )
            )
            at += 1
    for weight, shard in own.items():
        copies[weight].append(pltpu.make_async_copy(shard, targets[weight].at[0], sems.at[at]))
        at += 1
    for weight in copies:
        for copy in weight:
            copy.start()
    return copies


def finish(copies):
    for copy in copies:
        copy.wait()


def cross_kernel(groups, head_count, plan, meta, *refs):
    n = groups * head_count
    os_first, os_rest, refs = refs[:groups], refs[groups : 2 * groups], refs[2 * groups :]
    tok, vec, up, dn3 = refs[:4]
    ctx_own, ctx_sib, refs = refs[4 : 4 + groups], refs[4 + groups : 4 + 2 * groups], refs[4 + 2 * groups :]
    st_own, st_sib, wo_own, wq_own, wc_own = refs[:5]
    k = 1 + max(entry[0] for entry in plan)
    sources, refs = refs[5 : 5 + k], refs[5 + k :]
    y2, x2, x1, y3, qn, qc, oc, os_all, lse, lats = refs[:10]
    wo, wq, wc, sems = refs[10:]
    copies = start_copies(meta, plan, sources, (wo, wq, wc), sems, {0: wo_own, 2: wc_own})
    full = lambda weight: weight[...].reshape(weight.shape[0] * weight.shape[1], weight.shape[2])
    dn3 = dn3[0, 0]
    rank = dn3.shape[0]
    ctx_len = ctx_own[0].shape[0] - 4 * rank
    small = jnp.concatenate([ctx_own[r][ctx_len:, :] for r in range(groups)], axis=1)
    first = meta[AT_S] == 0
    key_row = context_row(groups, ctx_len, jnp.where(first, st_own[...], st_sib[...]))
    ctx_inverse = jnp.broadcast_to(key_row, (8, ctx_len)).T[:, 0:1]
    width = head_count * HEAD_DIM
    for r in range(groups):
        middle = r * width + os_first[r].shape[1]
        os_all[:, r * width : middle] = os_first[r][...]
        os_all[:, middle : (r + 1) * width] = os_rest[r][...]
    os_v = os_all[...]
    down0, down1 = small[rank : 2 * rank, :], small[2 * rank : 3 * rank, :]
    lat = nt(os_v, down0).astype(BF16)
    lats[0:rank, :] = nt(down0, os_v).astype(BF16)
    total = nn(lat, up[0, 0])
    finish(copies[0])
    total = total + nn(os_v, full(wo))
    x1_v = tok[...].astype(F32) + (total + vec[B0 : B0 + 1, :]) * vec[M2 : M2 + 1, :]
    x1[...] = x1_v
    normed, _ = normalize(x1_v)
    y3_v = (normed * vec[CG : CG + 1, :] + vec[CB : CB + 1, :]).astype(BF16)
    y3[...] = y3_v
    lat = nt(y3_v, dn3).astype(BF16)
    lats[2 * rank : 3 * rank, :] = nt(dn3, y3_v).astype(BF16)
    finish(copies[1])
    q = nn(lat, small[0:rank, :]) + small[3 * rank : 3 * rank + 1, :].astype(F32)
    q = q + jnp.concatenate([nn(y3_v, wq[r - 1] if r else wq_own[0]) for r in range(groups)], axis=1)
    qc[...] = q
    inverse = lax.rsqrt(mean(q * q) + EPS)
    gain = small[3 * rank + 1 : 3 * rank + 2, :].astype(F32)
    qn[...] = (q * (inverse * (SCALE * LOG2E)) * gain).astype(BF16)
    for j in range(n):
        r, lanes = j // head_count, slice((j % head_count) * HEAD_DIM, (j % head_count + 1) * HEAD_DIM)
        a, b = ctx_own[r][:ctx_len, lanes], ctx_sib[r][:ctx_len, lanes]
        keys, values = jnp.where(first, a, b), jnp.where(first, b, a)
        keys = (keys.astype(F32) * ctx_inverse).astype(BF16)
        scores = nt(keys, qn[:, j * HEAD_DIM : (j + 1) * HEAD_DIM])
        highest = jnp.max(scores, axis=0, keepdims=True)
        e = jnp.exp2(scores - highest)
        sums = jnp.sum(e, axis=0, keepdims=True)
        mixed = nn(values.astype(F32).T.astype(BF16), e.astype(BF16)) / sums
        oc[:, j * HEAD_DIM : (j + 1) * HEAD_DIM] = mixed.T.astype(BF16)
        lse[j : j + 1, :] = highest + jnp.log2(sums)
    oc_v = oc[...]
    lat = nt(oc_v, down1).astype(BF16)
    lats[rank : 2 * rank, :] = nt(down1, oc_v).astype(BF16)
    total = nn(lat, up[0, 1])
    finish(copies[2])
    total = total + nn(oc_v, full(wc))
    x2_v = x1_v + total + vec[B1 : B1 + 1, :]
    x2[...] = x2_v
    normed, _ = normalize(x2_v)
    y2[...] = (normed * vec[M4 : M4 + 1, :] + vec[M3 : M3 + 1, :]).astype(BF16)


def cross_back_kernel(groups, head_count, plan, meta, *refs):
    n = groups * head_count
    dy_own, dy_in, og, x2, x1, y3, qn, qc, oc, os_all, lse, lats, vec, up, dn3 = refs[:15]
    ctx_own, ctx_sib, refs = refs[15 : 15 + groups], refs[15 + groups : 15 + 2 * groups], refs[15 + 2 * groups :]
    st_own, st_sib, wo_own, wq_own, wc_own = refs[:5]
    k = 1 + max(entry[0] for entry in plan)
    sources, refs = refs[5 : 5 + k], refs[5 + k :]
    dos_first, dos_rest, refs = refs[:groups], refs[groups : 2 * groups], refs[2 * groups :]
    dx1, g_own, g_oth, g_up, g_split, g_dn, wo, wq, wc, dq_s, sems = refs
    copies = start_copies(meta, plan, sources, (wo, wq, wc), sems, {0: wo_own, 2: wc_own})
    full = lambda weight: weight[...].reshape(weight.shape[0] * weight.shape[1], weight.shape[2])
    dn3 = dn3[0, 0]
    rank = dn3.shape[0]
    ctx_len = ctx_own[0].shape[0] - 4 * rank
    small = jnp.concatenate([ctx_own[r][ctx_len:, :] for r in range(groups)], axis=1)
    first = meta[AT_S] == 0
    key_row = context_row(groups, ctx_len, jnp.where(first, st_own[...], st_sib[...]))
    ctx_inverse = jnp.broadcast_to(key_row, (8, ctx_len)).T[:, 0:1]
    width = head_count * HEAD_DIM
    down0, down1 = small[rank : 2 * rank, :], small[2 * rank : 3 * rank, :]
    normed, inverse = normalize(x2[...])
    dn = (dy_own[...] + dy_in[...].astype(F32)) * vec[M4 : M4 + 1, :]
    dx2 = og[...].astype(F32) + normalize_back(normed, inverse, dn)
    grad = dx2.astype(BF16)
    d_lat = nt(grad, up[0, 1]).astype(BF16)
    d_lat_t = nt(up[0, 1], grad).astype(BF16)
    oc_v = oc[...]
    g_up[rank : 2 * rank, :] = nn(lats[rank : 2 * rank, :], grad)
    split = nn(d_lat_t, oc_v)
    for r in range(groups):
        g_split[r, 2 * rank : 3 * rank, :] = split[:, r * width : (r + 1) * width]
    finish(copies[2])
    d_oc = nn(d_lat, down1) + nt(grad, full(wc))
    d_oc = d_oc.astype(BF16)
    for j in range(n):
        r, lanes = j // head_count, slice((j % head_count) * HEAD_DIM, (j % head_count + 1) * HEAD_DIM)
        head = slice(j * HEAD_DIM, (j + 1) * HEAD_DIM)
        a, b = ctx_own[r][:ctx_len, lanes], ctx_sib[r][:ctx_len, lanes]
        keys, values = jnp.where(first, a, b), jnp.where(first, b, a)
        keys = (keys.astype(F32) * ctx_inverse).astype(BF16)
        q, g = qn[:, head], d_oc[:, head]
        delta = row_total(g.astype(F32) * oc_v[:, head].astype(F32))[0:1, :]
        p = jnp.exp2(nt(keys, q) - lse[j : j + 1, :])
        dv = nn(p.astype(BF16), g)
        ds = (p * (nt(values, g) - delta)).astype(BF16)
        dk = nn(ds, q) * (1.0 / LOG2E)
        dq_s[:, head] = nn(keys.astype(F32).T.astype(BF16), ds).T * SCALE
        g_own[r, :, lanes] = jnp.where(first, dk, dv).astype(BF16)
        g_oth[r, :, lanes] = jnp.where(first, dv, dk).astype(BF16)
    q = qc[...]
    inverse = lax.rsqrt(mean(q * q) + EPS)
    gain = small[3 * rank + 1 : 3 * rank + 2, :].astype(F32)
    scaled = dq_s[...] * gain
    stat = mean(scaled * q)
    dqc = (inverse * scaled - q * (inverse * inverse * inverse * stat)).astype(BF16)
    up_q = small[0:rank, :]
    d_lat = nt(dqc, up_q).astype(BF16)
    d_lat_t = nt(up_q, dqc).astype(BF16)
    split = nn(lats[2 * rank : 3 * rank, :], dqc)
    for r in range(groups):
        g_split[r, 0:rank, :] = split[:, r * width : (r + 1) * width]
    g_dn[...] = nn(d_lat_t, y3[...])
    dy3 = nn(d_lat, dn3)
    finish(copies[1])
    for r in range(groups):
        part = dqc[:, r * width : (r + 1) * width]
        dy3 = dy3 + nt(part, wq[r - 1] if r else wq_own[0])
    normed, inverse = normalize(x1[...])
    dx1_v = dx2 + normalize_back(normed, inverse, dy3 * vec[CG : CG + 1, :])
    dx1[...] = dx1_v
    grad = (dx1_v * vec[M2 : M2 + 1, :]).astype(BF16)
    d_lat = nt(grad, up[0, 0]).astype(BF16)
    d_lat_t = nt(up[0, 0], grad).astype(BF16)
    g_up[0:rank, :] = nn(lats[0:rank, :], grad)
    split = nn(d_lat_t, os_all[...])
    for r in range(groups):
        g_split[r, rank : 2 * rank, :] = split[:, r * width : (r + 1) * width]
    finish(copies[0])
    d_os = nn(d_lat, down0) + nt(grad, full(wo))
    for r in range(groups):
        block = d_os[:, r * width : (r + 1) * width]
        dos_first[r][...] = block[:, :HEAD_DIM].astype(BF16)
        dos_rest[r][...] = block[:, HEAD_DIM:].astype(BF16)


def feed_kernel(tiles, first, meta, *refs):
    y2, og, vec, bias, dn1, up1, dn2, up2, w1_h, w2_h = refs[:10]
    if first:
        x2 = refs[10]
    else:
        acc = refs[10:14]
    refs = refs[11:] if first else refs[15:]
    dn1, up1, dn2, up2 = dn1.at[0], up1.at[0], dn2.at[0], up2.at[0]
    out, dy, g_up1, g_dn1, g_up2, g_dn2, w1, w2, sems = refs
    copies = []
    for at, (start, size) in enumerate(tiles):
        rows = pl.ds(start, size)
        pair = [
            pltpu.make_async_copy(h.at[rows, :], v.at[rows, :], sems.at[j, at])
            for j, (h, v) in enumerate(((w1_h, w1), (w2_h, w2)))
        ]
        for copy in pair:
            copy.start()
        copies.append(pair)
    y = y2[...]
    dff = (og[...].astype(F32) * vec[M5 : M5 + 1, :]).astype(BF16)
    lat = nt(y, dn1[...]).astype(BF16)
    lat_t = nt(dn1[...], y).astype(BF16)
    drl = nt(dff, up2[...]).astype(BF16)
    drl_t = nt(up2[...], dff).astype(BF16)
    part = grad = rl = rl_t = d_lat = d_lat_t = 0.0
    for (start, size), pair in zip(tiles, copies):
        cols = slice(start, start + size)
        finish(pair)
        h = nt(y, w1[cols, :]) + nn(lat, up1[:, cols]) + bias[:, cols]
        du = nt(dff, w2[cols, :]) + nn(drl, dn2[:, cols])
        sq = h * h
        t = jnp.tanh(GELU_C * h * (1.0 + 0.044715 * sq))
        act = (0.5 * h * (1.0 + t)).astype(BF16)
        slope = 0.5 * (1.0 + t) + (0.5 * GELU_C) * h * (1.0 - t * t) * (1.0 + (3.0 * 0.044715) * sq)
        dh = (du * slope).astype(BF16)
        part = part + nn(act, w2[cols, :])
        grad = grad + nn(dh, w1[cols, :])
        rl = rl + nt(act, dn2[:, cols])
        rl_t = rl_t + nt(dn2[:, cols], act)
        d_lat = d_lat + nt(dh, up1[:, cols])
        d_lat_t = d_lat_t + nt(up1[:, cols], dh)
        new_up1, new_dn2 = nn(lat_t, dh), nn(drl_t, act)
        g_up1[:, cols] = new_up1 if first else new_up1 + acc[0][:, cols]
        g_dn2[:, cols] = new_dn2 if first else new_dn2 + acc[3][:, cols]
    part = part + nn(rl.astype(BF16), up2[...])
    grad = grad + nn(d_lat.astype(BF16), dn1[...])
    new_dn1, new_up2 = nn(d_lat_t.astype(BF16), y), nn(rl_t.astype(BF16), dff)
    g_dn1[...] = new_dn1 if first else new_dn1 + acc[1][...]
    g_up2[...] = new_up2 if first else new_up2 + acc[2][...]
    part = part * vec[M5 : M5 + 1, :]
    if first:
        part = part + x2[...] + vec[B2 : B2 + 1, :] * vec[M5 : M5 + 1, :]
    out[...] = part.astype(out.dtype)
    dy[...] = grad.astype(dy.dtype)


def shift(count, step):
    return [(a, (a + step) % count) for a in range(count)]


def flip(count, step):
    return [(a, a ^ step) for a in range(count)]


def powers(count):
    return [1 << j for j in range(count.bit_length() - 1)]


def send(values, axis, pairs):
    return jax.tree.map(lambda v: lax.ppermute(v, axis, pairs), values)


def ring_pieces(own, axis):
    count = lax.axis_size(axis)
    pieces = [own]
    for _ in range(count - 1):
        pieces.append(send(pieces[-1], axis, shift(count, 1)))
    return pieces


def ring_total(parts, axis):
    count = lax.axis_size(axis)
    moving = parts[1]
    for r in range(2, count):
        moving = send(moving, axis, shift(count, 1))
        moving = (moving.astype(F32) + parts[r].astype(F32)).astype(BF16)
    return parts[0], send(moving, axis, shift(count, 1))


def gather_direct(own, axis):
    count = lax.axis_size(axis)
    return [own] + [send(own, axis, shift(count, r)) for r in range(1, count)]


def scatter_direct(parts, axis):
    count = lax.axis_size(axis)
    return parts[0].astype(F32) + sum(
        send(parts[r].astype(BF16), axis, shift(count, -r)).astype(F32) for r in range(1, count)
    )


def gather_flipped(own, axis):
    count = lax.axis_size(axis)
    return [own] + [send(own, axis, flip(count, j)) for j in range(1, count)]


def total_flipped(own, axis):
    terms = [v.astype(F32) for v in gather_flipped(own, axis)]
    while len(terms) > 1:
        terms = [terms[j] + terms[j + 1] for j in range(0, len(terms), 2)]
    return terms[0]


def halves(values, axis):
    half = values.shape[0] // 2
    low, high = values[:half], values[half:]
    upper = lax.axis_index(axis) == 1
    return jnp.where(upper, high, low), jnp.where(upper, low, high)


def pair_scatter(values):
    kept, sent = halves(values, "seq")
    return kept + send(sent.astype(BF16), "seq", flip(2, 1)).astype(F32)


def pair_gather(values, dim):
    other = send(values, "seq", flip(2, 1))
    upper = lax.axis_index("seq") == 1
    return jnp.concatenate([jnp.where(upper, other, values), jnp.where(upper, values, other)], axis=dim)


def place_blocks(blocks, axis):
    size = blocks[0].shape[0]
    out = jnp.zeros((size * len(blocks),) + blocks[0].shape[1:], blocks[0].dtype)
    index = lax.axis_index(axis)
    for j, block in enumerate(blocks):
        out = lax.dynamic_update_slice_in_dim(out, block, (index ^ j) * size, 0)
    return out


def total_twice(values, axis):
    for step in powers(lax.axis_size(axis)):
        values = values + send(values, axis, flip(lax.axis_size(axis), step))
    return values


class Chains:
    def __init__(self):
        self.chains, self.values, self.results = [], [], {}

    def add(self, chain):
        self.chains.append(chain)
        self.values.append(None)
        return len(self.chains) - 1

    def start(self, at):
        self.advance(at)

    def advance(self, at):
        try:
            self.values[at] = self.chains[at].send(self.values[at])
        except StopIteration as end:
            self.results[at] = end.value

    def step(self, skip=()):
        for at in range(len(self.chains)):
            if at not in self.results and at not in skip:
                self.advance(at)

    def live(self):
        return len(self.results) < len(self.chains)

    def done(self, at):
        return at in self.results

    def result(self, at):
        return self.results[at]

    def arrived(self):
        live = [self.values[at] for at in range(len(self.chains)) if at not in self.results]
        return jax.tree.leaves(live)

    def put(self, leaves):
        places = [at for at in range(len(self.chains)) if at not in self.results]
        structure = jax.tree.structure([self.values[at] for at in places])
        for at, value in zip(places, jax.tree.unflatten(structure, leaves)):
            self.values[at] = value


def seal(*values):
    return list(lax.optimization_barrier(values)) if values else []


def ring_steps(parts, axis):
    count = lax.axis_size(axis)
    moving = parts[1].astype(BF16)
    for r in range(2, count + 1):
        moving = yield send(moving, axis, shift(count, 1))
        if r < count:
            moving = (moving.astype(F32) + parts[r].astype(F32)).astype(BF16)
    return parts[0].astype(F32) + moving.astype(F32)


def line_kernel(shape, meta, *refs):
    inward, across, outward, both = shape
    inner = (meta[AT_T] == 1) | (meta[AT_T] == 2)
    count = (inward or outward) + inward + 2 * across + outward + both
    ins, outs = list(refs[:count]), list(refs[count:])
    add = lambda a, b: (a[...].astype(F32) + b[...].astype(F32)).astype(BF16)
    if inward or outward:
        first = ins.pop(0)
    if inward:
        outs.pop(0)[...] = add(ins.pop(0), first)
    if across:
        total = add(ins.pop(0), ins.pop(0))
        outs.pop(0)[...] = jnp.where(inner, total, ins.pop(0)[...]) if both else total
    if outward:
        outs.pop(0)[...] = jnp.where(inner, ins.pop(0)[...], first[...])


class Line:
    def __init__(self, meta, size):
        self.meta, self.size = meta, size
        self.parts, self.targets, self.outs = [], [], {}
        self.acc, self.total, self.at, self.moving = {}, {}, 0, []

    def add(self, array, block, target, out_block):
        self.parts.append((array, block))
        self.targets.append((target, out_block))

    def start(self):
        array, block = self.parts[self.at] if self.at < len(self.parts) else (None, None)
        inward, outward = array is not None, self.at - 2 in self.total
        pairs = [(0, 1), (3, 2)] * inward + [(1, 0), (2, 3)] * outward
        if inward and outward:
            mine = self.total[self.at - 2]
        elif inward:
            mine = array[block * self.size : (block + 1) * self.size]
        else:
            mine = self.total.get(self.at - 2)
        self.moving = [send(mine, "tensor", pairs)] if pairs else []
        across = self.at - 1 in self.acc
        if across:
            self.moving.append(send(self.acc[self.at - 1], "tensor", [(1, 2), (2, 1)]))
        self.shape = (inward, across, outward)

    def advance(self, moving):
        inward, across, outward = self.shape
        moving, at = list(moving), self.at
        first = moving.pop(0) if inward or outward else None
        second = moving.pop(0) if across else None
        both = across and at + 1 < len(self.parts)
        grid = 4
        rows = lambda block: pl.BlockSpec((self.size // grid, width), lambda b, m: (block * grid + b, 0))
        width = (second if first is None else first).shape[1]
        kind = sds((self.size, width), BF16)
        ins, outs, aliases = [], [], None
        if first is not None:
            ins.append((first, rows(0)))
        if inward:
            array, block = self.parts[at]
            ins.append((array, rows(block)))
            outs.append((kind, rows(0)))
        if across:
            ins += [(self.acc[at - 1], rows(0)), (second, rows(0))]
            outs.append((kind, rows(0)))
        if both:
            array, block = self.parts[at + 1]
            ins.append((array, rows(block)))
        if outward:
            ins.append((self.total[at - 2], rows(0)))
        count = len(ins)
        if outward:
            target, block = self.targets[at - 2]
            length = self.size * sum(t == target for t, _ in self.targets)
            outs.append((sds((length, width), BF16), rows(block)))
            if target in self.outs:
                ins.append((self.outs[target], pl.BlockSpec(memory_space=pl.ANY)))
                aliases = {count + 1: len(outs) - 1}

        def body(meta, *refs):
            line_kernel((inward, across, outward, both), meta, *refs[:count], *refs[len(ins) :])

        results = list(run_kernel(body, self.meta, ins, outs, grid=(grid,), us=3, aliases=aliases))
        if inward:
            self.acc[at] = results.pop(0)
        if across:
            self.total[at - 1] = results.pop(0)
        if outward:
            self.outs[self.targets[at - 2][0]] = results.pop(0)
        self.at, self.moving = at + 1, []
        if self.live():
            self.start()

    def live(self):
        return self.at < len(self.parts) + 2


def total_steps(value, axis):
    for step in powers(lax.axis_size(axis)):
        value = value + (yield send(value, axis, flip(lax.axis_size(axis), step)))
    return value


def adapter_steps(value, shared):
    groups, dp = lax.axis_size("tensor"), lax.axis_size("dp")
    pair, upper = flip(2, 1), lax.axis_index("seq") == 1
    kept, sent = halves(value, "seq")
    other = yield send(sent.astype(BF16), "seq", pair)
    value = kept + other.astype(F32)
    own, rest = value[:, :shared].astype(BF16), value[:, shared:].astype(BF16)
    for step in powers(groups):
        other = yield send(own, "tensor", flip(groups, step))
        own = (own.astype(F32) + other.astype(F32)).astype(BF16)
    value = jnp.concatenate([own, rest], axis=1)[None]
    for step in powers(dp):
        other = yield send(value, "dp", flip(dp, step))
        value = jnp.concatenate([value, other])
    other = yield send(value, "seq", pair)
    return jnp.concatenate([jnp.where(upper, other, value), jnp.where(upper, value, other)], axis=1)


def context_grad_steps(value):
    groups, dp = lax.axis_size("tensor"), lax.axis_size("dp")
    at_dp = lax.axis_index("dp")
    pair, second = flip(2, 1), lax.axis_index("seq") == 1
    kept, sent = halves(value, "seq")
    other = yield send(sent.astype(BF16), "seq", pair)
    value = kept + other.astype(F32)
    rows = value.shape[0] // dp
    parts = [lax.dynamic_slice_in_dim(value, (at_dp ^ j) * rows, rows, 0) for j in range(dp)]
    others = yield tuple(send(parts[j].astype(BF16), "dp", flip(dp, j)) for j in range(1, dp))
    value = (parts[0] + sum(other.astype(F32) for other in others)).astype(BF16)
    for step in powers(groups):
        other = yield send(value, "tensor", flip(groups, step))
        value = (value.astype(F32) + other.astype(F32)).astype(BF16)
    for step in powers(dp):
        other = yield send(value, "dp", flip(dp, step))
        upper = (at_dp & step) != 0
        value = jnp.concatenate([jnp.where(upper, other, value), jnp.where(upper, value, other)])
    other = yield send(value, "seq", pair)
    return jnp.concatenate([jnp.where(second, other, value), jnp.where(second, value, other)])


def weight_share():
    return 4 if lax.axis_size("dp") == 4 else 1


def weight_plan(rows, count):
    share, seq = weight_share(), lax.axis_size("seq")
    d, s = lax.axis_index("dp"), lax.axis_index("seq")
    slots = [(s ^ a) * share + ((d ^ b) if share > 1 else 0) for a in range(seq) for b in range(share)]
    total = rows * count
    cut = far_cut(total)
    half = [(0, 0, total, 0)]
    if share > 1:
        half += [(1, 0, total, 1), (2, 0, total, 2), (3, 0, cut, 3), (4, cut, total - cut, 3)]
    spans = half + [(len(half) + a, b, c, share + e) for a, b, c, e in half]
    plan = []
    for source, start, size, slot in spans:
        for weight in range(count):
            low, high = max(start, weight * rows), min(start + size, (weight + 1) * rows)
            if low < high:
                plan.append((source, weight, low - start, high - low, SLOTS + slot, low - weight * rows, rows))
    return plan, slots


def far_cut(total):
    return (total // 2 + 15) // 16 * 16


def rope_tables(grid_pos):
    sixth = HEAD_DIM // 6
    counts = [(HEAD_DIM - 4 * sixth) // 2, sixth, sixth]
    table = np.zeros((3, HEAD_DIM), np.float32)
    lane = 0
    for component, count in enumerate(counts):
        for pair in range(count):
            table[component, lane : lane + 2] = 10000.0 ** (-pair / count)
            lane += 2
    positions = grid_pos.astype(F32)
    angles = sum(positions[c][:, None] * table[c][None, :] for c in range(3))
    sign = np.where(np.arange(HEAD_DIM) % 2 == 0, -1.0, 1.0).astype(np.float32)
    return jnp.cos(angles), jnp.sin(angles) * sign[None, :]


def select_slot(table, index):
    return lax.dynamic_index_in_dim(table, index, 0, keepdims=False)


def spread(gradients, indices, slot_count):
    hits = (jnp.arange(slot_count)[:, None] == indices[None, :]).astype(F32)
    out = 0.0
    for latent in range(gradients.shape[0]):
        shape = (slot_count,) + (1,) * (gradients.ndim - 1)
        out = out + hits[:, latent].reshape(shape) * gradients[latent].astype(F32)[None]
    return out


def eight_rows(rows):
    return jnp.concatenate([jnp.stack(rows), jnp.zeros((8 - len(rows), rows[0].shape[0]), F32)])


def per_device(
    tokens,
    positions,
    time_emb,
    modulation,
    context,
    adapter_index,
    self_qkv,
    self_bias,
    self_gain,
    self_out,
    cross_qkv,
    cross_bias,
    cross_gain,
    cross_out,
    cross_norm_gain,
    cross_norm_bias,
    ffn_in,
    ffn_bias,
    ffn_out,
    out_bias,
    col_down,
    col_up,
    ffn1_down,
    ffn1_up,
    row_down,
    row_up,
    ffn2_down,
    ffn2_up,
    out_grad,
):
    groups = lax.axis_size("tensor")
    seq = lax.axis_size("seq")
    i, s = lax.axis_index("tensor"), lax.axis_index("seq")
    tl, d = tokens.shape[1:]
    tc = tl // groups
    ctx_len = context.shape[0]
    width = self_qkv.shape[2]
    hc = width // HEAD_DIM
    ff = ffn_in.shape[1]
    slots, rank = col_down.shape[0], col_down.shape[3]
    share = weight_share()
    slice_rows = width // (share * seq)
    plan, slot_list = weight_plan(slice_rows, 3)
    part_at = s * share + (lax.axis_index("dp") if share > 1 else 0)
    meta = jnp.stack([jnp.asarray(v, jnp.int32) for v in [i, s, adapter_index[0], part_at] + slot_list])
    tok, og = tokens[0], out_grad[0]
    block = pl.BlockSpec
    hbm = pl.BlockSpec(memory_space=pl.ANY)
    pair = flip(seq, 1)

    def table(array, *place, rows=1):
        if not place:
            return (array, block((1,) + array.shape[1:], lambda *a: (a[-1][ADAPTER],) + (0,) * (array.ndim - 1)))
        return (
            array,
            block(
                (1, rows) + array.shape[2:],
                lambda *a: (a[-1][ADAPTER], place[0](a[-1]) if callable(place[0]) else place[0], 0, 0),
            ),
        )

    col_dn, row_dn = jnp.swapaxes(col_down, 2, 3), jnp.swapaxes(row_down, 2, 3)
    feed_tables = [
        table(jnp.swapaxes(ffn1_down, 1, 2)),
        table(ffn1_up),
        table(jnp.swapaxes(ffn2_down, 1, 2)),
        table(ffn2_up),
    ]

    shard_at = lambda b, m: (m[PART], 0)
    (slices,) = run_kernel(
        pack_kernel,
        meta,
        [
            (self_out, block((slice_rows, d), shard_at)),
            (cross_qkv, block((1, slice_rows * groups, width), lambda b, m: (0, m[PART], 0))),
            (cross_out, block((slice_rows, d), shard_at)),
        ],
        [(sds((3 * slice_rows, d), BF16), whole((3 * slice_rows, d)))],
        us=1.5,
    )
    by_group = gather_direct(slices, "tensor")[1:]

    is_key = s == 0
    ctx_w = (cross_qkv, block((1, d, width), lambda b, m: (1 + m[AT_S], 0, 0)))
    ctx_up, ctx_dn = table(col_up, lambda m: 4 + m[AT_S]), table(col_dn, lambda m: 4 + m[AT_S])
    low_rows = ctx_len + 4 * rank
    ctx_pre, ctx_low, ctx_ssq, ctx_lat_t = run_kernel(
        functools.partial(context_kernel, groups),
        meta,
        [
            (context, whole(context.shape)),
            ctx_w,
            ctx_up,
            ctx_dn,
            (cross_bias, whole(cross_bias.shape)),
            (cross_gain, whole(cross_gain.shape)),
            table(col_up, 3),
            table(row_dn, 0, rows=2),
        ],
        [
            (sds((ctx_len, width), F32), whole((ctx_len, width))),
            (sds((low_rows, width), BF16), whole((low_rows, width))),
            (sds((8, tl), F32), whole((8, tl))),
            (sds((rank, ctx_len), BF16), whole((rank, ctx_len))),
        ],
        us=6,
        after=[slices],
    )
    cos, sin = rope_tables(positions[:, 0, :])
    rows_d = block((tc, d), lambda b, m: (b, 0))
    rows_w = block((tc, width), lambda b, m: (b, 0))
    rows_h = block((tc, HEAD_DIM), lambda b, m: (b, 0))
    lanes_8 = block((8, tc), lambda b, m: (0, b))
    self_tables = [table(col_up, 0, rows=3), table(col_dn, 0, rows=3)]
    y1, lat_t, pre_q, pre_k, raw_q, kv, ssq, vec = run_kernel(
        functools.partial(qkv_kernel, hc),
        meta,
        [
            (tok, rows_d),
            (modulation, whole(modulation.shape)),
            (time_emb[0], whole(modulation.shape)),
            (out_bias, whole(out_bias.shape)),
            (cross_norm_gain[None], whole((1, d))),
            (cross_norm_bias[None], whole((1, d))),
            (self_qkv, whole(self_qkv.shape)),
        ]
        + self_tables
        + [
            (self_bias, whole(self_bias.shape)),
            (self_gain, whole(self_gain.shape)),
            (cos, rows_h),
            (sin, rows_h),
            (ctx_ssq, lanes_8),
        ],
        [
            (sds((tl, d), BF16), rows_d),
            (sds((3 * rank, tl), BF16), block((3 * rank, tc), lambda b, m: (0, b))),
            (sds((tl, width), BF16), rows_w),
            (sds((tl, width), BF16), rows_w),
            (sds((tl, width), BF16), rows_w),
            (sds((tl, 2 * width), BF16), block((tc, 2 * width), lambda b, m: (b, 0))),
            (sds((8, tl), F32), lanes_8),
            (sds((16, d), F32), whole((16, d))),
        ],
        grid=(groups,),
        scratch=[pltpu.VMEM((3 * rank, 3 * width), BF16)],
        us=15,
    )
    kv_sib = send(kv, "seq", pair)
    *first_steps, last_step = powers(groups)
    for step in first_steps:
        ssq = ssq + send(ssq, "tensor", flip(groups, step))
    ssq, *by_group = seal(ssq, *by_group)
    (by_group,) = run_kernel(
        stack_kernel,
        meta,
        [(a, whole(a.shape)) for a in by_group],
        [(sds((groups - 1,) + slices.shape, BF16), whole((groups - 1,) + slices.shape))],
        us=2,
    )
    ssq, by_group = seal(ssq, by_group)
    along = [send(by_group, "dp", flip(share, 1)), send(by_group, "dp", flip(share, 2))] if share > 1 else []
    st_own = lax.rsqrt((ssq + send(ssq, "tensor", flip(groups, last_step))) / d + EPS)
    st_sib = send(st_own, "seq", pair)
    by_group_sib = send(by_group, "seq", pair)
    st_sib, by_group_sib = seal(st_sib, by_group_sib)
    ctx_low, _ = seal(ctx_low, st_own)
    ctx_pieces = [ctx_low, send(ctx_low, "tensor", shift(groups, 1))]

    all_8 = whole((8, tl))
    turned = lambda r, m: lax.rem(m[AT_T] + r, groups)
    parts = [(0, hc - 1), (hc - 1, 1)]
    mixed, lses, os_pieces = [], [], []
    for first, count in parts:
        kv_at = lambda lane: block((tl, HEAD_DIM), lambda h, r, m: (0, lane + h))
        own_rows = block((tc, HEAD_DIM), lambda h, r, m: (0, h))
        *blocks, out, lse = run_kernel(
            functools.partial(attention_kernel, groups),
            meta,
            [
                (raw_q, block((tc, HEAD_DIM), lambda h, r, m, first=first: (turned(r, m), first + h))),
                (st_own, block((8, tc), lambda h, r, m: (0, turned(r, m)))),
                (st_own, all_8),
                (st_sib, all_8),
                (kv, kv_at(first)),
                (kv_sib, kv_at(first)),
                (kv, kv_at(hc + first)),
                (kv_sib, kv_at(hc + first)),
            ],
            [(sds((tc, count * HEAD_DIM), BF16), own_rows)] * groups
            + [
                (sds((tl, count * HEAD_DIM), BF16), block((tc, HEAD_DIM), lambda h, r, m: (r, h))),
                (sds((8 * count, tl), F32), block((8, tc), lambda h, r, m: (h, r))),
            ],
            grid=(count, groups),
            scratch=[pltpu.VMEM((2 * tl, HEAD_DIM), BF16), pltpu.VMEM((HEAD_DIM, 2 * tl), BF16)],
            us=9.5 * count,
            after=[by_group] if first == 0 else [out],
        )
        mixed.append(out)
        lses.append(lse)
        if first:
            blocks[0], ctx_pieces[-1], *along = seal(blocks[0], ctx_pieces[-1], *along)
            ctx_pieces.append(send(ctx_pieces[-1], "tensor", shift(groups, 1)))
            blocks[1], *os_pieces = seal(blocks[1], *os_pieces)
        else:
            blocks[0], ctx_pieces[-1] = seal(blocks[0], ctx_pieces[-1])
            ctx_pieces.append(send(ctx_pieces[-1], "tensor", shift(groups, 1)))
        os_pieces += [send(a, "tensor", shift(groups, r)) if r else a for r, a in enumerate(blocks)]
    weight_parts = [by_group] + along
    if share > 1:
        middle = far_cut(by_group.shape[1])
        weight_parts += [
            send(along[1][:, :middle], "dp", flip(share, 1)),
            send(along[0][:, middle:], "dp", flip(share, 2)),
        ]
    near = seal(*os_pieces[-groups + 1 :], *weight_parts)
    os_pieces[-groups + 1 :], weight_parts = near[: groups - 1], near[groups - 1 :]
    weight_parts = weight_parts + [by_group_sib] + [send(p, "seq", pair) for p in weight_parts[1:]]
    ctx_sib = [send(p, "seq", pair) for p in ctx_pieces]

    vspec = whole(vec.shape)
    own_block = block((tc, d), lambda b, m: (m[AT_T], 0))
    weight_scratch = [
        pltpu.VMEM((groups, width, d), BF16),
        pltpu.VMEM((groups - 1, d, width), BF16),
        pltpu.VMEM((groups, width, d), BF16),
    ]
    sems = pltpu.SemaphoreType.DMA((len(plan) * groups + 2,))
    shared = [
        table(row_up),
        table(col_dn, 3),
        *[(p, whole(p.shape)) for p in ctx_pieces + ctx_sib],
        (st_own, all_8),
        (st_sib, all_8),
        (self_out, hbm),
        (cross_qkv, block((1, d, width), lambda b, m: (0, 0, 0))),
        (cross_out, hbm),
    ] + [(p, hbm) for p in weight_parts]
    whole_of = lambda shape, dtype: (sds(shape, dtype), whole(shape))
    y2, x2, x1, y3, qn, qc, oc, os_all, lse_c, lats = run_kernel(
        functools.partial(cross_kernel, groups, hc, plan),
        meta,
        [(p, whole(p.shape)) for p in os_pieces] + [(tok, own_block), (vec, vspec)] + shared,
        [
            whole_of((tc, d), BF16),
            whole_of((tc, d), F32),
            whole_of((tc, d), F32),
            whole_of((tc, d), BF16),
            whole_of((tc, d), BF16),
            whole_of((tc, d), F32),
            whole_of((tc, d), BF16),
            whole_of((tc, d), BF16),
            whole_of((16, tc), F32),
            whole_of((3 * rank, tc), BF16),
        ],
        scratch=weight_scratch + [sems],
        us=20,
    )

    tiles = [(a, min(768, ff - a)) for a in range(0, ff, 768)]
    w1t = ffn_in.T
    y2_pieces = ring_pieces(y2, "tensor")
    feed_bias = ffn_bias.astype(F32)[None]
    feed_out, dys, acc = None, [], None
    for r in range(groups):
        place = block((tc, d), lambda b, m, r=r: (lax.rem(m[AT_T] + groups - r, groups), 0))
        ins = [(y2_pieces[r], whole((tc, d))), (og, place), (vec, vspec), (feed_bias, whole(feed_bias.shape))]
        ins += feed_tables + [(w1t, hbm), (ffn_out, hbm)]
        if r == 0:
            ins += [(x2, whole((tc, d)))]
        else:
            ins += [(a, whole(a.shape)) for a in acc] + [(feed_out, hbm)]
        feed_out, dy, *acc = run_kernel(
            functools.partial(feed_kernel, tiles, r == 0),
            meta,
            ins,
            [(sds((tl, d), BF16), place), whole_of((tc, d), F32 if r == 0 else BF16)]
            + [whole_of((rank, n), F32) for n in (ff, d, d, ff)],
            scratch=[pltpu.VMEM((ff, d), BF16), pltpu.VMEM((ff, d), BF16), pltpu.SemaphoreType.DMA((2, len(tiles)))],
            us=18,
            aliases={15: 0} if r else None,
        )
        dys.append(dy)
    g_up1, g_dn1, g_up2, g_dn2 = acc

    dy_own, dy_in = ring_total(dys, "tensor")
    feed_out, dy_in = seal(feed_out, dy_in)
    line = Line(meta, tc) if groups == 4 else None
    if line:
        for r in range(groups):
            line.add(feed_out, r, "output", r)
        line.start()
    else:
        result = lax.psum(feed_out, "tensor")
    *dos, dx1, g_own, g_oth, g_rup, g_split, g_cqdn = run_kernel(
        functools.partial(cross_back_kernel, groups, hc, plan),
        meta,
        [(dy_own, whole((tc, d))), (dy_in, whole((tc, d))), (og, own_block)]
        + [(a, whole(a.shape)) for a in (x2, x1, y3, qn, qc, oc, os_all, lse_c, lats)]
        + [(vec, vspec)]
        + shared,
        [whole_of((tc, HEAD_DIM), BF16)] * groups
        + [whole_of((tc, width - HEAD_DIM), BF16)] * groups
        + [
            whole_of((tc, d), F32),
            whole_of((groups, ctx_len, width), BF16),
            whole_of((groups, ctx_len, width), BF16),
            whole_of((2 * rank, d), F32),
            whole_of((groups, 3 * rank, width), F32),
            whole_of((rank, d), F32),
        ],
        scratch=weight_scratch + [pltpu.VMEM((tc, d), F32), sems],
        us=26,
    )

    back_shift = lambda arrays: [send(a, "tensor", shift(groups, -r)) if r else a for r, a in enumerate(arrays)]
    moving = lambda: line.moving if line else []
    chains = Chains()
    dos[0], g_oth, g_cqdn, *arrived_line = seal(dos[0], g_oth, g_cqdn, *moving())
    dos_first = back_shift(dos[:groups])
    packed = jnp.concatenate([g_cqdn, g_dn1, g_rup[:rank], g_rup[rank:], g_up2, g_up1, g_dn2], axis=1)
    early_at = chains.add(adapter_steps(packed, 5 * d))
    g_oth = send(g_oth, "seq", pair)
    chains.step()
    g_oth, *dos_first = seal(g_oth, *dos_first)
    to_group = jnp.concatenate([g_own.astype(F32) + g_oth.astype(F32), g_split], axis=1)
    dos_rest = back_shift(dos[groups:])
    group_at = chains.add(ring_steps([to_group[r] for r in range(groups)], "tensor"))
    chains.step()

    back, dkv_in = [], []
    for h in range(hc):
        of, at = (0, h) if h < parts[1][0] else (1, h - parts[1][0])
        grads = dos_first if h == 0 else dos_rest
        lane = 0 if h == 0 else h - 1
        kv_at = lambda lane: block((tl, HEAD_DIM), lambda r, m: (0, lane))
        if h:
            if h == 1:
                tied = seal(*dos_rest, *chains.arrived(), back[-1][0], back[-1][2])
                dos_rest = tied[: len(dos_rest)]
                chains.put(tied[len(dos_rest) : -2])
                chains.step()
                if line:
                    line.advance(arrived_line)
            else:
                tied = seal(back[-1][0], back[-1][2])
            dkv_in.append(send(tied[-1], "seq", pair))
            grads = dos_rest
        back.append(
            run_kernel(
                functools.partial(attention_back_kernel, groups, h == 0),
                meta,
                [
                    (raw_q, block((tc, HEAD_DIM), lambda r, m, h=h: (turned(r, m), h))),
                    (st_own, block((8, tc), lambda r, m: (0, turned(r, m)))),
                    (st_own, all_8),
                    (st_sib, all_8),
                    (kv, kv_at(h)),
                    (kv_sib, kv_at(h)),
                    (kv, kv_at(hc + h)),
                    (kv_sib, kv_at(hc + h)),
                    (mixed[of], block((tc, HEAD_DIM), lambda r, m, at=at: (r, at))),
                    (lses[of], block((8, tc), lambda r, m, at=at: (at, r))),
                ]
                + [(g, block((tc, HEAD_DIM), lambda r, m, lane=lane: (0, lane))) for g in grads]
                + ([(a, all_8) for a in back[-1][3:]] if h else []),
                [
                    (sds((tl, HEAD_DIM), F32), block((tc, HEAD_DIM), lambda r, m: (turned(r, m), 0))),
                    whole_of((tl, 2 * HEAD_DIM), F32),
                    whole_of((tl, 2 * HEAD_DIM), BF16),
                    whole_of((8, tl), F32),
                    whole_of((8, tl), F32),
                ],
                grid=(groups,),
                scratch=[
                    pltpu.VMEM((2 * tl, HEAD_DIM), BF16),
                    pltpu.VMEM((HEAD_DIM, 2 * tl), BF16),
                    pltpu.VMEM((2 * tl, HEAD_DIM), BF16),
                    pltpu.VMEM((2 * tl, HEAD_DIM), F32),
                    pltpu.VMEM((2 * tl, HEAD_DIM), F32),
                    pltpu.VMEM((tc, HEAD_DIM), BF16),
                ],
                us=12.5,
                after=list(tied[-2:-1]) if h else [],
            )
        )
    dq, dkv, dkv_out = zip(*[b[:3] for b in back])
    stat, cross = back[-1][3:]
    last_dkv = dkv_out[-1]
    stat, cross, last_dkv, *tied = seal(stat, cross, last_dkv, *chains.arrived(), *moving())
    count = len(chains.arrived())
    chains.put(tied[:count])
    arrived_line = tied[count:]
    dkv_in.append(send(last_dkv, "seq", pair))
    stat = stat + send(cross, "seq", pair)
    chains.step([group_at])
    for step in powers(groups):
        (other,) = seal(send(stat, "tensor", flip(groups, step)))
        stat = stat + other
    st_back = st_own * st_own * st_own * stat / d
    st_back, *tied = seal(st_back, *chains.arrived())
    chains.put(tied)
    chains.step()
    if line:
        line.advance(arrived_line)

    q_parts, late = [], None
    calls = 2
    for call in range(calls):
        steps = groups // calls
        in_d = block((tc, d), lambda b, m, c=call * steps: (c + b, 0))
        in_w = block((tc, width), lambda b, m, c=call * steps: (c + b, 0))
        in_h = block((tc, HEAD_DIM), lambda b, m, c=call * steps: (c + b, 0))
        in_2h = block((tc, 2 * HEAD_DIM), lambda b, m, c=call * steps: (c + b, 0))
        in_8 = block((8, tc), lambda b, m, c=call * steps: (0, c + b))
        size = (rank, 3 * (d + width))
        part, late = run_kernel(
            functools.partial(qkv_back_kernel, hc, call),
            meta,
            [(a, in_h) for a in dq]
            + [(a, in_2h) for a in list(dkv) + dkv_in]
            + [
                (pre_q, in_w),
                (pre_k, in_w),
                (st_own, in_8),
                (st_back, in_8),
                (self_gain, whole(self_gain.shape)),
                (cos, in_h),
                (sin, in_h),
                (self_qkv, hbm),
            ]
            + self_tables
            + [
                (tok, in_d),
                (vec, vspec),
                (y1, in_d),
                (lat_t, block((3 * rank, tc), lambda b, m, c=call * steps: (0, c + b))),
                (dx1, whole((tc, d))),
            ]
            + ([(late, whole(size))] if call else []),
            [(sds((steps * tc, d), BF16), block((tc, d), lambda b, m: (b, 0))), whole_of(size, F32)],
            grid=(steps,),
            scratch=[
                pltpu.VMEM((3 * rank, 3 * width), BF16),
                pltpu.VMEM(self_qkv.shape, BF16),
                pltpu.SemaphoreType.DMA(()),
            ],
            us=14,
        )
        q_parts.append(part)
        if line:
            for r in range(steps):
                line.add(part, r, "input_grad", call * steps + r)
        late, *tied = seal(late, *chains.arrived(), *moving())
        count = len(chains.arrived())
        chains.put(tied[:count])
        chains.step()
        if call == 0:
            to_group = chains.result(group_at)
            g_ctx, split = to_group[:ctx_len], to_group[ctx_len:]
            ctx_gain = jnp.where(is_key, cross_gain[1:2].astype(F32), 1.0)
            ctx_stat = jnp.sum(g_ctx * ctx_gain * ctx_pre, axis=1)
            stat_at = chains.add(total_steps(ctx_stat, "tensor"))
            chains.advance(stat_at)
        if line:
            line.advance(tied[count:])
    while not chains.done(stat_at):
        chains.put(seal(*chains.arrived()))
        chains.step()
    ctx_stat = chains.result(stat_at)

    ctx_inverse = jnp.concatenate([st_own[2, j * tc : j * tc + ctx_len // groups] for j in range(groups)])
    ctx_cubed = ctx_inverse * ctx_inverse * ctx_inverse * ctx_stat / d
    d_key = ctx_inverse[:, None] * ctx_gain * g_ctx - ctx_pre * ctx_cubed[:, None]
    d_ctx = jnp.where(is_key, d_key, g_ctx).astype(BF16)
    ctx_part, g_ctx_up, g_ctx_dn = run_kernel(
        context_back_kernel,
        meta,
        [
            (context, whole(context.shape)),
            ctx_w,
            ctx_up,
            ctx_dn,
            (ctx_lat_t, whole(ctx_lat_t.shape)),
            (d_ctx, whole(d_ctx.shape)),
        ],
        [whole_of((ctx_len, d), F32), whole_of((rank, width), F32), whole_of((rank, d), F32)],
        us=6,
        after=[line.acc[max(line.acc)]] if line else [],
    )

    pick = lambda g: [jnp.where(is_key, g, 0.0), jnp.where(is_key, 0.0, g)]
    late = jnp.concatenate(
        [late[:, : 3 * d]]
        + pick(g_ctx_dn)
        + [late[:, 3 * d :], split[:rank]]
        + pick(g_ctx_up)
        + [split[rank : 2 * rank], split[2 * rank :]]
        + [jnp.broadcast_to(adapter_index[0].astype(F32) / seq, (rank, HEAD_DIM))],
        axis=1,
    )
    ctx_at = chains.add(context_grad_steps(ctx_part))
    late_at = chains.add(adapter_steps(late, 5 * d))
    chains.advance(ctx_at)
    chains.advance(late_at)
    while line and line.at < len(line.parts):
        tied = seal(*chains.arrived(), *moving())
        count = len(chains.arrived())
        chains.put(tied[:count])
        chains.step()
        line.advance(tied[count:])
    while line and line.live():
        line.advance(line.moving)
    while chains.live():
        chains.put(seal(*chains.arrived()))
        chains.step()
    early, late, context_grad = chains.result(early_at), chains.result(late_at), chains.result(ctx_at).astype(F32)
    if line:
        result, input_grad = line.outs["output"], line.outs["input_grad"]
    else:
        input_grad = lax.psum(jnp.concatenate(q_parts), "tensor")

    indices = jnp.round(late[:, 0, -1].astype(F32)).astype(jnp.int32)
    early, late = spread(early, indices, slots), spread(late[:, :, :-HEAD_DIM], indices, slots)
    cut = lambda grads, start, size, count: [
        grads[:, :, start + j * size : start + (j + 1) * size] for j in range(count)
    ]
    wide, feed = cut(early, 0, d, 5), cut(early, 5 * d, ff, 2)
    wide_late, narrow = cut(late, 0, d, 5), cut(late, 5 * d, width, 8)
    swap = lambda a: jnp.swapaxes(a, -1, -2)
    return (
        result[None],
        input_grad[None],
        context_grad,
        swap(jnp.stack(wide_late[:3] + wide[:1] + wide_late[3:], axis=1)),
        jnp.stack(narrow[:6], axis=1),
        swap(wide[1]),
        feed[0],
        swap(jnp.stack(narrow[6:], axis=1)),
        jnp.stack(wide[2:4], axis=1),
        swap(feed[1]),
        wide[4],
    )


def solution(mesh):
    placed = (
        P("dp", "seq", None),
        P(None, "dp", "seq"),
        P("dp", None, None),
        P(),
        P(),
        P("dp"),
        P(None, None, "tensor"),
        P(None, "tensor"),
        P(None, "tensor"),
        P("tensor", None),
        P(None, None, "tensor"),
        P(None, "tensor"),
        P(None, "tensor"),
        P("tensor", None),
        P(),
        P(),
        P(None, "tensor"),
        P("tensor"),
        P("tensor", None),
        P(),
        P(),
        P(None, None, None, "tensor"),
        P(),
        P(None, None, "tensor"),
        P(None, None, "tensor", None),
        P(),
        P(None, "tensor", None),
        P(),
        P("dp", "seq", None),
    )
    return jax.shard_map(
        per_device,
        mesh=mesh,
        in_specs=placed,
        out_specs=(
            P("dp", "seq", None),
            P("dp", "seq", None),
            P(),
            P(),
            P(None, None, None, "tensor"),
            P(),
            P(None, None, "tensor"),
            P(None, None, "tensor", None),
            P(),
            P(None, "tensor", None),
            P(),
        ),
        check_vma=False,
    )
```

```python
import functools
import math

import jax
import jax.numpy as jnp
import numpy as np
from jax import lax
from jax.experimental import pallas as pl
from jax.experimental.pallas import tpu as pltpu
from jax.sharding import PartitionSpec as P

F32 = jnp.float32
BF16 = jnp.bfloat16
HEAD_DIM = 128
EPS = 1e-06
LOG2E = 1.4426950408889634
SCALE = HEAD_DIM ** (-0.5)
VMEM_LIMIT = 58 * 1024 * 1024
GELU_C = math.sqrt(2.0 / math.pi)
M0, M1, M2, M3, M4, M5, B0, B1, B2, CG, CB = range(11)
AT_T, AT_S, ADAPTER, PART, SLOTS = range(5)


def nn(left, right):
    return jnp.dot(left, right, preferred_element_type=F32)


def nt(left, right):
    return lax.dot_general(left, right, (((1,), (1,)), ((), ())), preferred_element_type=F32)


def row_total(values):
    ones = jnp.ones((8, values.shape[1]), BF16)
    high = values.astype(BF16)
    return nt(ones, high) + nt(ones, (values - high.astype(F32)).astype(BF16))


def mean(values):
    return jnp.mean(values, axis=-1, keepdims=True)


def normalize(values):
    centered = values - mean(values)
    inverse = lax.rsqrt(mean(centered * centered) + EPS)
    return centered * inverse, inverse


def normalize_back(normed, inverse, upstream):
    return inverse * (upstream - mean(upstream) - normed * mean(upstream * normed))


def pair_swap(values):
    width = values.shape[1]
    lane = lax.broadcasted_iota(jnp.int32, values.shape, 1)
    return jnp.where(lane % 2 == 0, pltpu.roll(values, width - 1, 1), pltpu.roll(values, 1, 1))


def rope(values, cosine, sine):
    return values * cosine + pair_swap(values) * sine


def rope_back(values, cosine, sine):
    return values * cosine - pair_swap(values) * sine


def heads_of(array, count):
    return [array[:, h * HEAD_DIM : (h + 1) * HEAD_DIM] for h in range(count)]


def whole(shape):
    return pl.BlockSpec(shape, lambda *_: (0,) * len(shape))


def run_kernel(body, meta, ins, outs, grid=(1,), scratch=(), us=1.0, aliases=None, after=()):
    count = len(ins)
    ins = list(ins) + [(a, pl.BlockSpec(memory_space=pl.ANY)) for a in after]
    arrays = [a for a, _ in ins]
    moved = sum(math.prod(a.shape) * a.dtype.itemsize for a in arrays[:count]) + sum(
        math.prod(s.shape) * s.dtype.itemsize for s, _ in outs
    )

    def reading(meta_ref, *refs):
        return body(meta_ref, *refs[:count], *refs[len(arrays) :])

    return pl.pallas_call(
        reading,
        grid_spec=pltpu.PrefetchScalarGridSpec(
            num_scalar_prefetch=1,
            grid=grid,
            in_specs=[s for _, s in ins],
            out_specs=[s for _, s in outs],
            scratch_shapes=list(scratch),
        ),
        out_shape=[s for s, _ in outs],
        input_output_aliases=aliases or {},
        compiler_params=pltpu.CompilerParams(vmem_limit_bytes=VMEM_LIMIT),
        cost_estimate=pl.CostEstimate(
            flops=int(us * 1.15e9), bytes_accessed=int(min(moved, us * 2e6)), transcendentals=0
        ),
    )(meta, *arrays)


def sds(shape, dtype):
    return jax.ShapeDtypeStruct(shape, dtype)


def qkv_kernel(head_count, meta, tok, mod, emb, b_out, cg, cb, w, up, dn, bias, gain, cos, sin, ctx_ssq, *outs):
    y1, lat_t, pre_q, pre_k, raw_q, kv, ssq, vec, up_s = outs
    width = head_count * HEAD_DIM
    rank = up.shape[2]
    modes = mod[...] + emb[...]

    @pl.when(pl.program_id(0) == 0)
    def _():
        row = lax.broadcasted_iota(jnp.int32, modes.shape, 0)
        rows = [modes + jnp.where((row == 1) | (row == 4), 1.0, 0.0), b_out[...].astype(F32), cg[...], cb[...]]
        vec[...] = jnp.concatenate(rows + [jnp.zeros((5, modes.shape[1]), F32)], axis=0)
        up_s[...] = jnp.zeros_like(up_s)
        for j in range(3):
            up_s[j * rank : (j + 1) * rank, j * width : (j + 1) * width] = up[0, j]

    normed, _ = normalize(tok[...].astype(F32))
    y = (normed * (1.0 + modes[1:2, :]) + modes[0:1, :]).astype(BF16)
    y1[...] = y
    down = jnp.concatenate([dn[0, j] for j in range(3)], axis=0)
    lat = nt(y, down).astype(BF16)
    lat_t[...] = nt(down, y).astype(BF16)
    totals = []
    for j in range(3):
        lanes = slice(j * width, (j + 1) * width)
        u = nn(y, w[j]) + nn(lat, up_s[:, lanes]) + bias[j : j + 1, :].astype(F32)
        if j == 2:
            kv[:, width:] = u.astype(BF16)
            continue
        (pre_q, pre_k)[j][...] = u.astype(BF16)
        totals.append(row_total(u * u))
        scaled = u * gain[j : j + 1, :].astype(F32)
        for h in range(head_count):
            lanes = slice(h * HEAD_DIM, (h + 1) * HEAD_DIM)
            (raw_q, kv)[j][:, lanes] = rope(scaled[:, lanes], cos[...], sin[...]).astype(BF16)
    row = lax.broadcasted_iota(jnp.int32, totals[0].shape, 0)
    ssq[...] = jnp.where(row == 0, totals[0], jnp.where(row == 1, totals[1], ctx_ssq[...]))


def attention_kernel(groups, meta, raw_q, st, st_own, st_sib, k_own, k_sib, v_own, v_sib, *outs):
    blocks, (out, lse, kn, knt, vn, qn, vt) = outs[:groups], outs[groups:]
    count = k_own.shape[0]
    step = pl.program_id(1)

    @pl.when(step == 0)
    def _():
        for at, (k, s, v) in enumerate(((k_own, st_own, v_own), (k_sib, st_sib, v_sib))):
            rows = slice(at * count, (at + 1) * count)
            scaled = k[...].astype(F32) * s[...].T[:, 1:2]
            kn[rows, :] = scaled.astype(BF16)
            knt[:, rows] = scaled.T.astype(BF16)
            vn[rows, :] = v[...]
            vt[:, rows] = v[...].astype(F32).T.astype(BF16)

    q = (raw_q[...].astype(F32) * (st[...].T[:, 0:1] * (SCALE * LOG2E))).astype(BF16)
    qn[...] = q
    scores = nt(kn[...], q)
    highest = jnp.max(scores, axis=0, keepdims=True)
    e = jnp.exp2(scores - highest)
    total = jnp.sum(e, axis=0, keepdims=True)
    mixed = (nn(vt[...], e.astype(BF16)) / total).T.astype(BF16)
    out[...] = mixed
    for r in range(groups):

        @pl.when(step == r)
        def _(r=r):
            blocks[r][...] = mixed

    lse[...] = jnp.broadcast_to(highest + jnp.log2(total), lse.shape)


def attention_back_kernel(groups, first, meta, qn, st, st_own, st_sib, kn, knt, vn, out, lse, *rest):
    grads, rest = rest[:groups], rest[groups:]
    if not first:
        stat_in, cross_in = rest[:2]
        rest = rest[2:]
    dq, dkv_own, dkv_sib, stat, cross, dk_acc, dv_acc, g_s = rest
    count = kn.shape[0] // 2
    size = qn.shape[0]
    step = pl.program_id(0)

    @pl.when(step == 0)
    def _():
        dk_acc[...] = jnp.zeros_like(dk_acc)
        dv_acc[...] = jnp.zeros_like(dv_acc)
        stat[...] = jnp.zeros_like(stat) if first else stat_in[...]
        cross[...] = jnp.zeros_like(cross) if first else cross_in[...]

    for r in range(groups):

        @pl.when(step == r)
        def _(r=r):
            g_s[...] = grads[r][...]

    q = qn[...]
    g = g_s[...]
    delta = row_total(g.astype(F32) * out[...].astype(F32))[0:1, :]
    p = jnp.exp2(nt(kn[...], q) - lse[0:1, :])
    dv_acc[...] += nn(p.astype(BF16), g)
    ds = (p * (nt(vn[...], g) - delta)).astype(BF16)
    dk_acc[...] += nn(ds, q)
    dqs = nn(knt[...], ds).T * SCALE
    dq[...] = dqs
    lanes = pl.ds(pl.multiple_of(lax.rem(meta[AT_T] + step, groups) * size, size), size)
    total = row_total(dqs * q.astype(F32)) / (st[0:1, :] * (SCALE * LOG2E))
    stat[:, lanes] += jnp.where(lax.broadcasted_iota(jnp.int32, total.shape, 0) == 0, total, 0.0)

    @pl.when(step == pl.num_programs(0) - 1)
    def _():
        for at, (s, dkv, sums) in enumerate(((st_own, dkv_own, stat), (st_sib, dkv_sib, cross))):
            rows = slice(at * count, (at + 1) * count)
            dk = dk_acc[rows, :] * (1.0 / LOG2E)
            dkv[:, :HEAD_DIM] = dk.astype(dkv.dtype)
            dkv[:, HEAD_DIM:] = dv_acc[rows, :].astype(dkv.dtype)
            all_k = row_total(dk * kn[rows, :].astype(F32)) / s[1:2, :]
            sums[...] += jnp.where(lax.broadcasted_iota(jnp.int32, all_k.shape, 0) == 1, all_k, 0.0)


def qkv_back_kernel(head_count, call, meta, *refs):
    n = head_count
    dq, dkv, dkv_in = (refs[j * n : (j + 1) * n] for j in range(3))
    refs = refs[3 * n :]
    pre_q, pre_k, st, st_back, gain_in, cos, sin, w, up_in, dn_in, tok, vec, y1, lat_t, dx1 = refs[:15]
    packed_in = refs[15] if call else None
    part, packed, up, w_s, sem = refs[-5:]
    step = pl.program_id(0)
    fetch = pltpu.make_async_copy(w, w_s, sem)

    @pl.when(step == 0)
    def _():
        fetch.start()
        packed[...] = packed_in[...] if call else jnp.zeros_like(packed)

    inverse, cubed = st[...].T, st_back[...].T
    c, s = cos[...], sin[...]
    width = n * HEAD_DIM
    rank = up_in.shape[2]
    d = tok.shape[1]
    gain = gain_in[...].astype(F32)
    up[...] = jnp.zeros_like(up)
    for j in range(3):
        up[j * rank : (j + 1) * rank, j * width : (j + 1) * width] = up_in[0, j]
    dn = jnp.concatenate([dn_in[0, j] for j in range(3)], axis=0)
    dk = [a[:, :HEAD_DIM] + b[:, :HEAD_DIM].astype(F32) for a, b in zip(dkv, dkv_in)]
    dv = [a[:, HEAD_DIM:] + b[:, HEAD_DIM:].astype(F32) for a, b in zip(dkv, dkv_in)]
    grads = [
        jnp.concatenate([rope_back(ref[...], c, s) for ref in dq], axis=1),
        jnp.concatenate([rope_back(a, c, s) for a in dk], axis=1),
        jnp.concatenate(dv, axis=1).astype(BF16),
    ]
    for j, pre in enumerate((pre_q, pre_k)):
        grads[j] = (
            inverse[:, j : j + 1] * gain[j : j + 1, :] * grads[j] - pre[...].astype(F32) * cubed[:, j : j + 1]
        ).astype(BF16)
    joined = jnp.concatenate(grads, axis=1)
    d_lat = nt(joined, up[...]).astype(BF16)
    d_lat_t = nt(up[...], joined).astype(BF16)
    total = nn(d_lat, dn)

    @pl.when(step == 0)
    def _():
        fetch.wait()

    for j in range(3):
        total = total + nt(grads[j], w_s[j])
    normed, inverse = normalize(tok[...].astype(F32))
    back = normalize_back(normed, inverse, total * vec[M1 : M1 + 1, :])
    own = (meta[AT_T] == call * pl.num_programs(0) + step).astype(F32)
    part[...] = (back + dx1[...] * own).astype(part.dtype)
    g_dn = nn(d_lat_t, y1[...])
    for j in range(3):
        rows = slice(j * rank, (j + 1) * rank)
        g_up = nn(lat_t[rows, :], grads[j])
        for start, g in ((j * d, g_dn[rows, :]), (3 * d + j * width, g_up)):
            lanes = slice(start, start + g.shape[1])
            packed[:, lanes] += g


def context_kernel(groups, meta, ctx, w, up, dn, bias, gain, up_q, down_row, pre, low, ssq, lat_t):
    key = meta[AT_S] == 0
    c = ctx[...]
    count = c.shape[0]
    rank, width = up.shape[2:]
    lat = nt(c, dn[0, 0]).astype(BF16)
    lat_t[...] = nt(dn[0, 0], c).astype(BF16)
    b, g = bias[...].astype(F32), gain[...].astype(F32)
    u = nn(c, w[0]) + nn(lat, up[0, 0]) + jnp.where(key, b[1:2, :], b[2:3, :])
    pre[...] = u
    low[:count, :] = (u * jnp.where(key, g[1:2, :], 1.0)).astype(BF16)
    low[count : count + rank, :] = up_q[0, 0]
    low[count + rank : count + 2 * rank, :] = down_row[0, 0]
    low[count + 2 * rank : count + 3 * rank, :] = down_row[0, 1]
    row = lax.broadcasted_iota(jnp.int32, (rank, width), 0)
    low[count + 3 * rank :, :] = jnp.where(row == 0, b[0:1, :], jnp.where(row == 1, g[0:1, :], 0.0)).astype(BF16)
    total = row_total(u * u)
    share, block = count // groups, ssq.shape[1] // groups
    ssq[...] = jnp.zeros_like(ssq)
    for j in range(groups):
        ssq[:, j * block : j * block + share] = total[:, j * share : (j + 1) * share]


def context_row(groups, count, rows):
    share, block = count // groups, rows.shape[1] // groups
    return jnp.concatenate([rows[2:3, j * block : j * block + share] for j in range(groups)], axis=1)


def context_back_kernel(meta, ctx, w, up_in, dn_in, lat_t, grad, out, g_up, g_dn):
    g = grad[...]
    up, dn = up_in[0, 0], dn_in[0, 0]
    d_lat = nt(g, up).astype(BF16)
    d_lat_t = nt(up, g).astype(BF16)
    out[...] = nt(g, w[0]) + nn(d_lat, dn)
    g_up[...] = nn(lat_t[...], g)
    g_dn[...] = nn(d_lat_t, ctx[...])


def pack_kernel(meta, wo, wq, wc, out):
    rows, width = wo.shape[0], wq.shape[2]
    out[:rows, :] = wo[...]
    for j in range(out.shape[1] // width):
        out[rows : 2 * rows, j * width : (j + 1) * width] = wq[0, j * rows : (j + 1) * rows, :]
    out[2 * rows :, :] = wc[...]


def stack_kernel(meta, *refs):
    for j, ref in enumerate(refs[:-1]):
        refs[-1][j] = ref[...]


def start_copies(meta, plan, refs, targets, sems, own):
    copies = [[] for _ in targets]
    at = 0
    for source, weight, first, rows, slot, inner, size in plan:
        target = targets[weight]
        width = target.shape[2]
        sides = refs[source].shape[2] // width
        for j in range(sides):
            start = pl.multiple_of(meta[slot] * (size * sides) + (j * size + inner), 16)
            copies[weight].append(
                pltpu.make_async_copy(
                    refs[source].at[:, pl.ds(first, rows), pl.ds(j * width, width)],
                    target.at[pl.ds(target.shape[0] - refs[source].shape[0], refs[source].shape[0]), pl.ds(start, rows), :],
                    sems.at[at],
                )
            )
            at += 1
    for weight, shard in own.items():
        copies[weight].append(pltpu.make_async_copy(shard, targets[weight].at[0], sems.at[at]))
        at += 1
    for weight in copies:
        for copy in weight:
            copy.start()
    return copies


def finish(copies):
    for copy in copies:
        copy.wait()


def cross_kernel(groups, head_count, plan, meta, *refs):
    n = groups * head_count
    os_in, refs = refs[:groups], refs[groups:]
    tok, vec, up, dn3 = refs[:4]
    ctx_own, ctx_sib, refs = refs[4 : 4 + groups], refs[4 + groups : 4 + 2 * groups], refs[4 + 2 * groups :]
    st_own, st_sib, wo_own, wq_own, wc_own = refs[:5]
    k = 1 + max(entry[0] for entry in plan)
    sources, refs = refs[5 : 5 + k], refs[5 + k :]
    y2, x2, x1, y3, qn, qc, oc, os_all, lse, lats = refs[:10]
    wo, wq, wc, sems = refs[10:]
    copies = start_copies(meta, plan, sources, (wo, wq, wc), sems, {0: wo_own, 2: wc_own})
    full = lambda weight: weight[...].reshape(weight.shape[0] * weight.shape[1], weight.shape[2])
    dn3 = dn3[0, 0]
    rank = dn3.shape[0]
    ctx_len = ctx_own[0].shape[0] - 4 * rank
    small = jnp.concatenate([ctx_own[r][ctx_len:, :] for r in range(groups)], axis=1)
    first = meta[AT_S] == 0
    key_row = context_row(groups, ctx_len, jnp.where(first, st_own[...], st_sib[...]))
    ctx_inverse = jnp.broadcast_to(key_row, (8, ctx_len)).T[:, 0:1]
    width = head_count * HEAD_DIM
    for r in range(groups):
        os_all[:, r * width : (r + 1) * width] = os_in[r][...]
    os_v = os_all[...]
    down0, down1 = small[rank : 2 * rank, :], small[2 * rank : 3 * rank, :]
    lat = nt(os_v, down0).astype(BF16)
    lats[0:rank, :] = nt(down0, os_v).astype(BF16)
    total = nn(lat, up[0, 0])
    finish(copies[0])
    total = total + nn(os_v, full(wo))
    x1_v = tok[...].astype(F32) + (total + vec[B0 : B0 + 1, :]) * vec[M2 : M2 + 1, :]
    x1[...] = x1_v
    normed, _ = normalize(x1_v)
    y3_v = (normed * vec[CG : CG + 1, :] + vec[CB : CB + 1, :]).astype(BF16)
    y3[...] = y3_v
    lat = nt(y3_v, dn3).astype(BF16)
    lats[2 * rank : 3 * rank, :] = nt(dn3, y3_v).astype(BF16)
    finish(copies[1])
    q = nn(lat, small[0:rank, :]) + small[3 * rank : 3 * rank + 1, :].astype(F32)
    q = q + jnp.concatenate([nn(y3_v, wq[r - 1] if r else wq_own[0]) for r in range(groups)], axis=1)
    qc[...] = q
    inverse = lax.rsqrt(mean(q * q) + EPS)
    gain = small[3 * rank + 1 : 3 * rank + 2, :].astype(F32)
    qn[...] = (q * (inverse * (SCALE * LOG2E)) * gain).astype(BF16)
    for j in range(n):
        r, lanes = j // head_count, slice((j % head_count) * HEAD_DIM, (j % head_count + 1) * HEAD_DIM)
        a, b = ctx_own[r][:ctx_len, lanes], ctx_sib[r][:ctx_len, lanes]
        keys, values = jnp.where(first, a, b), jnp.where(first, b, a)
        keys = (keys.astype(F32) * ctx_inverse).astype(BF16)
        scores = nt(keys, qn[:, j * HEAD_DIM : (j + 1) * HEAD_DIM])
        highest = jnp.max(scores, axis=0, keepdims=True)
        e = jnp.exp2(scores - highest)
        sums = jnp.sum(e, axis=0, keepdims=True)
        mixed = nn(values.astype(F32).T.astype(BF16), e.astype(BF16)) / sums
        oc[:, j * HEAD_DIM : (j + 1) * HEAD_DIM] = mixed.T.astype(BF16)
        lse[j : j + 1, :] = highest + jnp.log2(sums)
    oc_v = oc[...]
    lat = nt(oc_v, down1).astype(BF16)
    lats[rank : 2 * rank, :] = nt(down1, oc_v).astype(BF16)
    total = nn(lat, up[0, 1])
    finish(copies[2])
    total = total + nn(oc_v, full(wc))
    x2_v = x1_v + total + vec[B1 : B1 + 1, :]
    x2[...] = x2_v
    normed, _ = normalize(x2_v)
    y2[...] = (normed * vec[M4 : M4 + 1, :] + vec[M3 : M3 + 1, :]).astype(BF16)


def cross_back_kernel(groups, head_count, plan, meta, *refs):
    n = groups * head_count
    dy_own, dy_in, og, x2, x1, y3, qn, qc, oc, os_all, lse, lats, vec, up, dn3 = refs[:15]
    ctx_own, ctx_sib, refs = refs[15 : 15 + groups], refs[15 + groups : 15 + 2 * groups], refs[15 + 2 * groups :]
    st_own, st_sib, wo_own, wq_own, wc_own = refs[:5]
    k = 1 + max(entry[0] for entry in plan)
    sources, refs = refs[5 : 5 + k], refs[5 + k :]
    dos_first, dos_rest, refs = refs[:groups], refs[groups : 2 * groups], refs[2 * groups :]
    dx1, g_own, g_oth, g_up, g_split, g_dn, wo, wq, wc, dq_s, sems = refs
    copies = start_copies(meta, plan, sources, (wo, wq, wc), sems, {0: wo_own, 2: wc_own})
    full = lambda weight: weight[...].reshape(weight.shape[0] * weight.shape[1], weight.shape[2])
    dn3 = dn3[0, 0]
    rank = dn3.shape[0]
    ctx_len = ctx_own[0].shape[0] - 4 * rank
    small = jnp.concatenate([ctx_own[r][ctx_len:, :] for r in range(groups)], axis=1)
    first = meta[AT_S] == 0
    key_row = context_row(groups, ctx_len, jnp.where(first, st_own[...], st_sib[...]))
    ctx_inverse = jnp.broadcast_to(key_row, (8, ctx_len)).T[:, 0:1]
    width = head_count * HEAD_DIM
    down0, down1 = small[rank : 2 * rank, :], small[2 * rank : 3 * rank, :]
    normed, inverse = normalize(x2[...])
    dn = (dy_own[...] + dy_in[...].astype(F32)) * vec[M4 : M4 + 1, :]
    dx2 = og[...].astype(F32) + normalize_back(normed, inverse, dn)
    grad = dx2.astype(BF16)
    d_lat = nt(grad, up[0, 1]).astype(BF16)
    d_lat_t = nt(up[0, 1], grad).astype(BF16)
    oc_v = oc[...]
    g_up[rank : 2 * rank, :] = nn(lats[rank : 2 * rank, :], grad)
    split = nn(d_lat_t, oc_v)
    for r in range(groups):
        g_split[r, 2 * rank : 3 * rank, :] = split[:, r * width : (r + 1) * width]
    finish(copies[2])
    d_oc = nn(d_lat, down1) + nt(grad, full(wc))
    d_oc = d_oc.astype(BF16)
    for j in range(n):
        r, lanes = j // head_count, slice((j % head_count) * HEAD_DIM, (j % head_count + 1) * HEAD_DIM)
        head = slice(j * HEAD_DIM, (j + 1) * HEAD_DIM)
        a, b = ctx_own[r][:ctx_len, lanes], ctx_sib[r][:ctx_len, lanes]
        keys, values = jnp.where(first, a, b), jnp.where(first, b, a)
        keys = (keys.astype(F32) * ctx_inverse).astype(BF16)
        q, g = qn[:, head], d_oc[:, head]
        delta = row_total(g.astype(F32) * oc_v[:, head].astype(F32))[0:1, :]
        p = jnp.exp2(nt(keys, q) - lse[j : j + 1, :])
        dv = nn(p.astype(BF16), g)
        ds = (p * (nt(values, g) - delta)).astype(BF16)
        dk = nn(ds, q) * (1.0 / LOG2E)
        dq_s[:, head] = nn(keys.astype(F32).T.astype(BF16), ds).T * SCALE
        g_own[r, :, lanes] = jnp.where(first, dk, dv).astype(BF16)
        g_oth[r, :, lanes] = jnp.where(first, dv, dk).astype(BF16)
    q = qc[...]
    inverse = lax.rsqrt(mean(q * q) + EPS)
    gain = small[3 * rank + 1 : 3 * rank + 2, :].astype(F32)
    scaled = dq_s[...] * gain
    stat = mean(scaled * q)
    dqc = (inverse * scaled - q * (inverse * inverse * inverse * stat)).astype(BF16)
    up_q = small[0:rank, :]
    d_lat = nt(dqc, up_q).astype(BF16)
    d_lat_t = nt(up_q, dqc).astype(BF16)
    split = nn(lats[2 * rank : 3 * rank, :], dqc)
    for r in range(groups):
        g_split[r, 0:rank, :] = split[:, r * width : (r + 1) * width]
    g_dn[...] = nn(d_lat_t, y3[...])
    dy3 = nn(d_lat, dn3)
    finish(copies[1])
    for r in range(groups):
        part = dqc[:, r * width : (r + 1) * width]
        dy3 = dy3 + nt(part, wq[r - 1] if r else wq_own[0])
    normed, inverse = normalize(x1[...])
    dx1_v = dx2 + normalize_back(normed, inverse, dy3 * vec[CG : CG + 1, :])
    dx1[...] = dx1_v
    grad = (dx1_v * vec[M2 : M2 + 1, :]).astype(BF16)
    d_lat = nt(grad, up[0, 0]).astype(BF16)
    d_lat_t = nt(up[0, 0], grad).astype(BF16)
    g_up[0:rank, :] = nn(lats[0:rank, :], grad)
    split = nn(d_lat_t, os_all[...])
    for r in range(groups):
        g_split[r, rank : 2 * rank, :] = split[:, r * width : (r + 1) * width]
    finish(copies[0])
    d_os = nn(d_lat, down0) + nt(grad, full(wo))
    for r in range(groups):
        block = d_os[:, r * width : (r + 1) * width]
        dos_first[r][...] = block[:, :HEAD_DIM].astype(BF16)
        dos_rest[r][...] = block[:, HEAD_DIM:].astype(BF16)


def feed_kernel(tiles, first, meta, *refs):
    y2, og, vec, bias, dn1, up1, dn2, up2, w1_h, w2_h = refs[:10]
    if first:
        x2 = refs[10]
    else:
        acc = refs[10:14]
    refs = refs[11:] if first else refs[15:]
    dn1, up1, dn2, up2 = dn1.at[0], up1.at[0], dn2.at[0], up2.at[0]
    out, dy, g_up1, g_dn1, g_up2, g_dn2, w1, w2, sems = refs
    copies = []
    for at, (start, size) in enumerate(tiles):
        rows = pl.ds(start, size)
        pair = [
            pltpu.make_async_copy(h.at[rows, :], v.at[rows, :], sems.at[j, at])
            for j, (h, v) in enumerate(((w1_h, w1), (w2_h, w2)))
        ]
        for copy in pair:
            copy.start()
        copies.append(pair)
    y = y2[...]
    dff = (og[...].astype(F32) * vec[M5 : M5 + 1, :]).astype(BF16)
    lat = nt(y, dn1[...]).astype(BF16)
    lat_t = nt(dn1[...], y).astype(BF16)
    drl = nt(dff, up2[...]).astype(BF16)
    drl_t = nt(up2[...], dff).astype(BF16)
    part = grad = rl = rl_t = d_lat = d_lat_t = 0.0
    for (start, size), pair in zip(tiles, copies):
        cols = slice(start, start + size)
        finish(pair)
        h = nt(y, w1[cols, :]) + nn(lat, up1[:, cols]) + bias[:, cols]
        du = nt(dff, w2[cols, :]) + nn(drl, dn2[:, cols])
        sq = h * h
        t = jnp.tanh(GELU_C * h * (1.0 + 0.044715 * sq))
        act = (0.5 * h * (1.0 + t)).astype(BF16)
        slope = 0.5 * (1.0 + t) + (0.5 * GELU_C) * h * (1.0 - t * t) * (1.0 + (3.0 * 0.044715) * sq)
        dh = (du * slope).astype(BF16)
        part = part + nn(act, w2[cols, :])
        grad = grad + nn(dh, w1[cols, :])
        rl = rl + nt(act, dn2[:, cols])
        rl_t = rl_t + nt(dn2[:, cols], act)
        d_lat = d_lat + nt(dh, up1[:, cols])
        d_lat_t = d_lat_t + nt(up1[:, cols], dh)
        new_up1, new_dn2 = nn(lat_t, dh), nn(drl_t, act)
        g_up1[:, cols] = new_up1 if first else new_up1 + acc[0][:, cols]
        g_dn2[:, cols] = new_dn2 if first else new_dn2 + acc[3][:, cols]
    part = part + nn(rl.astype(BF16), up2[...])
    grad = grad + nn(d_lat.astype(BF16), dn1[...])
    new_dn1, new_up2 = nn(d_lat_t.astype(BF16), y), nn(rl_t.astype(BF16), dff)
    g_dn1[...] = new_dn1 if first else new_dn1 + acc[1][...]
    g_up2[...] = new_up2 if first else new_up2 + acc[2][...]
    part = part * vec[M5 : M5 + 1, :]
    if first:
        part = part + x2[...] + vec[B2 : B2 + 1, :] * vec[M5 : M5 + 1, :]
    out[...] = part.astype(out.dtype)
    dy[...] = grad.astype(dy.dtype)


def shift(count, step):
    return [(a, (a + step) % count) for a in range(count)]


def flip(count, step):
    return [(a, a ^ step) for a in range(count)]


def powers(count):
    return [1 << j for j in range(count.bit_length() - 1)]


def send(values, axis, pairs):
    return jax.tree.map(lambda v: lax.ppermute(v, axis, pairs), values)


def ring_pieces(own, axis):
    count = lax.axis_size(axis)
    pieces = [own]
    for _ in range(count - 1):
        pieces.append(send(pieces[-1], axis, shift(count, 1)))
    return pieces


def ring_total(parts, axis):
    count = lax.axis_size(axis)
    moving = parts[1]
    for r in range(2, count):
        moving = send(moving, axis, shift(count, 1))
        moving = (moving.astype(F32) + parts[r].astype(F32)).astype(BF16)
    return parts[0], send(moving, axis, shift(count, 1))


def gather_direct(own, axis):
    count = lax.axis_size(axis)
    return [own] + [send(own, axis, shift(count, r)) for r in range(1, count)]


def scatter_direct(parts, axis):
    count = lax.axis_size(axis)
    return parts[0].astype(F32) + sum(
        send(parts[r].astype(BF16), axis, shift(count, -r)).astype(F32) for r in range(1, count)
    )


def gather_flipped(own, axis):
    count = lax.axis_size(axis)
    return [own] + [send(own, axis, flip(count, j)) for j in range(1, count)]


def total_flipped(own, axis):
    terms = [v.astype(F32) for v in gather_flipped(own, axis)]
    while len(terms) > 1:
        terms = [terms[j] + terms[j + 1] for j in range(0, len(terms), 2)]
    return terms[0]


def halves(values, axis):
    half = values.shape[0] // 2
    low, high = values[:half], values[half:]
    upper = lax.axis_index(axis) == 1
    return jnp.where(upper, high, low), jnp.where(upper, low, high)


def pair_scatter(values):
    kept, sent = halves(values, "seq")
    return kept + send(sent.astype(BF16), "seq", flip(2, 1)).astype(F32)


def pair_gather(values, dim):
    other = send(values, "seq", flip(2, 1))
    upper = lax.axis_index("seq") == 1
    return jnp.concatenate([jnp.where(upper, other, values), jnp.where(upper, values, other)], axis=dim)


def place_blocks(blocks, axis):
    size = blocks[0].shape[0]
    out = jnp.zeros((size * len(blocks),) + blocks[0].shape[1:], blocks[0].dtype)
    index = lax.axis_index(axis)
    for j, block in enumerate(blocks):
        out = lax.dynamic_update_slice_in_dim(out, block, (index ^ j) * size, 0)
    return out


def total_twice(values, axis):
    for step in powers(lax.axis_size(axis)):
        values = values + send(values, axis, flip(lax.axis_size(axis), step))
    return values


class Chains:
    def __init__(self):
        self.chains, self.values, self.results = [], [], {}

    def add(self, chain):
        self.chains.append(chain)
        self.values.append(None)
        return len(self.chains) - 1

    def start(self, at):
        self.advance(at)

    def advance(self, at):
        try:
            self.values[at] = self.chains[at].send(self.values[at])
        except StopIteration as end:
            self.results[at] = end.value

    def step(self, skip=()):
        for at in range(len(self.chains)):
            if at not in self.results and at not in skip:
                self.advance(at)

    def live(self):
        return len(self.results) < len(self.chains)

    def done(self, at):
        return at in self.results

    def result(self, at):
        return self.results[at]

    def arrived(self):
        live = [self.values[at] for at in range(len(self.chains)) if at not in self.results]
        return jax.tree.leaves(live)

    def put(self, leaves):
        places = [at for at in range(len(self.chains)) if at not in self.results]
        structure = jax.tree.structure([self.values[at] for at in places])
        for at, value in zip(places, jax.tree.unflatten(structure, leaves)):
            self.values[at] = value


def seal(*values):
    return list(lax.optimization_barrier(values)) if values else []


def ring_steps(parts, axis):
    count = lax.axis_size(axis)
    moving = parts[1].astype(BF16)
    for r in range(2, count + 1):
        moving = yield send(moving, axis, shift(count, 1))
        if r < count:
            moving = (moving.astype(F32) + parts[r].astype(F32)).astype(BF16)
    return parts[0].astype(F32) + moving.astype(F32)


def line_kernel(shape, meta, *refs):
    inward, across, outward, both = shape
    inner = (meta[AT_T] == 1) | (meta[AT_T] == 2)
    count = (inward or outward) + inward + 2 * across + outward + both
    ins, outs = list(refs[:count]), list(refs[count:])
    add = lambda a, b: (a[...].astype(F32) + b[...].astype(F32)).astype(BF16)
    if inward or outward:
        first = ins.pop(0)
    if inward:
        outs.pop(0)[...] = add(ins.pop(0), first)
    if across:
        total = add(ins.pop(0), ins.pop(0))
        outs.pop(0)[...] = jnp.where(inner, total, ins.pop(0)[...]) if both else total
    if outward:
        outs.pop(0)[...] = jnp.where(inner, ins.pop(0)[...], first[...])


class Line:
    def __init__(self, meta, size):
        self.meta, self.size = meta, size
        self.parts, self.targets, self.outs = [], [], {}
        self.acc, self.total, self.at, self.moving = {}, {}, 0, []

    def add(self, array, block, target, out_block):
        self.parts.append((array, block))
        self.targets.append((target, out_block))

    def start(self):
        array, block = self.parts[self.at] if self.at < len(self.parts) else (None, None)
        inward, outward = array is not None, self.at - 2 in self.total
        pairs = [(0, 1), (3, 2)] * inward + [(1, 0), (2, 3)] * outward
        if inward and outward:
            mine = self.total[self.at - 2]
        elif inward:
            mine = array[block * self.size : (block + 1) * self.size]
        else:
            mine = self.total.get(self.at - 2)
        self.moving = [send(mine, "tensor", pairs)] if pairs else []
        across = self.at - 1 in self.acc
        if across:
            self.moving.append(send(self.acc[self.at - 1], "tensor", [(1, 2), (2, 1)]))
        self.shape = (inward, across, outward)

    def advance(self, moving):
        inward, across, outward = self.shape
        moving, at = list(moving), self.at
        first = moving.pop(0) if inward or outward else None
        second = moving.pop(0) if across else None
        both = across and at + 1 < len(self.parts)
        grid = 4
        rows = lambda block: pl.BlockSpec((self.size // grid, width), lambda b, m: (block * grid + b, 0))
        width = (second if first is None else first).shape[1]
        kind = sds((self.size, width), BF16)
        ins, outs, aliases = [], [], None
        if first is not None:
            ins.append((first, rows(0)))
        if inward:
            array, block = self.parts[at]
            ins.append((array, rows(block)))
            outs.append((kind, rows(0)))
        if across:
            ins += [(self.acc[at - 1], rows(0)), (second, rows(0))]
            outs.append((kind, rows(0)))
        if both:
            array, block = self.parts[at + 1]
            ins.append((array, rows(block)))
        if outward:
            ins.append((self.total[at - 2], rows(0)))
        count = len(ins)
        if outward:
            target, block = self.targets[at - 2]
            length = self.size * sum(t == target for t, _ in self.targets)
            outs.append((sds((length, width), BF16), rows(block)))
            if target in self.outs:
                ins.append((self.outs[target], pl.BlockSpec(memory_space=pl.ANY)))
                aliases = {count + 1: len(outs) - 1}

        def body(meta, *refs):
            line_kernel((inward, across, outward, both), meta, *refs[:count], *refs[len(ins) :])

        results = list(run_kernel(body, self.meta, ins, outs, grid=(grid,), us=3, aliases=aliases))
        if inward:
            self.acc[at] = results.pop(0)
        if across:
            self.total[at - 1] = results.pop(0)
        if outward:
            self.outs[self.targets[at - 2][0]] = results.pop(0)
        self.at, self.moving = at + 1, []
        if self.live():
            self.start()

    def live(self):
        return self.at < len(self.parts) + 2


def total_steps(value, axis):
    for step in powers(lax.axis_size(axis)):
        value = value + (yield send(value, axis, flip(lax.axis_size(axis), step)))
    return value


def adapter_steps(value, shared):
    groups, dp = lax.axis_size("tensor"), lax.axis_size("dp")
    pair, upper = flip(2, 1), lax.axis_index("seq") == 1
    kept, sent = halves(value, "seq")
    other = yield send(sent.astype(BF16), "seq", pair)
    value = kept + other.astype(F32)
    own, rest = value[:, :shared].astype(BF16), value[:, shared:].astype(BF16)
    for step in powers(groups):
        other = yield send(own, "tensor", flip(groups, step))
        own = (own.astype(F32) + other.astype(F32)).astype(BF16)
    value = jnp.concatenate([own, rest], axis=1)[None]
    for step in powers(dp):
        other = yield send(value, "dp", flip(dp, step))
        value = jnp.concatenate([value, other])
    other = yield send(value, "seq", pair)
    return jnp.concatenate([jnp.where(upper, other, value), jnp.where(upper, value, other)], axis=1)


def context_grad_steps(value):
    groups, dp = lax.axis_size("tensor"), lax.axis_size("dp")
    at_dp = lax.axis_index("dp")
    pair, second = flip(2, 1), lax.axis_index("seq") == 1
    kept, sent = halves(value, "seq")
    other = yield send(sent.astype(BF16), "seq", pair)
    value = kept + other.astype(F32)
    rows = value.shape[0] // dp
    parts = [lax.dynamic_slice_in_dim(value, (at_dp ^ j) * rows, rows, 0) for j in range(dp)]
    others = yield tuple(send(parts[j].astype(BF16), "dp", flip(dp, j)) for j in range(1, dp))
    value = (parts[0] + sum(other.astype(F32) for other in others)).astype(BF16)
    for step in powers(groups):
        other = yield send(value, "tensor", flip(groups, step))
        value = (value.astype(F32) + other.astype(F32)).astype(BF16)
    for step in powers(dp):
        other = yield send(value, "dp", flip(dp, step))
        upper = (at_dp & step) != 0
        value = jnp.concatenate([jnp.where(upper, other, value), jnp.where(upper, value, other)])
    other = yield send(value, "seq", pair)
    return jnp.concatenate([jnp.where(second, other, value), jnp.where(second, value, other)])


def weight_share():
    return 4 if lax.axis_size("dp") == 4 else 1


def weight_plan(rows, count):
    share, seq = weight_share(), lax.axis_size("seq")
    d, s = lax.axis_index("dp"), lax.axis_index("seq")
    slots = [(s ^ a) * share + ((d ^ b) if share > 1 else 0) for a in range(seq) for b in range(share)]
    total = rows * count
    cut = far_cut(total)
    half = [(0, 0, total, 0)]
    if share > 1:
        half += [(1, 0, total, 1), (2, 0, total, 2), (3, 0, cut, 3), (4, cut, total - cut, 3)]
    spans = half + [(len(half) + a, b, c, share + e) for a, b, c, e in half]
    plan = []
    for source, start, size, slot in spans:
        for weight in range(count):
            low, high = max(start, weight * rows), min(start + size, (weight + 1) * rows)
            if low < high:
                plan.append((source, weight, low - start, high - low, SLOTS + slot, low - weight * rows, rows))
    return plan, slots


def far_cut(total):
    return (total // 2 + 15) // 16 * 16


def rope_tables(grid_pos):
    sixth = HEAD_DIM // 6
    counts = [(HEAD_DIM - 4 * sixth) // 2, sixth, sixth]
    table = np.zeros((3, HEAD_DIM), np.float32)
    lane = 0
    for component, count in enumerate(counts):
        for pair in range(count):
            table[component, lane : lane + 2] = 10000.0 ** (-pair / count)
            lane += 2
    positions = grid_pos.astype(F32)
    angles = sum(positions[c][:, None] * table[c][None, :] for c in range(3))
    sign = np.where(np.arange(HEAD_DIM) % 2 == 0, -1.0, 1.0).astype(np.float32)
    return jnp.cos(angles), jnp.sin(angles) * sign[None, :]


def select_slot(table, index):
    return lax.dynamic_index_in_dim(table, index, 0, keepdims=False)


def spread(gradients, indices, slot_count):
    hits = (jnp.arange(slot_count)[:, None] == indices[None, :]).astype(F32)
    out = 0.0
    for latent in range(gradients.shape[0]):
        shape = (slot_count,) + (1,) * (gradients.ndim - 1)
        out = out + hits[:, latent].reshape(shape) * gradients[latent].astype(F32)[None]
    return out


def eight_rows(rows):
    return jnp.concatenate([jnp.stack(rows), jnp.zeros((8 - len(rows), rows[0].shape[0]), F32)])


def per_device(
    tokens,
    positions,
    time_emb,
    modulation,
    context,
    adapter_index,
    self_qkv,
    self_bias,
    self_gain,
    self_out,
    cross_qkv,
    cross_bias,
    cross_gain,
    cross_out,
    cross_norm_gain,
    cross_norm_bias,
    ffn_in,
    ffn_bias,
    ffn_out,
    out_bias,
    col_down,
    col_up,
    ffn1_down,
    ffn1_up,
    row_down,
    row_up,
    ffn2_down,
    ffn2_up,
    out_grad,
):
    groups = lax.axis_size("tensor")
    seq = lax.axis_size("seq")
    i, s = lax.axis_index("tensor"), lax.axis_index("seq")
    tl, d = tokens.shape[1:]
    tc = tl // groups
    ctx_len = context.shape[0]
    width = self_qkv.shape[2]
    hc = width // HEAD_DIM
    ff = ffn_in.shape[1]
    slots, rank = col_down.shape[0], col_down.shape[3]
    share = weight_share()
    slice_rows = width // (share * seq)
    plan, slot_list = weight_plan(slice_rows, 3)
    part_at = s * share + (lax.axis_index("dp") if share > 1 else 0)
    meta = jnp.stack([jnp.asarray(v, jnp.int32) for v in [i, s, adapter_index[0], part_at] + slot_list])
    tok, og = tokens[0], out_grad[0]
    block = pl.BlockSpec
    hbm = pl.BlockSpec(memory_space=pl.ANY)
    pair = flip(seq, 1)

    def table(array, *place, rows=1):
        if not place:
            return (array, block((1,) + array.shape[1:], lambda *a: (a[-1][ADAPTER],) + (0,) * (array.ndim - 1)))
        return (
            array,
            block(
                (1, rows) + array.shape[2:],
                lambda *a: (a[-1][ADAPTER], place[0](a[-1]) if callable(place[0]) else place[0], 0, 0),
            ),
        )

    col_dn, row_dn = jnp.swapaxes(col_down, 2, 3), jnp.swapaxes(row_down, 2, 3)
    feed_tables = [
        table(jnp.swapaxes(ffn1_down, 1, 2)),
        table(ffn1_up),
        table(jnp.swapaxes(ffn2_down, 1, 2)),
        table(ffn2_up),
    ]

    shard_at = lambda b, m: (m[PART], 0)
    (slices,) = run_kernel(
        pack_kernel,
        meta,
        [
            (self_out, block((slice_rows, d), shard_at)),
            (cross_qkv, block((1, slice_rows * groups, width), lambda b, m: (0, m[PART], 0))),
            (cross_out, block((slice_rows, d), shard_at)),
        ],
        [(sds((3 * slice_rows, d), BF16), whole((3 * slice_rows, d)))],
        us=1.5,
    )
    by_group = gather_direct(slices, "tensor")[1:]

    is_key = s == 0
    ctx_w = (cross_qkv, block((1, d, width), lambda b, m: (1 + m[AT_S], 0, 0)))
    ctx_up, ctx_dn = table(col_up, lambda m: 4 + m[AT_S]), table(col_dn, lambda m: 4 + m[AT_S])
    low_rows = ctx_len + 4 * rank
    ctx_pre, ctx_low, ctx_ssq, ctx_lat_t = run_kernel(
        functools.partial(context_kernel, groups),
        meta,
        [
            (context, whole(context.shape)),
            ctx_w,
            ctx_up,
            ctx_dn,
            (cross_bias, whole(cross_bias.shape)),
            (cross_gain, whole(cross_gain.shape)),
            table(col_up, 3),
            table(row_dn, 0, rows=2),
        ],
        [
            (sds((ctx_len, width), F32), whole((ctx_len, width))),
            (sds((low_rows, width), BF16), whole((low_rows, width))),
            (sds((8, tl), F32), whole((8, tl))),
            (sds((rank, ctx_len), BF16), whole((rank, ctx_len))),
        ],
        us=6,
        after=[slices],
    )
    cos, sin = rope_tables(positions[:, 0, :])
    rows_d = block((tc, d), lambda b, m: (b, 0))
    rows_w = block((tc, width), lambda b, m: (b, 0))
    rows_h = block((tc, HEAD_DIM), lambda b, m: (b, 0))
    lanes_8 = block((8, tc), lambda b, m: (0, b))
    self_tables = [table(col_up, 0, rows=3), table(col_dn, 0, rows=3)]
    y1, lat_t, pre_q, pre_k, raw_q, kv, ssq, vec = run_kernel(
        functools.partial(qkv_kernel, hc),
        meta,
        [
            (tok, rows_d),
            (modulation, whole(modulation.shape)),
            (time_emb[0], whole(modulation.shape)),
            (out_bias, whole(out_bias.shape)),
            (cross_norm_gain[None], whole((1, d))),
            (cross_norm_bias[None], whole((1, d))),
            (self_qkv, whole(self_qkv.shape)),
        ]
        + self_tables
        + [
            (self_bias, whole(self_bias.shape)),
            (self_gain, whole(self_gain.shape)),
            (cos, rows_h),
            (sin, rows_h),
            (ctx_ssq, lanes_8),
        ],
        [
            (sds((tl, d), BF16), rows_d),
            (sds((3 * rank, tl), BF16), block((3 * rank, tc), lambda b, m: (0, b))),
            (sds((tl, width), BF16), rows_w),
            (sds((tl, width), BF16), rows_w),
            (sds((tl, width), BF16), rows_w),
            (sds((tl, 2 * width), BF16), block((tc, 2 * width), lambda b, m: (b, 0))),
            (sds((8, tl), F32), lanes_8),
            (sds((16, d), F32), whole((16, d))),
        ],
        grid=(groups,),
        scratch=[pltpu.VMEM((3 * rank, 3 * width), BF16)],
        us=15,
    )
    kv_sib = send(kv, "seq", pair)
    *first_steps, last_step = powers(groups)
    for step in first_steps:
        ssq = ssq + send(ssq, "tensor", flip(groups, step))
    ssq, *by_group = seal(ssq, *by_group)
    (by_group,) = run_kernel(
        stack_kernel,
        meta,
        [(a, whole(a.shape)) for a in by_group],
        [(sds((groups - 1,) + slices.shape, BF16), whole((groups - 1,) + slices.shape))],
        us=2,
    )
    ssq, by_group = seal(ssq, by_group)
    along = [send(by_group, "dp", flip(share, 1)), send(by_group, "dp", flip(share, 2))] if share > 1 else []
    st_own = lax.rsqrt((ssq + send(ssq, "tensor", flip(groups, last_step))) / d + EPS)
    st_sib = send(st_own, "seq", pair)
    by_group_sib = send(by_group, "seq", pair)
    st_sib, by_group_sib, kv_sib = seal(st_sib, by_group_sib, kv_sib)
    ctx_low, _ = seal(ctx_low, st_own)
    ctx_pieces = gather_direct(ctx_low, "tensor")

    all_8 = whole((8, tl))
    turned = lambda r, m: lax.rem(m[AT_T] + r, groups)
    kv_at = lambda lane: block((tl, HEAD_DIM), lambda h, r, m: (0, lane + h))
    own_rows = block((tc, HEAD_DIM), lambda h, r, m: (0, h))
    *blocks, mixed, lses, kn, knt, vn, qn_self = run_kernel(
        functools.partial(attention_kernel, groups),
        meta,
        [
            (raw_q, block((tc, HEAD_DIM), lambda h, r, m: (turned(r, m), h))),
            (st_own, block((8, tc), lambda h, r, m: (0, turned(r, m)))),
            (st_own, all_8),
            (st_sib, all_8),
            (kv, kv_at(0)),
            (kv_sib, kv_at(0)),
            (kv, kv_at(hc)),
            (kv_sib, kv_at(hc)),
        ],
        [(sds((tc, width), BF16), own_rows)] * groups
        + [
            (sds((tl, width), BF16), block((tc, HEAD_DIM), lambda h, r, m: (r, h))),
            (sds((8 * hc, tl), F32), block((8, tc), lambda h, r, m: (h, r))),
            (sds((2 * tl, width), BF16), block((2 * tl, HEAD_DIM), lambda h, r, m: (0, h))),
            (sds((width, 2 * tl), BF16), block((HEAD_DIM, 2 * tl), lambda h, r, m: (h, 0))),
            (sds((2 * tl, width), BF16), block((2 * tl, HEAD_DIM), lambda h, r, m: (0, h))),
            (sds((tl, width), BF16), block((tc, HEAD_DIM), lambda h, r, m: (r, h))),
        ],
        grid=(hc, groups),
        scratch=[pltpu.VMEM((HEAD_DIM, 2 * tl), BF16)],
        us=25,
        after=[by_group],
    )
    tied = seal(*blocks, *along, *ctx_pieces[1:])
    blocks, along, ctx_pieces[1:] = tied[:groups], tied[groups : groups + len(along)], tied[groups + len(along) :]
    os_pieces = [send(a, "tensor", shift(groups, r)) if r else a for r, a in enumerate(blocks)]
    weight_parts = [by_group] + along
    if share > 1:
        middle = far_cut(by_group.shape[1])
        weight_parts += [
            send(along[1][:, :middle], "dp", flip(share, 1)),
            send(along[0][:, middle:], "dp", flip(share, 2)),
        ]
    tied = seal(*os_pieces[1:], *along, *ctx_pieces)
    os_pieces[1:], tied = tied[: groups - 1], tied[groups - 1 :]
    weight_parts[1 : 1 + len(along)], ctx_pieces = tied[: len(along)], tied[len(along) :]
    weight_parts = weight_parts + [by_group_sib] + [send(p, "seq", pair) for p in weight_parts[1:]]
    ctx_sib = [send(p, "seq", pair) for p in ctx_pieces]

    vspec = whole(vec.shape)
    own_block = block((tc, d), lambda b, m: (m[AT_T], 0))
    weight_scratch = [
        pltpu.VMEM((groups, width, d), BF16),
        pltpu.VMEM((groups - 1, d, width), BF16),
        pltpu.VMEM((groups, width, d), BF16),
    ]
    sems = pltpu.SemaphoreType.DMA((len(plan) * groups + 2,))
    shared = [
        table(row_up),
        table(col_dn, 3),
        *[(p, whole(p.shape)) for p in ctx_pieces + ctx_sib],
        (st_own, all_8),
        (st_sib, all_8),
        (self_out, hbm),
        (cross_qkv, block((1, d, width), lambda b, m: (0, 0, 0))),
        (cross_out, hbm),
    ] + [(p, hbm) for p in weight_parts]
    whole_of = lambda shape, dtype: (sds(shape, dtype), whole(shape))
    y2, x2, x1, y3, qn, qc, oc, os_all, lse_c, lats = run_kernel(
        functools.partial(cross_kernel, groups, hc, plan),
        meta,
        [(p, whole(p.shape)) for p in os_pieces] + [(tok, own_block), (vec, vspec)] + shared,
        [
            whole_of((tc, d), BF16),
            whole_of((tc, d), F32),
            whole_of((tc, d), F32),
            whole_of((tc, d), BF16),
            whole_of((tc, d), BF16),
            whole_of((tc, d), F32),
            whole_of((tc, d), BF16),
            whole_of((tc, d), BF16),
            whole_of((16, tc), F32),
            whole_of((3 * rank, tc), BF16),
        ],
        scratch=weight_scratch + [sems],
        us=20,
    )

    tiles = [(a, min(768, ff - a)) for a in range(0, ff, 768)]
    w1t = ffn_in.T
    y2_pieces = ring_pieces(y2, "tensor")
    feed_bias = ffn_bias.astype(F32)[None]
    feed_out, dys, acc = None, [], None
    for r in range(groups):
        place = block((tc, d), lambda b, m, r=r: (lax.rem(m[AT_T] + groups - r, groups), 0))
        ins = [(y2_pieces[r], whole((tc, d))), (og, place), (vec, vspec), (feed_bias, whole(feed_bias.shape))]
        ins += feed_tables + [(w1t, hbm), (ffn_out, hbm)]
        if r == 0:
            ins += [(x2, whole((tc, d)))]
        else:
            ins += [(a, whole(a.shape)) for a in acc] + [(feed_out, hbm)]
        feed_out, dy, *acc = run_kernel(
            functools.partial(feed_kernel, tiles, r == 0),
            meta,
            ins,
            [(sds((tl, d), BF16), place), whole_of((tc, d), F32 if r == 0 else BF16)]
            + [whole_of((rank, n), F32) for n in (ff, d, d, ff)],
            scratch=[pltpu.VMEM((ff, d), BF16), pltpu.VMEM((ff, d), BF16), pltpu.SemaphoreType.DMA((2, len(tiles)))],
            us=18,
            aliases={15: 0} if r else None,
        )
        dys.append(dy)
    g_up1, g_dn1, g_up2, g_dn2 = acc

    dy_own, dy_in = ring_total(dys, "tensor")
    feed_out, dy_in = seal(feed_out, dy_in)
    line = Line(meta, tc) if groups == 4 else None
    if line:
        for r in range(groups):
            line.add(feed_out, r, "output", r)
        line.start()
    else:
        result = lax.psum(feed_out, "tensor")
    *dos, dx1, g_own, g_oth, g_rup, g_split, g_cqdn = run_kernel(
        functools.partial(cross_back_kernel, groups, hc, plan),
        meta,
        [(dy_own, whole((tc, d))), (dy_in, whole((tc, d))), (og, own_block)]
        + [(a, whole(a.shape)) for a in (x2, x1, y3, qn, qc, oc, os_all, lse_c, lats)]
        + [(vec, vspec)]
        + shared,
        [whole_of((tc, HEAD_DIM), BF16)] * groups
        + [whole_of((tc, width - HEAD_DIM), BF16)] * groups
        + [
            whole_of((tc, d), F32),
            whole_of((groups, ctx_len, width), BF16),
            whole_of((groups, ctx_len, width), BF16),
            whole_of((2 * rank, d), F32),
            whole_of((groups, 3 * rank, width), F32),
            whole_of((rank, d), F32),
        ],
        scratch=weight_scratch + [pltpu.VMEM((tc, d), F32), sems],
        us=26,
    )

    back_shift = lambda arrays: [send(a, "tensor", shift(groups, -r)) if r else a for r, a in enumerate(arrays)]
    moving = lambda: line.moving if line else []
    chains = Chains()
    dos[0], g_oth, g_cqdn, *arrived_line = seal(dos[0], g_oth, g_cqdn, *moving())
    dos_first = back_shift(dos[:groups])
    packed = jnp.concatenate([g_cqdn, g_dn1, g_rup[:rank], g_rup[rank:], g_up2, g_up1, g_dn2], axis=1)
    early_at = chains.add(adapter_steps(packed, 5 * d))
    g_oth = send(g_oth, "seq", pair)
    chains.step()
    g_oth, *dos_first = seal(g_oth, *dos_first)
    to_group = jnp.concatenate([g_own.astype(F32) + g_oth.astype(F32), g_split], axis=1)
    dos_rest = back_shift(dos[groups:])
    group_at = chains.add(ring_steps([to_group[r] for r in range(groups)], "tensor"))
    chains.step()

    back, dkv_in = [], []
    for h in range(hc):
        grads = dos_first if h == 0 else dos_rest
        lane = 0 if h == 0 else h - 1
        if h:
            if h == 1:
                tied = seal(*dos_rest, *chains.arrived(), back[-1][0], back[-1][2])
                dos_rest = tied[: len(dos_rest)]
                chains.put(tied[len(dos_rest) : -2])
                chains.step()
                if line:
                    line.advance(arrived_line)
            else:
                tied = seal(back[-1][0], back[-1][2])
            dkv_in.append(send(tied[-1], "seq", pair))
            grads = dos_rest
        back.append(
            run_kernel(
                functools.partial(attention_back_kernel, groups, h == 0),
                meta,
                [
                    (qn_self, block((tc, HEAD_DIM), lambda r, m, h=h: (r, h))),
                    (st_own, block((8, tc), lambda r, m: (0, turned(r, m)))),
                    (st_own, all_8),
                    (st_sib, all_8),
                    (kn, block((2 * tl, HEAD_DIM), lambda r, m, h=h: (0, h))),
                    (knt, block((HEAD_DIM, 2 * tl), lambda r, m, h=h: (h, 0))),
                    (vn, block((2 * tl, HEAD_DIM), lambda r, m, h=h: (0, h))),
                    (mixed, block((tc, HEAD_DIM), lambda r, m, h=h: (r, h))),
                    (lses, block((8, tc), lambda r, m, h=h: (h, r))),
                ]
                + [(g, block((tc, HEAD_DIM), lambda r, m, lane=lane: (0, lane))) for g in grads]
                + ([(a, all_8) for a in back[-1][3:]] if h else []),
                [
                    (sds((tl, HEAD_DIM), F32), block((tc, HEAD_DIM), lambda r, m: (turned(r, m), 0))),
                    whole_of((tl, 2 * HEAD_DIM), F32),
                    whole_of((tl, 2 * HEAD_DIM), BF16),
                    whole_of((8, tl), F32),
                    whole_of((8, tl), F32),
                ],
                grid=(groups,),
                scratch=[
                    pltpu.VMEM((2 * tl, HEAD_DIM), F32),
                    pltpu.VMEM((2 * tl, HEAD_DIM), F32),
                    pltpu.VMEM((tc, HEAD_DIM), BF16),
                ],
                us=12.5,
                after=list(tied[-2:-1]) if h else [],
            )
        )
    dq, dkv, dkv_out = zip(*[b[:3] for b in back])
    stat, cross = back[-1][3:]
    last_dkv = dkv_out[-1]
    stat, cross, last_dkv, *tied = seal(stat, cross, last_dkv, *chains.arrived(), *moving())
    count = len(chains.arrived())
    chains.put(tied[:count])
    arrived_line = tied[count:]
    dkv_in.append(send(last_dkv, "seq", pair))
    stat = stat + send(cross, "seq", pair)
    chains.step([group_at])
    for step in powers(groups):
        (other,) = seal(send(stat, "tensor", flip(groups, step)))
        stat = stat + other
    st_back = st_own * st_own * st_own * stat / d
    st_back, *tied = seal(st_back, *chains.arrived())
    chains.put(tied)
    chains.step()
    if line:
        line.advance(arrived_line)

    q_parts, late = [], None
    calls = 2
    for call in range(calls):
        steps = groups // calls
        in_d = block((tc, d), lambda b, m, c=call * steps: (c + b, 0))
        in_w = block((tc, width), lambda b, m, c=call * steps: (c + b, 0))
        in_h = block((tc, HEAD_DIM), lambda b, m, c=call * steps: (c + b, 0))
        in_2h = block((tc, 2 * HEAD_DIM), lambda b, m, c=call * steps: (c + b, 0))
        in_8 = block((8, tc), lambda b, m, c=call * steps: (0, c + b))
        size = (rank, 3 * (d + width))
        part, late = run_kernel(
            functools.partial(qkv_back_kernel, hc, call),
            meta,
            [(a, in_h) for a in dq]
            + [(a, in_2h) for a in list(dkv) + dkv_in]
            + [
                (pre_q, in_w),
                (pre_k, in_w),
                (st_own, in_8),
                (st_back, in_8),
                (self_gain, whole(self_gain.shape)),
                (cos, in_h),
                (sin, in_h),
                (self_qkv, hbm),
            ]
            + self_tables
            + [
                (tok, in_d),
                (vec, vspec),
                (y1, in_d),
                (lat_t, block((3 * rank, tc), lambda b, m, c=call * steps: (0, c + b))),
                (dx1, whole((tc, d))),
            ]
            + ([(late, whole(size))] if call else []),
            [(sds((steps * tc, d), BF16), block((tc, d), lambda b, m: (b, 0))), whole_of(size, F32)],
            grid=(steps,),
            scratch=[
                pltpu.VMEM((3 * rank, 3 * width), BF16),
                pltpu.VMEM(self_qkv.shape, BF16),
                pltpu.SemaphoreType.DMA(()),
            ],
            us=14,
        )
        q_parts.append(part)
        if line:
            for r in range(steps):
                line.add(part, r, "input_grad", call * steps + r)
        late, *tied = seal(late, *chains.arrived(), *moving())
        count = len(chains.arrived())
        chains.put(tied[:count])
        chains.step()
        if call == 0:
            to_group = chains.result(group_at)
            g_ctx, split = to_group[:ctx_len], to_group[ctx_len:]
            ctx_gain = jnp.where(is_key, cross_gain[1:2].astype(F32), 1.0)
            ctx_stat = jnp.sum(g_ctx * ctx_gain * ctx_pre, axis=1)
            stat_at = chains.add(total_steps(ctx_stat, "tensor"))
            chains.advance(stat_at)
        if line:
            line.advance(tied[count:])
    while not chains.done(stat_at):
        chains.put(seal(*chains.arrived()))
        chains.step()
    ctx_stat = chains.result(stat_at)

    ctx_inverse = jnp.concatenate([st_own[2, j * tc : j * tc + ctx_len // groups] for j in range(groups)])
    ctx_cubed = ctx_inverse * ctx_inverse * ctx_inverse * ctx_stat / d
    d_key = ctx_inverse[:, None] * ctx_gain * g_ctx - ctx_pre * ctx_cubed[:, None]
    d_ctx = jnp.where(is_key, d_key, g_ctx).astype(BF16)
    ctx_part, g_ctx_up, g_ctx_dn = run_kernel(
        context_back_kernel,
        meta,
        [
            (context, whole(context.shape)),
            ctx_w,
            ctx_up,
            ctx_dn,
            (ctx_lat_t, whole(ctx_lat_t.shape)),
            (d_ctx, whole(d_ctx.shape)),
        ],
        [whole_of((ctx_len, d), F32), whole_of((rank, width), F32), whole_of((rank, d), F32)],
        us=6,
        after=[line.acc[max(line.acc)]] if line else [],
    )

    pick = lambda g: [jnp.where(is_key, g, 0.0), jnp.where(is_key, 0.0, g)]
    late = jnp.concatenate(
        [late[:, : 3 * d]]
        + pick(g_ctx_dn)
        + [late[:, 3 * d :], split[:rank]]
        + pick(g_ctx_up)
        + [split[rank : 2 * rank], split[2 * rank :]]
        + [jnp.broadcast_to(adapter_index[0].astype(F32) / seq, (rank, HEAD_DIM))],
        axis=1,
    )
    ctx_at = chains.add(context_grad_steps(ctx_part))
    late_at = chains.add(adapter_steps(late, 5 * d))
    chains.advance(ctx_at)
    chains.advance(late_at)
    while line and line.at < len(line.parts):
        tied = seal(*chains.arrived(), *moving())
        count = len(chains.arrived())
        chains.put(tied[:count])
        chains.step()
        line.advance(tied[count:])
    while line and line.live():
        line.advance(line.moving)
    while chains.live():
        chains.put(seal(*chains.arrived()))
        chains.step()
    early, late, context_grad = chains.result(early_at), chains.result(late_at), chains.result(ctx_at).astype(F32)
    if line:
        result, input_grad = line.outs["output"], line.outs["input_grad"]
    else:
        input_grad = lax.psum(jnp.concatenate(q_parts), "tensor")

    indices = jnp.round(late[:, 0, -1].astype(F32)).astype(jnp.int32)
    early, late = spread(early, indices, slots), spread(late[:, :, :-HEAD_DIM], indices, slots)
    cut = lambda grads, start, size, count: [
        grads[:, :, start + j * size : start + (j + 1) * size] for j in range(count)
    ]
    wide, feed = cut(early, 0, d, 5), cut(early, 5 * d, ff, 2)
    wide_late, narrow = cut(late, 0, d, 5), cut(late, 5 * d, width, 8)
    swap = lambda a: jnp.swapaxes(a, -1, -2)
    return (
        result[None],
        input_grad[None],
        context_grad,
        swap(jnp.stack(wide_late[:3] + wide[:1] + wide_late[3:], axis=1)),
        jnp.stack(narrow[:6], axis=1),
        swap(wide[1]),
        feed[0],
        swap(jnp.stack(narrow[6:], axis=1)),
        jnp.stack(wide[2:4], axis=1),
        swap(feed[1]),
        wide[4],
    )


def solution(mesh):
    placed = (
        P("dp", "seq", None),
        P(None, "dp", "seq"),
        P("dp", None, None),
        P(),
        P(),
        P("dp"),
        P(None, None, "tensor"),
        P(None, "tensor"),
        P(None, "tensor"),
        P("tensor", None),
        P(None, None, "tensor"),
        P(None, "tensor"),
        P(None, "tensor"),
        P("tensor", None),
        P(),
        P(),
        P(None, "tensor"),
        P("tensor"),
        P("tensor", None),
        P(),
        P(),
        P(None, None, None, "tensor"),
        P(),
        P(None, None, "tensor"),
        P(None, None, "tensor", None),
        P(),
        P(None, "tensor", None),
        P(),
        P("dp", "seq", None),
    )
    return jax.shard_map(
        per_device,
        mesh=mesh,
        in_specs=placed,
        out_specs=(
            P("dp", "seq", None),
            P("dp", "seq", None),
            P(),
            P(),
            P(None, None, None, "tensor"),
            P(),
            P(None, None, "tensor"),
            P(None, None, "tensor", None),
            P(),
            P(None, "tensor", None),
            P(),
        ),
        check_vma=False,
    )
```

```python
import functools
import math

import jax
import jax.numpy as jnp
import numpy as np
from jax import lax
from jax.experimental import pallas as pl
from jax.experimental.pallas import tpu as pltpu
from jax.sharding import PartitionSpec as P

F32 = jnp.float32
BF16 = jnp.bfloat16
HEAD_DIM = 128
EPS = 1e-06
LOG2E = 1.4426950408889634
SCALE = HEAD_DIM ** (-0.5)
VMEM_LIMIT = 58 * 1024 * 1024
GELU_C = math.sqrt(2.0 / math.pi)
M0, M1, M2, M3, M4, M5, B0, B1, B2, CG, CB = range(11)
AT_T, AT_S, ADAPTER, PART, SLOTS = range(5)


def nn(left, right):
    return jnp.dot(left, right, preferred_element_type=F32)


def nt(left, right):
    return lax.dot_general(left, right, (((1,), (1,)), ((), ())), preferred_element_type=F32)


def both_ways(values):
    return values.astype(BF16), values.T.astype(BF16)


def row_total(values):
    ones = jnp.ones((8, values.shape[1]), BF16)
    high = values.astype(BF16)
    return nt(ones, high) + nt(ones, (values - high.astype(F32)).astype(BF16))


def mean(values):
    return jnp.mean(values, axis=-1, keepdims=True)


def normalize(values):
    centered = values - mean(values)
    inverse = lax.rsqrt(mean(centered * centered) + EPS)
    return centered * inverse, inverse


def normalize_back(normed, inverse, upstream):
    return inverse * (upstream - mean(upstream) - normed * mean(upstream * normed))


def pair_swap(values):
    width = values.shape[1]
    lane = lax.broadcasted_iota(jnp.int32, values.shape, 1)
    return jnp.where(lane % 2 == 0, pltpu.roll(values, width - 1, 1), pltpu.roll(values, 1, 1))


def rope(values, cosine, sine):
    return values * cosine + pair_swap(values) * sine


def rope_back(values, cosine, sine):
    return values * cosine - pair_swap(values) * sine


def heads_of(array, count):
    return [array[:, h * HEAD_DIM : (h + 1) * HEAD_DIM] for h in range(count)]


def whole(shape):
    return pl.BlockSpec(shape, lambda *_: (0,) * len(shape))


def run_kernel(body, meta, ins, outs, grid=(1,), scratch=(), us=1.0, aliases=None, after=()):
    count = len(ins)
    ins = list(ins) + [(a, pl.BlockSpec(memory_space=pl.ANY)) for a in after]
    arrays = [a for a, _ in ins]
    moved = sum(math.prod(a.shape) * a.dtype.itemsize for a in arrays[:count]) + sum(
        math.prod(s.shape) * s.dtype.itemsize for s, _ in outs
    )

    def reading(meta_ref, *refs):
        return body(meta_ref, *refs[:count], *refs[len(arrays) :])

    return pl.pallas_call(
        reading,
        grid_spec=pltpu.PrefetchScalarGridSpec(
            num_scalar_prefetch=1,
            grid=grid,
            in_specs=[s for _, s in ins],
            out_specs=[s for _, s in outs],
            scratch_shapes=list(scratch),
        ),
        out_shape=[s for s, _ in outs],
        input_output_aliases=aliases or {},
        compiler_params=pltpu.CompilerParams(vmem_limit_bytes=VMEM_LIMIT),
        cost_estimate=pl.CostEstimate(
            flops=int(us * 1.15e9), bytes_accessed=int(min(moved, us * 2e6)), transcendentals=0
        ),
    )(meta, *arrays)


def sds(shape, dtype):
    return jax.ShapeDtypeStruct(shape, dtype)


def qkv_kernel(head_count, meta, tok, mod, emb, b_out, cg, cb, w, up, dn, bias, gain, cos, sin, ctx_ssq, *outs):
    y1, lat_t, pre_q, pre_k, raw_q, kv, ssq, vec, up_s = outs
    width = head_count * HEAD_DIM
    rank = up.shape[2]
    modes = mod[...] + emb[...]

    @pl.when(pl.program_id(0) == 0)
    def _():
        row = lax.broadcasted_iota(jnp.int32, modes.shape, 0)
        rows = [modes + jnp.where((row == 1) | (row == 4), 1.0, 0.0), b_out[...].astype(F32), cg[...], cb[...]]
        vec[...] = jnp.concatenate(rows + [jnp.zeros((5, modes.shape[1]), F32)], axis=0)
        up_s[...] = jnp.zeros_like(up_s)
        for j in range(3):
            up_s[j * rank : (j + 1) * rank, j * width : (j + 1) * width] = up[0, j]

    normed, _ = normalize(tok[...].astype(F32))
    y = (normed * (1.0 + modes[1:2, :]) + modes[0:1, :]).astype(BF16)
    y1[...] = y
    down = jnp.concatenate([dn[0, j] for j in range(3)], axis=0)
    lat = nt(y, down).astype(BF16)
    lat_t[...] = nt(down, y).astype(BF16)
    totals = []
    for j in range(3):
        lanes = slice(j * width, (j + 1) * width)
        u = nn(y, w[j]) + nn(lat, up_s[:, lanes]) + bias[j : j + 1, :].astype(F32)
        if j == 2:
            kv[:, width:] = u.astype(BF16)
            continue
        (pre_q, pre_k)[j][...] = u.astype(BF16)
        totals.append(row_total(u * u))
        scaled = u * gain[j : j + 1, :].astype(F32)
        for h in range(head_count):
            lanes = slice(h * HEAD_DIM, (h + 1) * HEAD_DIM)
            (raw_q, kv)[j][:, lanes] = rope(scaled[:, lanes], cos[...], sin[...]).astype(BF16)
    row = lax.broadcasted_iota(jnp.int32, totals[0].shape, 0)
    ssq[...] = jnp.where(row == 0, totals[0], jnp.where(row == 1, totals[1], ctx_ssq[...]))


def attention_kernel(groups, meta, raw_q, st, st_own, st_sib, k_own, k_sib, v_own, v_sib, *outs):
    blocks, (out, lse, kn, knt, vn, qn, vt) = outs[:groups], outs[groups:]
    count = k_own.shape[0]
    step = pl.program_id(1)

    @pl.when(step == 0)
    def _():
        for at, (k, s, v) in enumerate(((k_own, st_own, v_own), (k_sib, st_sib, v_sib))):
            rows = slice(at * count, (at + 1) * count)
            scaled = k[...].astype(F32) * s[...].T[:, 1:2]
            kn[rows, :] = scaled.astype(BF16)
            knt[:, rows] = scaled.T.astype(BF16)
            vn[rows, :] = v[...]
            vt[:, rows] = v[...].astype(F32).T.astype(BF16)

    q = (raw_q[...].astype(F32) * (st[...].T[:, 0:1] * (SCALE * LOG2E))).astype(BF16)
    qn[...] = q
    scores = nt(kn[...], q)
    highest = jnp.max(scores, axis=0, keepdims=True)
    e = jnp.exp2(scores - highest)
    total = jnp.sum(e, axis=0, keepdims=True)
    mixed = (nn(vt[...], e.astype(BF16)) / total).T.astype(BF16)
    out[...] = mixed
    for r in range(groups):

        @pl.when(step == r)
        def _(r=r):
            blocks[r][...] = mixed

    lse[...] = jnp.broadcast_to(highest + jnp.log2(total), lse.shape)


def attention_back_kernel(groups, first, meta, qn, st, st_own, st_sib, kn, knt, vn, out, lse, *rest):
    grads, rest = rest[:groups], rest[groups:]
    if not first:
        stat_in, cross_in = rest[:2]
        rest = rest[2:]
    dq, dkv_own, dkv_sib, stat, cross, dk_acc, dv_acc, g_s = rest
    count = kn.shape[0] // 2
    size = qn.shape[0]
    step = pl.program_id(0)

    @pl.when(step == 0)
    def _():
        dk_acc[...] = jnp.zeros_like(dk_acc)
        dv_acc[...] = jnp.zeros_like(dv_acc)
        stat[...] = jnp.zeros_like(stat) if first else stat_in[...]
        cross[...] = jnp.zeros_like(cross) if first else cross_in[...]

    for r in range(groups):

        @pl.when(step == r)
        def _(r=r):
            g_s[...] = grads[r][...]

    q = qn[...]
    g = g_s[...]
    delta = row_total(g.astype(F32) * out[...].astype(F32))[0:1, :]
    p = jnp.exp2(nt(kn[...], q) - lse[0:1, :])
    dv_acc[...] += nn(p.astype(BF16), g)
    ds = (p * (nt(vn[...], g) - delta)).astype(BF16)
    dk_acc[...] += nn(ds, q)
    dqs = nn(knt[...], ds).T * SCALE
    dq[...] = dqs
    lanes = pl.ds(pl.multiple_of(lax.rem(meta[AT_T] + step, groups) * size, size), size)
    total = row_total(dqs * q.astype(F32)) / (st[0:1, :] * (SCALE * LOG2E))
    stat[:, lanes] += jnp.where(lax.broadcasted_iota(jnp.int32, total.shape, 0) == 0, total, 0.0)

    @pl.when(step == pl.num_programs(0) - 1)
    def _():
        for at, (s, dkv, sums) in enumerate(((st_own, dkv_own, stat), (st_sib, dkv_sib, cross))):
            rows = slice(at * count, (at + 1) * count)
            dk = dk_acc[rows, :] * (1.0 / LOG2E)
            dkv[:, :HEAD_DIM] = dk.astype(dkv.dtype)
            dkv[:, HEAD_DIM:] = dv_acc[rows, :].astype(dkv.dtype)
            all_k = row_total(dk * kn[rows, :].astype(F32)) / s[1:2, :]
            sums[...] += jnp.where(lax.broadcasted_iota(jnp.int32, all_k.shape, 0) == 1, all_k, 0.0)


def qkv_back_kernel(head_count, call, meta, *refs):
    n = head_count
    dq, dkv, dkv_in = (refs[j * n : (j + 1) * n] for j in range(3))
    refs = refs[3 * n :]
    pre_q, pre_k, st, st_back, gain_in, cos, sin, w, up_in, dn_in, tok, vec, y1, lat_t, dx1 = refs[:15]
    packed_in = refs[15] if call else None
    part, packed, up, w_s, sem = refs[-5:]
    step = pl.program_id(0)
    fetch = pltpu.make_async_copy(w, w_s, sem)

    @pl.when(step == 0)
    def _():
        fetch.start()
        packed[...] = packed_in[...] if call else jnp.zeros_like(packed)

    inverse, cubed = st[...].T, st_back[...].T
    c, s = cos[...], sin[...]
    width = n * HEAD_DIM
    rank = up_in.shape[2]
    d = tok.shape[1]
    gain = gain_in[...].astype(F32)
    up[...] = jnp.zeros_like(up)
    for j in range(3):
        up[j * rank : (j + 1) * rank, j * width : (j + 1) * width] = up_in[0, j]
    dn = jnp.concatenate([dn_in[0, j] for j in range(3)], axis=0)
    dk = [a[:, :HEAD_DIM] + b[:, :HEAD_DIM].astype(F32) for a, b in zip(dkv, dkv_in)]
    dv = [a[:, HEAD_DIM:] + b[:, HEAD_DIM:].astype(F32) for a, b in zip(dkv, dkv_in)]
    grads = [
        jnp.concatenate([rope_back(ref[...], c, s) for ref in dq], axis=1),
        jnp.concatenate([rope_back(a, c, s) for a in dk], axis=1),
        jnp.concatenate(dv, axis=1).astype(BF16),
    ]
    for j, pre in enumerate((pre_q, pre_k)):
        grads[j] = (
            inverse[:, j : j + 1] * gain[j : j + 1, :] * grads[j] - pre[...].astype(F32) * cubed[:, j : j + 1]
        ).astype(BF16)
    joined = jnp.concatenate(grads, axis=1)
    d_lat = nt(joined, up[...]).astype(BF16)
    d_lat_t = nt(up[...], joined).astype(BF16)
    total = nn(d_lat, dn)

    @pl.when(step == 0)
    def _():
        fetch.wait()

    for j in range(3):
        total = total + nt(grads[j], w_s[j])
    normed, inverse = normalize(tok[...].astype(F32))
    back = normalize_back(normed, inverse, total * vec[M1 : M1 + 1, :])
    own = (meta[AT_T] == call * pl.num_programs(0) + step).astype(F32)
    part[...] = (back + dx1[...] * own).astype(part.dtype)
    g_dn = nn(d_lat_t, y1[...])
    for j in range(3):
        rows = slice(j * rank, (j + 1) * rank)
        g_up = nn(lat_t[rows, :], grads[j])
        for start, g in ((j * d, g_dn[rows, :]), (3 * d + j * width, g_up)):
            lanes = slice(start, start + g.shape[1])
            packed[:, lanes] += g


def context_kernel(groups, meta, ctx, w, up, dn, bias, gain, up_q, down_row, pre, low, ssq, lat_t):
    key = meta[AT_S] == 0
    c = ctx[...]
    count = c.shape[0]
    rank, width = up.shape[2:]
    lat = nt(c, dn[0, 0]).astype(BF16)
    lat_t[...] = nt(dn[0, 0], c).astype(BF16)
    b, g = bias[...].astype(F32), gain[...].astype(F32)
    u = nn(c, w[0]) + nn(lat, up[0, 0]) + jnp.where(key, b[1:2, :], b[2:3, :])
    pre[...] = u
    low[:count, :] = (u * jnp.where(key, g[1:2, :], 1.0)).astype(BF16)
    low[count : count + rank, :] = up_q[0, 0]
    low[count + rank : count + 2 * rank, :] = down_row[0, 0]
    low[count + 2 * rank : count + 3 * rank, :] = down_row[0, 1]
    row = lax.broadcasted_iota(jnp.int32, (rank, width), 0)
    low[count + 3 * rank :, :] = jnp.where(row == 0, b[0:1, :], jnp.where(row == 1, g[0:1, :], 0.0)).astype(BF16)
    total = row_total(u * u)
    share, block = count // groups, ssq.shape[1] // groups
    ssq[...] = jnp.zeros_like(ssq)
    for j in range(groups):
        ssq[:, j * block : j * block + share] = total[:, j * share : (j + 1) * share]


def context_row(groups, count, rows):
    share, block = count // groups, rows.shape[1] // groups
    return jnp.concatenate([rows[2:3, j * block : j * block + share] for j in range(groups)], axis=1)


def context_back_kernel(meta, ctx, w, up_in, dn_in, lat_t, grad, out, g_up, g_dn):
    g = grad[...]
    up, dn = up_in[0, 0], dn_in[0, 0]
    d_lat = nt(g, up).astype(BF16)
    d_lat_t = nt(up, g).astype(BF16)
    out[...] = nt(g, w[0]) + nn(d_lat, dn)
    g_up[...] = nn(lat_t[...], g)
    g_dn[...] = nn(d_lat_t, ctx[...])


def pack_kernel(meta, wo, wq, wc, out):
    rows, width = wo.shape[0], wq.shape[2]
    out[:rows, :] = wo[...]
    for j in range(out.shape[1] // width):
        out[rows : 2 * rows, j * width : (j + 1) * width] = wq[0, j * rows : (j + 1) * rows, :]
    out[2 * rows :, :] = wc[...]


def stack_kernel(meta, *refs):
    for j, ref in enumerate(refs[:-1]):
        refs[-1][j] = ref[...]


def start_copies(meta, plan, refs, targets, sems, own):
    copies = [[] for _ in targets]
    at = 0
    for source, weight, first, rows, slot, inner, size in plan:
        target = targets[weight]
        width = target.shape[2]
        sides = refs[source].shape[2] // width
        for j in range(sides):
            start = pl.multiple_of(meta[slot] * (size * sides) + (j * size + inner), 16)
            copies[weight].append(
                pltpu.make_async_copy(
                    refs[source].at[:, pl.ds(first, rows), pl.ds(j * width, width)],
                    target.at[pl.ds(target.shape[0] - refs[source].shape[0], refs[source].shape[0]), pl.ds(start, rows), :],
                    sems.at[at],
                )
            )
            at += 1
    for weight, shard in own.items():
        copies[weight].append(pltpu.make_async_copy(shard, targets[weight].at[0], sems.at[at]))
        at += 1
    for weight in copies:
        for copy in weight:
            copy.start()
    return copies


def finish(copies):
    for copy in copies:
        copy.wait()


def cross_kernel(groups, head_count, plan, meta, *refs):
    n = groups * head_count
    os_in, refs = refs[:groups], refs[groups:]
    tok, vec, up, dn3 = refs[:4]
    ctx_own, ctx_sib, refs = refs[4 : 4 + groups], refs[4 + groups : 4 + 2 * groups], refs[4 + 2 * groups :]
    st_own, st_sib, wo_own, wq_own, wc_own = refs[:5]
    k = 1 + max(entry[0] for entry in plan)
    sources, refs = refs[5 : 5 + k], refs[5 + k :]
    y2, x2, x1, y3, qn, qc, oc, os_all, lse, lats = refs[:10]
    wo, wq, wc, sems = refs[10:]
    copies = start_copies(meta, plan, sources, (wo, wq, wc), sems, {0: wo_own, 2: wc_own})
    full = lambda weight: weight[...].reshape(weight.shape[0] * weight.shape[1], weight.shape[2])
    dn3 = dn3[0, 0]
    rank = dn3.shape[0]
    ctx_len = ctx_own[0].shape[0] - 4 * rank
    small = jnp.concatenate([ctx_own[r][ctx_len:, :] for r in range(groups)], axis=1)
    first = meta[AT_S] == 0
    key_row = context_row(groups, ctx_len, jnp.where(first, st_own[...], st_sib[...]))
    ctx_inverse = jnp.broadcast_to(key_row, (8, ctx_len)).T[:, 0:1]
    width = head_count * HEAD_DIM
    for r in range(groups):
        os_all[:, r * width : (r + 1) * width] = os_in[r][...]
    os_v = os_all[...]
    down0, down1 = small[rank : 2 * rank, :], small[2 * rank : 3 * rank, :]
    lat = nt(os_v, down0).astype(BF16)
    lats[0:rank, :] = nt(down0, os_v).astype(BF16)
    total = nn(lat, up[0, 0])
    finish(copies[0])
    total = total + nn(os_v, full(wo))
    x1_v = tok[...].astype(F32) + (total + vec[B0 : B0 + 1, :]) * vec[M2 : M2 + 1, :]
    x1[...] = x1_v
    normed, _ = normalize(x1_v)
    y3_v = (normed * vec[CG : CG + 1, :] + vec[CB : CB + 1, :]).astype(BF16)
    y3[...] = y3_v
    lat = nt(y3_v, dn3).astype(BF16)
    lats[2 * rank : 3 * rank, :] = nt(dn3, y3_v).astype(BF16)
    finish(copies[1])
    q = nn(lat, small[0:rank, :]) + small[3 * rank : 3 * rank + 1, :].astype(F32)
    q = q + jnp.concatenate([nn(y3_v, wq[r - 1] if r else wq_own[0]) for r in range(groups)], axis=1)
    qc[...] = q
    inverse = lax.rsqrt(mean(q * q) + EPS)
    gain = small[3 * rank + 1 : 3 * rank + 2, :].astype(F32)
    qn[...] = (q * (inverse * (SCALE * LOG2E)) * gain).astype(BF16)
    for j in range(n):
        r, lanes = j // head_count, slice((j % head_count) * HEAD_DIM, (j % head_count + 1) * HEAD_DIM)
        a, b = ctx_own[r][:ctx_len, lanes], ctx_sib[r][:ctx_len, lanes]
        keys, values = jnp.where(first, a, b), jnp.where(first, b, a)
        keys = (keys.astype(F32) * ctx_inverse).astype(BF16)
        scores = nt(keys, qn[:, j * HEAD_DIM : (j + 1) * HEAD_DIM])
        highest = jnp.max(scores, axis=0, keepdims=True)
        e = jnp.exp2(scores - highest)
        sums = jnp.sum(e, axis=0, keepdims=True)
        mixed = nn(values.astype(F32).T.astype(BF16), e.astype(BF16)) / sums
        oc[:, j * HEAD_DIM : (j + 1) * HEAD_DIM] = mixed.T.astype(BF16)
        lse[j : j + 1, :] = highest + jnp.log2(sums)
    oc_v = oc[...]
    lat = nt(oc_v, down1).astype(BF16)
    lats[rank : 2 * rank, :] = nt(down1, oc_v).astype(BF16)
    total = nn(lat, up[0, 1])
    finish(copies[2])
    total = total + nn(oc_v, full(wc))
    x2_v = x1_v + total + vec[B1 : B1 + 1, :]
    x2[...] = x2_v
    normed, _ = normalize(x2_v)
    y2[...] = (normed * vec[M4 : M4 + 1, :] + vec[M3 : M3 + 1, :]).astype(BF16)


def cross_back_kernel(groups, head_count, plan, meta, *refs):
    n = groups * head_count
    dy_own, dy_in, og, x2, x1, y3, qn, qc, oc, os_all, lse, lats, vec, up, dn3 = refs[:15]
    ctx_own, ctx_sib, refs = refs[15 : 15 + groups], refs[15 + groups : 15 + 2 * groups], refs[15 + 2 * groups :]
    st_own, st_sib, wo_own, wq_own, wc_own = refs[:5]
    k = 1 + max(entry[0] for entry in plan)
    sources, refs = refs[5 : 5 + k], refs[5 + k :]
    dos_first, dos_rest, refs = refs[:groups], refs[groups : 2 * groups], refs[2 * groups :]
    dx1, g_own, g_oth, g_up, g_split, g_dn, wo, wq, wc, dq_s, sems = refs
    copies = start_copies(meta, plan, sources, (wo, wq, wc), sems, {0: wo_own, 2: wc_own})
    full = lambda weight: weight[...].reshape(weight.shape[0] * weight.shape[1], weight.shape[2])
    dn3 = dn3[0, 0]
    rank = dn3.shape[0]
    ctx_len = ctx_own[0].shape[0] - 4 * rank
    small = jnp.concatenate([ctx_own[r][ctx_len:, :] for r in range(groups)], axis=1)
    first = meta[AT_S] == 0
    key_row = context_row(groups, ctx_len, jnp.where(first, st_own[...], st_sib[...]))
    ctx_inverse = jnp.broadcast_to(key_row, (8, ctx_len)).T[:, 0:1]
    width = head_count * HEAD_DIM
    down0, down1 = small[rank : 2 * rank, :], small[2 * rank : 3 * rank, :]
    normed, inverse = normalize(x2[...])
    dn = (dy_own[...] + dy_in[...].astype(F32)) * vec[M4 : M4 + 1, :]
    dx2 = og[...].astype(F32) + normalize_back(normed, inverse, dn)
    grad = dx2.astype(BF16)
    d_lat = nt(grad, up[0, 1]).astype(BF16)
    d_lat_t = nt(up[0, 1], grad).astype(BF16)
    oc_v = oc[...]
    g_up[rank : 2 * rank, :] = nn(lats[rank : 2 * rank, :], grad)
    split = nn(d_lat_t, oc_v)
    for r in range(groups):
        g_split[r, 2 * rank : 3 * rank, :] = split[:, r * width : (r + 1) * width]
    finish(copies[2])
    d_oc = nn(d_lat, down1) + nt(grad, full(wc))
    d_oc = d_oc.astype(BF16)
    for j in range(n):
        r, lanes = j // head_count, slice((j % head_count) * HEAD_DIM, (j % head_count + 1) * HEAD_DIM)
        head = slice(j * HEAD_DIM, (j + 1) * HEAD_DIM)
        a, b = ctx_own[r][:ctx_len, lanes], ctx_sib[r][:ctx_len, lanes]
        keys, values = jnp.where(first, a, b), jnp.where(first, b, a)
        keys = (keys.astype(F32) * ctx_inverse).astype(BF16)
        q, g = qn[:, head], d_oc[:, head]
        delta = row_total(g.astype(F32) * oc_v[:, head].astype(F32))[0:1, :]
        p = jnp.exp2(nt(keys, q) - lse[j : j + 1, :])
        dv = nn(p.astype(BF16), g)
        ds = (p * (nt(values, g) - delta)).astype(BF16)
        dk = nn(ds, q) * (1.0 / LOG2E)
        dq_s[:, head] = nn(keys.astype(F32).T.astype(BF16), ds).T * SCALE
        g_own[r, :, lanes] = jnp.where(first, dk, dv).astype(BF16)
        g_oth[r, :, lanes] = jnp.where(first, dv, dk).astype(BF16)
    q = qc[...]
    inverse = lax.rsqrt(mean(q * q) + EPS)
    gain = small[3 * rank + 1 : 3 * rank + 2, :].astype(F32)
    scaled = dq_s[...] * gain
    stat = mean(scaled * q)
    dqc = (inverse * scaled - q * (inverse * inverse * inverse * stat)).astype(BF16)
    up_q = small[0:rank, :]
    d_lat = nt(dqc, up_q).astype(BF16)
    d_lat_t = nt(up_q, dqc).astype(BF16)
    split = nn(lats[2 * rank : 3 * rank, :], dqc)
    for r in range(groups):
        g_split[r, 0:rank, :] = split[:, r * width : (r + 1) * width]
    g_dn[...] = nn(d_lat_t, y3[...])
    dy3 = nn(d_lat, dn3)
    finish(copies[1])
    for r in range(groups):
        part = dqc[:, r * width : (r + 1) * width]
        dy3 = dy3 + nt(part, wq[r - 1] if r else wq_own[0])
    normed, inverse = normalize(x1[...])
    dx1_v = dx2 + normalize_back(normed, inverse, dy3 * vec[CG : CG + 1, :])
    dx1[...] = dx1_v
    grad = (dx1_v * vec[M2 : M2 + 1, :]).astype(BF16)
    d_lat = nt(grad, up[0, 0]).astype(BF16)
    d_lat_t = nt(up[0, 0], grad).astype(BF16)
    g_up[0:rank, :] = nn(lats[0:rank, :], grad)
    split = nn(d_lat_t, os_all[...])
    for r in range(groups):
        g_split[r, rank : 2 * rank, :] = split[:, r * width : (r + 1) * width]
    finish(copies[0])
    d_os = nn(d_lat, down0) + nt(grad, full(wo))
    for r in range(groups):
        block = d_os[:, r * width : (r + 1) * width]
        dos_first[r][...] = block[:, :HEAD_DIM].astype(BF16)
        dos_rest[r][...] = block[:, HEAD_DIM:].astype(BF16)


def feed_kernel(tiles, first, meta, *refs):
    y2, og, vec, bias, dn1, up1, dn2, up2, w1_h, w2_h = refs[:10]
    if first:
        x2 = refs[10]
    else:
        acc = refs[10:14]
    refs = refs[11:] if first else refs[15:]
    dn1, up1, dn2, up2 = dn1.at[0], up1.at[0], dn2.at[0], up2.at[0]
    out, dy, g_up1, g_dn1, g_up2, g_dn2, w1, w2, sems = refs
    copies = []
    for at, (start, size) in enumerate(tiles):
        rows = pl.ds(start, size)
        pair = [
            pltpu.make_async_copy(h.at[rows, :], v.at[rows, :], sems.at[j, at])
            for j, (h, v) in enumerate(((w1_h, w1), (w2_h, w2)))
        ]
        for copy in pair:
            copy.start()
        copies.append(pair)
    y = y2[...]
    dff = (og[...].astype(F32) * vec[M5 : M5 + 1, :]).astype(BF16)
    lat, lat_t = both_ways(nt(y, dn1[...]))
    drl, drl_t = both_ways(nt(dff, up2[...]))
    part = grad = rl = d_lat = 0.0
    for (start, size), pair in zip(tiles, copies):
        cols = slice(start, start + size)
        finish(pair)
        h = nt(y, w1[cols, :]) + nn(lat, up1[:, cols]) + bias[:, cols]
        du = nt(dff, w2[cols, :]) + nn(drl, dn2[:, cols])
        sq = h * h
        t = jnp.tanh(GELU_C * h * (1.0 + 0.044715 * sq))
        act = (0.5 * h * (1.0 + t)).astype(BF16)
        slope = 0.5 * (1.0 + t) + (0.5 * GELU_C) * h * (1.0 - t * t) * (1.0 + (3.0 * 0.044715) * sq)
        dh = (du * slope).astype(BF16)
        part = part + nn(act, w2[cols, :])
        grad = grad + nn(dh, w1[cols, :])
        rl = rl + nt(act, dn2[:, cols])
        d_lat = d_lat + nt(dh, up1[:, cols])
        new_up1, new_dn2 = nn(lat_t, dh), nn(drl_t, act)
        g_up1[:, cols] = new_up1 if first else new_up1 + acc[0][:, cols]
        g_dn2[:, cols] = new_dn2 if first else new_dn2 + acc[3][:, cols]
    rl, rl_t = both_ways(rl)
    d_lat, d_lat_t = both_ways(d_lat)
    part = part + nn(rl, up2[...])
    grad = grad + nn(d_lat, dn1[...])
    new_dn1, new_up2 = nn(d_lat_t, y), nn(rl_t, dff)
    g_dn1[...] = new_dn1 if first else new_dn1 + acc[1][...]
    g_up2[...] = new_up2 if first else new_up2 + acc[2][...]
    part = part * vec[M5 : M5 + 1, :]
    if first:
        part = part + x2[...] + vec[B2 : B2 + 1, :] * vec[M5 : M5 + 1, :]
    out[...] = part.astype(out.dtype)
    dy[...] = grad.astype(dy.dtype)


def shift(count, step):
    return [(a, (a + step) % count) for a in range(count)]


def flip(count, step):
    return [(a, a ^ step) for a in range(count)]


def powers(count):
    return [1 << j for j in range(count.bit_length() - 1)]


def send(values, axis, pairs):
    return jax.tree.map(lambda v: lax.ppermute(v, axis, pairs), values)


def ring_pieces(own, axis):
    count = lax.axis_size(axis)
    pieces = [own]
    for _ in range(count - 1):
        pieces.append(send(pieces[-1], axis, shift(count, 1)))
    return pieces


def ring_total(parts, axis):
    count = lax.axis_size(axis)
    moving = parts[1]
    for r in range(2, count):
        moving = send(moving, axis, shift(count, 1))
        moving = (moving.astype(F32) + parts[r].astype(F32)).astype(BF16)
    return parts[0], send(moving, axis, shift(count, 1))


def gather_direct(own, axis):
    count = lax.axis_size(axis)
    return [own] + [send(own, axis, shift(count, r)) for r in range(1, count)]


def scatter_direct(parts, axis):
    count = lax.axis_size(axis)
    return parts[0].astype(F32) + sum(
        send(parts[r].astype(BF16), axis, shift(count, -r)).astype(F32) for r in range(1, count)
    )


def gather_flipped(own, axis):
    count = lax.axis_size(axis)
    return [own] + [send(own, axis, flip(count, j)) for j in range(1, count)]


def total_flipped(own, axis):
    terms = [v.astype(F32) for v in gather_flipped(own, axis)]
    while len(terms) > 1:
        terms = [terms[j] + terms[j + 1] for j in range(0, len(terms), 2)]
    return terms[0]


def halves(values, axis):
    half = values.shape[0] // 2
    low, high = values[:half], values[half:]
    upper = lax.axis_index(axis) == 1
    return jnp.where(upper, high, low), jnp.where(upper, low, high)


def pair_scatter(values):
    kept, sent = halves(values, "seq")
    return kept + send(sent.astype(BF16), "seq", flip(2, 1)).astype(F32)


def pair_gather(values, dim):
    other = send(values, "seq", flip(2, 1))
    upper = lax.axis_index("seq") == 1
    return jnp.concatenate([jnp.where(upper, other, values), jnp.where(upper, values, other)], axis=dim)


def place_blocks(blocks, axis):
    size = blocks[0].shape[0]
    out = jnp.zeros((size * len(blocks),) + blocks[0].shape[1:], blocks[0].dtype)
    index = lax.axis_index(axis)
    for j, block in enumerate(blocks):
        out = lax.dynamic_update_slice_in_dim(out, block, (index ^ j) * size, 0)
    return out


def total_twice(values, axis):
    for step in powers(lax.axis_size(axis)):
        values = values + send(values, axis, flip(lax.axis_size(axis), step))
    return values


class Chains:
    def __init__(self):
        self.chains, self.values, self.results = [], [], {}

    def add(self, chain):
        self.chains.append(chain)
        self.values.append(None)
        return len(self.chains) - 1

    def start(self, at):
        self.advance(at)

    def advance(self, at):
        try:
            self.values[at] = self.chains[at].send(self.values[at])
        except StopIteration as end:
            self.results[at] = end.value

    def step(self, skip=()):
        for at in range(len(self.chains)):
            if at not in self.results and at not in skip:
                self.advance(at)

    def live(self):
        return len(self.results) < len(self.chains)

    def done(self, at):
        return at in self.results

    def result(self, at):
        return self.results[at]

    def arrived(self):
        live = [self.values[at] for at in range(len(self.chains)) if at not in self.results]
        return jax.tree.leaves(live)

    def put(self, leaves):
        places = [at for at in range(len(self.chains)) if at not in self.results]
        structure = jax.tree.structure([self.values[at] for at in places])
        for at, value in zip(places, jax.tree.unflatten(structure, leaves)):
            self.values[at] = value


def seal(*values):
    return list(lax.optimization_barrier(values)) if values else []


def ring_steps(parts, axis):
    count = lax.axis_size(axis)
    moving = parts[1].astype(BF16)
    for r in range(2, count + 1):
        moving = yield send(moving, axis, shift(count, 1))
        if r < count:
            moving = (moving.astype(F32) + parts[r].astype(F32)).astype(BF16)
    return parts[0].astype(F32) + moving.astype(F32)


def line_kernel(shape, meta, *refs):
    inward, across, outward, both = shape
    inner = (meta[AT_T] == 1) | (meta[AT_T] == 2)
    count = (inward or outward) + inward + 2 * across + outward + both
    ins, outs = list(refs[:count]), list(refs[count:])
    add = lambda a, b: (a[...].astype(F32) + b[...].astype(F32)).astype(BF16)
    if inward or outward:
        first = ins.pop(0)
    if inward:
        outs.pop(0)[...] = add(ins.pop(0), first)
    if across:
        total = add(ins.pop(0), ins.pop(0))
        outs.pop(0)[...] = jnp.where(inner, total, ins.pop(0)[...]) if both else total
    if outward:
        outs.pop(0)[...] = jnp.where(inner, ins.pop(0)[...], first[...])


class Line:
    def __init__(self, meta, size):
        self.meta, self.size = meta, size
        self.parts, self.targets, self.outs = [], [], {}
        self.acc, self.total, self.at, self.moving = {}, {}, 0, []

    def add(self, array, block, target, out_block):
        self.parts.append((array, block))
        self.targets.append((target, out_block))

    def start(self):
        array, block = self.parts[self.at] if self.at < len(self.parts) else (None, None)
        inward, outward = array is not None, self.at - 2 in self.total
        pairs = [(0, 1), (3, 2)] * inward + [(1, 0), (2, 3)] * outward
        if inward and outward:
            mine = self.total[self.at - 2]
        elif inward:
            mine = array if array.shape[0] == self.size else array[block * self.size : (block + 1) * self.size]
        else:
            mine = self.total.get(self.at - 2)
        self.moving = [send(mine, "tensor", pairs)] if pairs else []
        across = self.at - 1 in self.acc
        if across:
            self.moving.append(send(self.acc[self.at - 1], "tensor", [(1, 2), (2, 1)]))
        self.shape = (inward, across, outward)

    def advance(self, moving):
        inward, across, outward = self.shape
        moving, at = list(moving), self.at
        first = moving.pop(0) if inward or outward else None
        second = moving.pop(0) if across else None
        both = across and at + 1 < len(self.parts)
        grid = 2
        rows = lambda block: pl.BlockSpec((self.size // grid, width), lambda b, m: (block * grid + b, 0))
        width = (second if first is None else first).shape[1]
        kind = sds((self.size, width), BF16)
        ins, outs, aliases = [], [], None
        if first is not None:
            ins.append((first, rows(0)))
        if inward:
            array, block = self.parts[at]
            ins.append((array, rows(block)))
            outs.append((kind, rows(0)))
        if across:
            ins += [(self.acc[at - 1], rows(0)), (second, rows(0))]
            outs.append((kind, rows(0)))
        if both:
            array, block = self.parts[at + 1]
            ins.append((array, rows(block)))
        if outward:
            ins.append((self.total[at - 2], rows(0)))
        count = len(ins)
        if outward:
            target, block = self.targets[at - 2]
            length = self.size * sum(t == target for t, _ in self.targets)
            outs.append((sds((length, width), BF16), rows(block)))
            if target in self.outs:
                ins.append((self.outs[target], pl.BlockSpec(memory_space=pl.ANY)))
                aliases = {count + 1: len(outs) - 1}

        def body(meta, *refs):
            line_kernel((inward, across, outward, both), meta, *refs[:count], *refs[len(ins) :])

        results = list(run_kernel(body, self.meta, ins, outs, grid=(grid,), us=3, aliases=aliases))
        if inward:
            self.acc[at] = results.pop(0)
        if across:
            self.total[at - 1] = results.pop(0)
        if outward:
            self.outs[self.targets[at - 2][0]] = results.pop(0)
        self.at, self.moving = at + 1, []
        if self.live():
            self.start()

    def live(self):
        return self.at < len(self.parts) + 2


def total_steps(value, axis):
    for step in powers(lax.axis_size(axis)):
        value = value + (yield send(value, axis, flip(lax.axis_size(axis), step)))
    return value


def adapter_steps(value, shared):
    groups, dp = lax.axis_size("tensor"), lax.axis_size("dp")
    pair, upper = flip(2, 1), lax.axis_index("seq") == 1
    kept, sent = halves(value, "seq")
    other = yield send(sent.astype(BF16), "seq", pair)
    value = kept + other.astype(F32)
    own, rest = value[:, :shared].astype(BF16), value[:, shared:].astype(BF16)
    for step in powers(groups):
        other = yield send(own, "tensor", flip(groups, step))
        own = (own.astype(F32) + other.astype(F32)).astype(BF16)
    value = jnp.concatenate([own, rest], axis=1)[None]
    for step in powers(dp):
        other = yield send(value, "dp", flip(dp, step))
        value = jnp.concatenate([value, other])
    other = yield send(value, "seq", pair)
    return jnp.concatenate([jnp.where(upper, other, value), jnp.where(upper, value, other)], axis=1)


def context_grad_steps(value):
    groups, dp = lax.axis_size("tensor"), lax.axis_size("dp")
    at_dp = lax.axis_index("dp")
    pair, second = flip(2, 1), lax.axis_index("seq") == 1
    kept, sent = halves(value, "seq")
    other = yield send(sent.astype(BF16), "seq", pair)
    value = kept + other.astype(F32)
    rows = value.shape[0] // dp
    parts = [lax.dynamic_slice_in_dim(value, (at_dp ^ j) * rows, rows, 0) for j in range(dp)]
    others = yield tuple(send(parts[j].astype(BF16), "dp", flip(dp, j)) for j in range(1, dp))
    value = (parts[0] + sum(other.astype(F32) for other in others)).astype(BF16)
    for step in powers(groups):
        other = yield send(value, "tensor", flip(groups, step))
        value = (value.astype(F32) + other.astype(F32)).astype(BF16)
    for step in powers(dp):
        other = yield send(value, "dp", flip(dp, step))
        upper = (at_dp & step) != 0
        value = jnp.concatenate([jnp.where(upper, other, value), jnp.where(upper, value, other)])
    other = yield send(value, "seq", pair)
    return jnp.concatenate([jnp.where(second, other, value), jnp.where(second, value, other)])


def weight_share():
    return 4 if lax.axis_size("dp") == 4 else 1


def weight_plan(rows, count):
    share, seq = weight_share(), lax.axis_size("seq")
    d, s = lax.axis_index("dp"), lax.axis_index("seq")
    slots = [(s ^ a) * share + ((d ^ b) if share > 1 else 0) for a in range(seq) for b in range(share)]
    total = rows * count
    cut = far_cut(total)
    half = [(0, 0, total, 0)]
    if share > 1:
        half += [(1, 0, total, 1), (2, 0, total, 2), (3, 0, cut, 3), (4, cut, total - cut, 3)]
    spans = half + [(len(half) + a, b, c, share + e) for a, b, c, e in half]
    plan = []
    for source, start, size, slot in spans:
        for weight in range(count):
            low, high = max(start, weight * rows), min(start + size, (weight + 1) * rows)
            if low < high:
                plan.append((source, weight, low - start, high - low, SLOTS + slot, low - weight * rows, rows))
    return plan, slots


def far_cut(total):
    return (total // 2 + 15) // 16 * 16


def rope_tables(grid_pos):
    sixth = HEAD_DIM // 6
    counts = [(HEAD_DIM - 4 * sixth) // 2, sixth, sixth]
    table = np.zeros((3, HEAD_DIM), np.float32)
    lane = 0
    for component, count in enumerate(counts):
        for pair in range(count):
            table[component, lane : lane + 2] = 10000.0 ** (-pair / count)
            lane += 2
    positions = grid_pos.astype(F32)
    angles = sum(positions[c][:, None] * table[c][None, :] for c in range(3))
    sign = np.where(np.arange(HEAD_DIM) % 2 == 0, -1.0, 1.0).astype(np.float32)
    return jnp.cos(angles), jnp.sin(angles) * sign[None, :]


def select_slot(table, index):
    return lax.dynamic_index_in_dim(table, index, 0, keepdims=False)


def spread(gradients, indices, slot_count):
    hits = (jnp.arange(slot_count)[:, None] == indices[None, :]).astype(F32)
    out = 0.0
    for latent in range(gradients.shape[0]):
        shape = (slot_count,) + (1,) * (gradients.ndim - 1)
        out = out + hits[:, latent].reshape(shape) * gradients[latent].astype(F32)[None]
    return out


def eight_rows(rows):
    return jnp.concatenate([jnp.stack(rows), jnp.zeros((8 - len(rows), rows[0].shape[0]), F32)])


def per_device(
    tokens,
    positions,
    time_emb,
    modulation,
    context,
    adapter_index,
    self_qkv,
    self_bias,
    self_gain,
    self_out,
    cross_qkv,
    cross_bias,
    cross_gain,
    cross_out,
    cross_norm_gain,
    cross_norm_bias,
    ffn_in,
    ffn_bias,
    ffn_out,
    out_bias,
    col_down,
    col_up,
    ffn1_down,
    ffn1_up,
    row_down,
    row_up,
    ffn2_down,
    ffn2_up,
    out_grad,
):
    groups = lax.axis_size("tensor")
    seq = lax.axis_size("seq")
    i, s = lax.axis_index("tensor"), lax.axis_index("seq")
    tl, d = tokens.shape[1:]
    tc = tl // groups
    ctx_len = context.shape[0]
    width = self_qkv.shape[2]
    hc = width // HEAD_DIM
    ff = ffn_in.shape[1]
    slots, rank = col_down.shape[0], col_down.shape[3]
    share = weight_share()
    slice_rows = width // (share * seq)
    plan, slot_list = weight_plan(slice_rows, 3)
    part_at = s * share + (lax.axis_index("dp") if share > 1 else 0)
    meta = jnp.stack([jnp.asarray(v, jnp.int32) for v in [i, s, adapter_index[0], part_at] + slot_list])
    tok, og = tokens[0], out_grad[0]
    block = pl.BlockSpec
    hbm = pl.BlockSpec(memory_space=pl.ANY)
    pair = flip(seq, 1)

    def table(array, *place, rows=1):
        if not place:
            return (array, block((1,) + array.shape[1:], lambda *a: (a[-1][ADAPTER],) + (0,) * (array.ndim - 1)))
        return (
            array,
            block(
                (1, rows) + array.shape[2:],
                lambda *a: (a[-1][ADAPTER], place[0](a[-1]) if callable(place[0]) else place[0], 0, 0),
            ),
        )

    col_dn, row_dn = jnp.swapaxes(col_down, 2, 3), jnp.swapaxes(row_down, 2, 3)
    feed_tables = [
        table(jnp.swapaxes(ffn1_down, 1, 2)),
        table(ffn1_up),
        table(jnp.swapaxes(ffn2_down, 1, 2)),
        table(ffn2_up),
    ]

    shard_at = lambda b, m: (m[PART], 0)
    (slices,) = run_kernel(
        pack_kernel,
        meta,
        [
            (self_out, block((slice_rows, d), shard_at)),
            (cross_qkv, block((1, slice_rows * groups, width), lambda b, m: (0, m[PART], 0))),
            (cross_out, block((slice_rows, d), shard_at)),
        ],
        [(sds((3 * slice_rows, d), BF16), whole((3 * slice_rows, d)))],
        us=1.5,
    )
    by_group = gather_direct(slices, "tensor")[1:]

    is_key = s == 0
    ctx_w = (cross_qkv, block((1, d, width), lambda b, m: (1 + m[AT_S], 0, 0)))
    ctx_up, ctx_dn = table(col_up, lambda m: 4 + m[AT_S]), table(col_dn, lambda m: 4 + m[AT_S])
    low_rows = ctx_len + 4 * rank
    ctx_pre, ctx_low, ctx_ssq, ctx_lat_t = run_kernel(
        functools.partial(context_kernel, groups),
        meta,
        [
            (context, whole(context.shape)),
            ctx_w,
            ctx_up,
            ctx_dn,
            (cross_bias, whole(cross_bias.shape)),
            (cross_gain, whole(cross_gain.shape)),
            table(col_up, 3),
            table(row_dn, 0, rows=2),
        ],
        [
            (sds((ctx_len, width), F32), whole((ctx_len, width))),
            (sds((low_rows, width), BF16), whole((low_rows, width))),
            (sds((8, tl), F32), whole((8, tl))),
            (sds((rank, ctx_len), BF16), whole((rank, ctx_len))),
        ],
        us=6,
        after=[slices],
    )
    cos, sin = rope_tables(positions[:, 0, :])
    rows_d = block((tc, d), lambda b, m: (b, 0))
    rows_w = block((tc, width), lambda b, m: (b, 0))
    rows_h = block((tc, HEAD_DIM), lambda b, m: (b, 0))
    lanes_8 = block((8, tc), lambda b, m: (0, b))
    self_tables = [table(col_up, 0, rows=3), table(col_dn, 0, rows=3)]
    y1, lat_t, pre_q, pre_k, raw_q, kv, ssq, vec = run_kernel(
        functools.partial(qkv_kernel, hc),
        meta,
        [
            (tok, rows_d),
            (modulation, whole(modulation.shape)),
            (time_emb[0], whole(modulation.shape)),
            (out_bias, whole(out_bias.shape)),
            (cross_norm_gain[None], whole((1, d))),
            (cross_norm_bias[None], whole((1, d))),
            (self_qkv, whole(self_qkv.shape)),
        ]
        + self_tables
        + [
            (self_bias, whole(self_bias.shape)),
            (self_gain, whole(self_gain.shape)),
            (cos, rows_h),
            (sin, rows_h),
            (ctx_ssq, lanes_8),
        ],
        [
            (sds((tl, d), BF16), rows_d),
            (sds((3 * rank, tl), BF16), block((3 * rank, tc), lambda b, m: (0, b))),
            (sds((tl, width), BF16), rows_w),
            (sds((tl, width), BF16), rows_w),
            (sds((tl, width), BF16), rows_w),
            (sds((tl, 2 * width), BF16), block((tc, 2 * width), lambda b, m: (b, 0))),
            (sds((8, tl), F32), lanes_8),
            (sds((16, d), F32), whole((16, d))),
        ],
        grid=(groups,),
        scratch=[pltpu.VMEM((3 * rank, 3 * width), BF16)],
        us=15,
    )
    kv_sib = send(kv, "seq", pair)
    *first_steps, last_step = powers(groups)
    for step in first_steps:
        ssq = ssq + send(ssq, "tensor", flip(groups, step))
    ssq, *by_group = seal(ssq, *by_group)
    (by_group,) = run_kernel(
        stack_kernel,
        meta,
        [(a, whole(a.shape)) for a in by_group],
        [(sds((groups - 1,) + slices.shape, BF16), whole((groups - 1,) + slices.shape))],
        us=2,
    )
    ssq, by_group = seal(ssq, by_group)
    along = [send(by_group, "dp", flip(share, 1)), send(by_group, "dp", flip(share, 2))] if share > 1 else []
    st_own = lax.rsqrt((ssq + send(ssq, "tensor", flip(groups, last_step))) / d + EPS)
    st_sib = send(st_own, "seq", pair)
    by_group_sib = send(by_group, "seq", pair)
    st_sib, by_group_sib, kv_sib = seal(st_sib, by_group_sib, kv_sib)
    ctx_low, _ = seal(ctx_low, st_own)
    ctx_pieces = gather_direct(ctx_low, "tensor")

    all_8 = whole((8, tl))
    turned = lambda r, m: lax.rem(m[AT_T] + r, groups)
    kv_at = lambda lane: block((tl, HEAD_DIM), lambda h, r, m: (0, lane + h))
    own_rows = block((tc, HEAD_DIM), lambda h, r, m: (0, h))
    *blocks, mixed, lses, kn, knt, vn, qn_self = run_kernel(
        functools.partial(attention_kernel, groups),
        meta,
        [
            (raw_q, block((tc, HEAD_DIM), lambda h, r, m: (turned(r, m), h))),
            (st_own, block((8, tc), lambda h, r, m: (0, turned(r, m)))),
            (st_own, all_8),
            (st_sib, all_8),
            (kv, kv_at(0)),
            (kv_sib, kv_at(0)),
            (kv, kv_at(hc)),
            (kv_sib, kv_at(hc)),
        ],
        [(sds((tc, width), BF16), own_rows)] * groups
        + [
            (sds((tl, width), BF16), block((tc, HEAD_DIM), lambda h, r, m: (r, h))),
            (sds((8 * hc, tl), F32), block((8, tc), lambda h, r, m: (h, r))),
            (sds((2 * tl, width), BF16), block((2 * tl, HEAD_DIM), lambda h, r, m: (0, h))),
            (sds((width, 2 * tl), BF16), block((HEAD_DIM, 2 * tl), lambda h, r, m: (h, 0))),
            (sds((2 * tl, width), BF16), block((2 * tl, HEAD_DIM), lambda h, r, m: (0, h))),
            (sds((tl, width), BF16), block((tc, HEAD_DIM), lambda h, r, m: (r, h))),
        ],
        grid=(hc, groups),
        scratch=[pltpu.VMEM((HEAD_DIM, 2 * tl), BF16)],
        us=25,
        after=[by_group],
    )
    tied = seal(*blocks, *along, *ctx_pieces[1:])
    blocks, along, ctx_pieces[1:] = tied[:groups], tied[groups : groups + len(along)], tied[groups + len(along) :]
    os_pieces = [send(a, "tensor", shift(groups, r)) if r else a for r, a in enumerate(blocks)]
    weight_parts = [by_group] + along
    if share > 1:
        middle = far_cut(by_group.shape[1])
        weight_parts += [
            send(along[1][:, :middle], "dp", flip(share, 1)),
            send(along[0][:, middle:], "dp", flip(share, 2)),
        ]
    tied = seal(*os_pieces[1:], *along, *ctx_pieces)
    os_pieces[1:], tied = tied[: groups - 1], tied[groups - 1 :]
    weight_parts[1 : 1 + len(along)], ctx_pieces = tied[: len(along)], tied[len(along) :]
    weight_parts = weight_parts + [by_group_sib] + [send(p, "seq", pair) for p in weight_parts[1:]]
    ctx_sib = [send(p, "seq", pair) for p in ctx_pieces]

    vspec = whole(vec.shape)
    own_block = block((tc, d), lambda b, m: (m[AT_T], 0))
    weight_scratch = [
        pltpu.VMEM((groups, width, d), BF16),
        pltpu.VMEM((groups - 1, d, width), BF16),
        pltpu.VMEM((groups, width, d), BF16),
    ]
    sems = pltpu.SemaphoreType.DMA((len(plan) * groups + 2,))
    shared = [
        table(row_up),
        table(col_dn, 3),
        *[(p, whole(p.shape)) for p in ctx_pieces + ctx_sib],
        (st_own, all_8),
        (st_sib, all_8),
        (self_out, hbm),
        (cross_qkv, block((1, d, width), lambda b, m: (0, 0, 0))),
        (cross_out, hbm),
    ] + [(p, hbm) for p in weight_parts]
    whole_of = lambda shape, dtype: (sds(shape, dtype), whole(shape))
    y2, x2, x1, y3, qn, qc, oc, os_all, lse_c, lats = run_kernel(
        functools.partial(cross_kernel, groups, hc, plan),
        meta,
        [(p, whole(p.shape)) for p in os_pieces] + [(tok, own_block), (vec, vspec)] + shared,
        [
            whole_of((tc, d), BF16),
            whole_of((tc, d), F32),
            whole_of((tc, d), F32),
            whole_of((tc, d), BF16),
            whole_of((tc, d), BF16),
            whole_of((tc, d), F32),
            whole_of((tc, d), BF16),
            whole_of((tc, d), BF16),
            whole_of((16, tc), F32),
            whole_of((3 * rank, tc), BF16),
        ],
        scratch=weight_scratch + [sems],
        us=20,
    )

    tiles = [(a, min(768, ff - a)) for a in range(0, ff, 768)]
    w1t = ffn_in.T
    y2_pieces = ring_pieces(y2, "tensor")
    feed_bias = ffn_bias.astype(F32)[None]
    feed_out, dys, acc = None, [], None
    for r in range(groups):
        place = block((tc, d), lambda b, m, r=r: (lax.rem(m[AT_T] + groups - r, groups), 0))
        ins = [(y2_pieces[r], whole((tc, d))), (og, place), (vec, vspec), (feed_bias, whole(feed_bias.shape))]
        ins += feed_tables + [(w1t, hbm), (ffn_out, hbm)]
        if r == 0:
            ins += [(x2, whole((tc, d)))]
        else:
            ins += [(a, whole(a.shape)) for a in acc] + [(feed_out, hbm)]
        feed_out, dy, *acc = run_kernel(
            functools.partial(feed_kernel, tiles, r == 0),
            meta,
            ins,
            [(sds((tl, d), BF16), place), whole_of((tc, d), F32 if r == 0 else BF16)]
            + [whole_of((rank, n), F32) for n in (ff, d, d, ff)],
            scratch=[pltpu.VMEM((ff, d), BF16), pltpu.VMEM((ff, d), BF16), pltpu.SemaphoreType.DMA((2, len(tiles)))],
            us=18,
            aliases={15: 0} if r else None,
        )
        dys.append(dy)
    g_up1, g_dn1, g_up2, g_dn2 = acc

    dy_own, dy_in = ring_total(dys, "tensor")
    feed_first = [feed_out[r * tc : (r + 1) * tc] for r in range(2)]
    feed_out, dy_in, *feed_first = seal(feed_out, dy_in, *feed_first)
    line = Line(meta, tc) if groups == 4 else None
    if line:
        for r in range(groups):
            line.add(*((feed_first[r], 0) if r < 2 else (feed_out, r)), "output", r)
        line.start()
    else:
        result = lax.psum(feed_out, "tensor")
    *dos, dx1, g_own, g_oth, g_rup, g_split, g_cqdn = run_kernel(
        functools.partial(cross_back_kernel, groups, hc, plan),
        meta,
        [(dy_own, whole((tc, d))), (dy_in, whole((tc, d))), (og, own_block)]
        + [(a, whole(a.shape)) for a in (x2, x1, y3, qn, qc, oc, os_all, lse_c, lats)]
        + [(vec, vspec)]
        + shared,
        [whole_of((tc, HEAD_DIM), BF16)] * groups
        + [whole_of((tc, width - HEAD_DIM), BF16)] * groups
        + [
            whole_of((tc, d), F32),
            whole_of((groups, ctx_len, width), BF16),
            whole_of((groups, ctx_len, width), BF16),
            whole_of((2 * rank, d), F32),
            whole_of((groups, 3 * rank, width), F32),
            whole_of((rank, d), F32),
        ],
        scratch=weight_scratch + [pltpu.VMEM((tc, d), F32), sems],
        us=26,
    )

    back_shift = lambda arrays: [send(a, "tensor", shift(groups, -r)) if r else a for r, a in enumerate(arrays)]
    moving = lambda: line.moving if line else []
    chains = Chains()
    dos[0], g_oth, g_cqdn, *arrived_line = seal(dos[0], g_oth, g_cqdn, *moving())
    dos_first = back_shift(dos[:groups])
    packed = jnp.concatenate([g_cqdn, g_dn1, g_rup[:rank], g_rup[rank:], g_up2, g_up1, g_dn2], axis=1)
    early_at = chains.add(adapter_steps(packed, 5 * d))
    g_oth = send(g_oth, "seq", pair)
    chains.step()
    g_oth, *dos_first = seal(g_oth, *dos_first)
    to_group = jnp.concatenate([g_own.astype(F32) + g_oth.astype(F32), g_split], axis=1)
    dos_rest = back_shift(dos[groups:])
    group_at = chains.add(ring_steps([to_group[r] for r in range(groups)], "tensor"))
    chains.step()

    back, dkv_in = [], []
    for h in range(hc):
        grads = dos_first if h == 0 else dos_rest
        lane = 0 if h == 0 else h - 1
        if h:
            if h == 1:
                tied = seal(*dos_rest, *chains.arrived(), back[-1][0], back[-1][2])
                dos_rest = tied[: len(dos_rest)]
                chains.put(tied[len(dos_rest) : -2])
                chains.step()
                if line:
                    line.advance(arrived_line)
            else:
                tied = seal(back[-1][0], back[-1][2])
            dkv_in.append(send(tied[-1], "seq", pair))
            grads = dos_rest
        back.append(
            run_kernel(
                functools.partial(attention_back_kernel, groups, h == 0),
                meta,
                [
                    (qn_self, block((tc, HEAD_DIM), lambda r, m, h=h: (r, h))),
                    (st_own, block((8, tc), lambda r, m: (0, turned(r, m)))),
                    (st_own, all_8),
                    (st_sib, all_8),
                    (kn, block((2 * tl, HEAD_DIM), lambda r, m, h=h: (0, h))),
                    (knt, block((HEAD_DIM, 2 * tl), lambda r, m, h=h: (h, 0))),
                    (vn, block((2 * tl, HEAD_DIM), lambda r, m, h=h: (0, h))),
                    (mixed, block((tc, HEAD_DIM), lambda r, m, h=h: (r, h))),
                    (lses, block((8, tc), lambda r, m, h=h: (h, r))),
                ]
                + [(g, block((tc, HEAD_DIM), lambda r, m, lane=lane: (0, lane))) for g in grads]
                + ([(a, all_8) for a in back[-1][3:]] if h else []),
                [
                    (sds((tl, HEAD_DIM), F32), block((tc, HEAD_DIM), lambda r, m: (turned(r, m), 0))),
                    whole_of((tl, 2 * HEAD_DIM), F32),
                    whole_of((tl, 2 * HEAD_DIM), BF16),
                    whole_of((8, tl), F32),
                    whole_of((8, tl), F32),
                ],
                grid=(groups,),
                scratch=[
                    pltpu.VMEM((2 * tl, HEAD_DIM), F32),
                    pltpu.VMEM((2 * tl, HEAD_DIM), F32),
                    pltpu.VMEM((tc, HEAD_DIM), BF16),
                ],
                us=12.5,
                after=list(tied[-2:-1]) if h else [],
            )
        )
    dq, dkv, dkv_out = zip(*[b[:3] for b in back])
    stat, cross = back[-1][3:]
    last_dkv = dkv_out[-1]
    stat, cross, last_dkv, *tied = seal(stat, cross, last_dkv, *chains.arrived(), *moving())
    count = len(chains.arrived())
    chains.put(tied[:count])
    arrived_line = tied[count:]
    dkv_in.append(send(last_dkv, "seq", pair))
    stat = stat + send(cross, "seq", pair)
    chains.step([group_at])
    for step in powers(groups):
        (other,) = seal(send(stat, "tensor", flip(groups, step)))
        stat = stat + other
    st_back = st_own * st_own * st_own * stat / d
    st_back, *tied = seal(st_back, *chains.arrived())
    chains.put(tied)
    chains.step()
    if line:
        line.advance(arrived_line)

    q_parts, late = [], None
    calls = 2
    for call in range(calls):
        steps = groups // calls
        in_d = block((tc, d), lambda b, m, c=call * steps: (c + b, 0))
        in_w = block((tc, width), lambda b, m, c=call * steps: (c + b, 0))
        in_h = block((tc, HEAD_DIM), lambda b, m, c=call * steps: (c + b, 0))
        in_2h = block((tc, 2 * HEAD_DIM), lambda b, m, c=call * steps: (c + b, 0))
        in_8 = block((8, tc), lambda b, m, c=call * steps: (0, c + b))
        size = (rank, 3 * (d + width))
        part, late = run_kernel(
            functools.partial(qkv_back_kernel, hc, call),
            meta,
            [(a, in_h) for a in dq]
            + [(a, in_2h) for a in list(dkv) + dkv_in]
            + [
                (pre_q, in_w),
                (pre_k, in_w),
                (st_own, in_8),
                (st_back, in_8),
                (self_gain, whole(self_gain.shape)),
                (cos, in_h),
                (sin, in_h),
                (self_qkv, hbm),
            ]
            + self_tables
            + [
                (tok, in_d),
                (vec, vspec),
                (y1, in_d),
                (lat_t, block((3 * rank, tc), lambda b, m, c=call * steps: (0, c + b))),
                (dx1, whole((tc, d))),
            ]
            + ([(late, whole(size))] if call else []),
            [(sds((steps * tc, d), BF16), block((tc, d), lambda b, m: (b, 0))), whole_of(size, F32)],
            grid=(steps,),
            scratch=[
                pltpu.VMEM((3 * rank, 3 * width), BF16),
                pltpu.VMEM(self_qkv.shape, BF16),
                pltpu.SemaphoreType.DMA(()),
            ],
            us=14,
        )
        q_parts.append(part)
        if line:
            for r in range(steps):
                line.add(part, r, "input_grad", call * steps + r)
        late, *tied = seal(late, *chains.arrived(), *moving())
        count = len(chains.arrived())
        chains.put(tied[:count])
        chains.step()
        if call == 0:
            to_group = chains.result(group_at)
            g_ctx, split = to_group[:ctx_len], to_group[ctx_len:]
            ctx_gain = jnp.where(is_key, cross_gain[1:2].astype(F32), 1.0)
            ctx_stat = jnp.sum(g_ctx * ctx_gain * ctx_pre, axis=1)
            stat_at = chains.add(total_steps(ctx_stat, "tensor"))
            chains.advance(stat_at)
        if line:
            line.advance(tied[count:])
    while not chains.done(stat_at):
        chains.put(seal(*chains.arrived()))
        chains.step()
    ctx_stat = chains.result(stat_at)

    ctx_inverse = jnp.concatenate([st_own[2, j * tc : j * tc + ctx_len // groups] for j in range(groups)])
    ctx_cubed = ctx_inverse * ctx_inverse * ctx_inverse * ctx_stat / d
    d_key = ctx_inverse[:, None] * ctx_gain * g_ctx - ctx_pre * ctx_cubed[:, None]
    d_ctx = jnp.where(is_key, d_key, g_ctx).astype(BF16)
    ctx_part, g_ctx_up, g_ctx_dn = run_kernel(
        context_back_kernel,
        meta,
        [
            (context, whole(context.shape)),
            ctx_w,
            ctx_up,
            ctx_dn,
            (ctx_lat_t, whole(ctx_lat_t.shape)),
            (d_ctx, whole(d_ctx.shape)),
        ],
        [whole_of((ctx_len, d), F32), whole_of((rank, width), F32), whole_of((rank, d), F32)],
        us=6,
        after=[line.acc[max(line.acc)]] if line else [],
    )

    pick = lambda g: [jnp.where(is_key, g, 0.0), jnp.where(is_key, 0.0, g)]
    late = jnp.concatenate(
        [late[:, : 3 * d]]
        + pick(g_ctx_dn)
        + [late[:, 3 * d :], split[:rank]]
        + pick(g_ctx_up)
        + [split[rank : 2 * rank], split[2 * rank :]]
        + [jnp.broadcast_to(adapter_index[0].astype(F32) / seq, (rank, HEAD_DIM))],
        axis=1,
    )
    ctx_at = chains.add(context_grad_steps(ctx_part))
    late_at = chains.add(adapter_steps(late, 5 * d))
    chains.advance(ctx_at)
    chains.advance(late_at)
    while line and line.at < len(line.parts):
        tied = seal(*chains.arrived(), *moving())
        count = len(chains.arrived())
        chains.put(tied[:count])
        chains.step()
        line.advance(tied[count:])
    while line and line.live():
        line.advance(line.moving)
    while chains.live():
        chains.put(seal(*chains.arrived()))
        chains.step()
    early, late, context_grad = chains.result(early_at), chains.result(late_at), chains.result(ctx_at).astype(F32)
    if line:
        result, input_grad = line.outs["output"], line.outs["input_grad"]
    else:
        input_grad = lax.psum(jnp.concatenate(q_parts), "tensor")

    indices = jnp.round(late[:, 0, -1].astype(F32)).astype(jnp.int32)
    early, late = spread(early, indices, slots), spread(late[:, :, :-HEAD_DIM], indices, slots)
    cut = lambda grads, start, size, count: [
        grads[:, :, start + j * size : start + (j + 1) * size] for j in range(count)
    ]
    wide, feed = cut(early, 0, d, 5), cut(early, 5 * d, ff, 2)
    wide_late, narrow = cut(late, 0, d, 5), cut(late, 5 * d, width, 8)
    swap = lambda a: jnp.swapaxes(a, -1, -2)
    return (
        result[None],
        input_grad[None],
        context_grad,
        swap(jnp.stack(wide_late[:3] + wide[:1] + wide_late[3:], axis=1)),
        jnp.stack(narrow[:6], axis=1),
        swap(wide[1]),
        feed[0],
        swap(jnp.stack(narrow[6:], axis=1)),
        jnp.stack(wide[2:4], axis=1),
        swap(feed[1]),
        wide[4],
    )


def solution(mesh):
    placed = (
        P("dp", "seq", None),
        P(None, "dp", "seq"),
        P("dp", None, None),
        P(),
        P(),
        P("dp"),
        P(None, None, "tensor"),
        P(None, "tensor"),
        P(None, "tensor"),
        P("tensor", None),
        P(None, None, "tensor"),
        P(None, "tensor"),
        P(None, "tensor"),
        P("tensor", None),
        P(),
        P(),
        P(None, "tensor"),
        P("tensor"),
        P("tensor", None),
        P(),
        P(),
        P(None, None, None, "tensor"),
        P(),
        P(None, None, "tensor"),
        P(None, None, "tensor", None),
        P(),
        P(None, "tensor", None),
        P(),
        P("dp", "seq", None),
    )
    return jax.shard_map(
        per_device,
        mesh=mesh,
        in_specs=placed,
        out_specs=(
            P("dp", "seq", None),
            P("dp", "seq", None),
            P(),
            P(),
            P(None, None, None, "tensor"),
            P(),
            P(None, None, "tensor"),
            P(None, None, "tensor", None),
            P(),
            P(None, "tensor", None),
            P(),
        ),
        check_vma=False,
    )
```

```python
import functools
import math

import jax
import jax.numpy as jnp
import numpy as np
from jax import lax
from jax.experimental import pallas as pl
from jax.experimental.pallas import tpu as pltpu
from jax.sharding import PartitionSpec as P

F32 = jnp.float32
BF16 = jnp.bfloat16
HEAD_DIM = 128
EPS = 1e-06
LOG2E = 1.4426950408889634
SCALE = HEAD_DIM ** (-0.5)
VMEM_LIMIT = 58 * 1024 * 1024
GELU_C = math.sqrt(2.0 / math.pi)
M0, M1, M2, M3, M4, M5, B0, B1, B2, CG, CB = range(11)
AT_T, AT_S, ADAPTER, PART, SLOTS = range(5)


def nn(left, right):
    return jnp.dot(left, right, preferred_element_type=F32)


def nt(left, right):
    return lax.dot_general(left, right, (((1,), (1,)), ((), ())), preferred_element_type=F32)


def both_ways(values):
    return values.astype(BF16), values.T.astype(BF16)


def row_total(values):
    ones = jnp.ones((8, values.shape[1]), BF16)
    high = values.astype(BF16)
    return nt(ones, high) + nt(ones, (values - high.astype(F32)).astype(BF16))


def mean(values):
    return jnp.mean(values, axis=-1, keepdims=True)


def normalize(values):
    centered = values - mean(values)
    inverse = lax.rsqrt(mean(centered * centered) + EPS)
    return centered * inverse, inverse


def normalize_back(normed, inverse, upstream):
    return inverse * (upstream - mean(upstream) - normed * mean(upstream * normed))


def pair_swap(values):
    width = values.shape[1]
    lane = lax.broadcasted_iota(jnp.int32, values.shape, 1)
    return jnp.where(lane % 2 == 0, pltpu.roll(values, width - 1, 1), pltpu.roll(values, 1, 1))


def rope(values, cosine, sine):
    return values * cosine + pair_swap(values) * sine


def rope_back(values, cosine, sine):
    return values * cosine - pair_swap(values) * sine


def heads_of(array, count):
    return [array[:, h * HEAD_DIM : (h + 1) * HEAD_DIM] for h in range(count)]


def whole(shape):
    return pl.BlockSpec(shape, lambda *_: (0,) * len(shape))


def run_kernel(body, meta, ins, outs, grid=(1,), scratch=(), us=1.0, aliases=None, after=()):
    count = len(ins)
    ins = list(ins) + [(a, pl.BlockSpec(memory_space=pl.ANY)) for a in after]
    arrays = [a for a, _ in ins]
    moved = sum(math.prod(a.shape) * a.dtype.itemsize for a in arrays[:count]) + sum(
        math.prod(s.shape) * s.dtype.itemsize for s, _ in outs
    )

    def reading(meta_ref, *refs):
        return body(meta_ref, *refs[:count], *refs[len(arrays) :])

    return pl.pallas_call(
        reading,
        grid_spec=pltpu.PrefetchScalarGridSpec(
            num_scalar_prefetch=1,
            grid=grid,
            in_specs=[s for _, s in ins],
            out_specs=[s for _, s in outs],
            scratch_shapes=list(scratch),
        ),
        out_shape=[s for s, _ in outs],
        input_output_aliases=aliases or {},
        compiler_params=pltpu.CompilerParams(vmem_limit_bytes=VMEM_LIMIT),
        cost_estimate=pl.CostEstimate(
            flops=int(us * 1.15e9), bytes_accessed=int(min(moved, us * 2e6)), transcendentals=0
        ),
    )(meta, *arrays)


def sds(shape, dtype):
    return jax.ShapeDtypeStruct(shape, dtype)


def qkv_kernel(head_count, meta, tok, mod, emb, b_out, cg, cb, w, up, dn, bias, gain, cos, sin, ctx_ssq, *outs):
    y1, lat_t, pre_q, pre_k, raw_q, kv, ssq, vec, up_s = outs
    width = head_count * HEAD_DIM
    rank = up.shape[2]
    modes = mod[...] + emb[...]

    @pl.when(pl.program_id(0) == 0)
    def _():
        row = lax.broadcasted_iota(jnp.int32, modes.shape, 0)
        rows = [modes + jnp.where((row == 1) | (row == 4), 1.0, 0.0), b_out[...].astype(F32), cg[...], cb[...]]
        vec[...] = jnp.concatenate(rows + [jnp.zeros((5, modes.shape[1]), F32)], axis=0)
        up_s[...] = jnp.zeros_like(up_s)
        for j in range(3):
            up_s[j * rank : (j + 1) * rank, j * width : (j + 1) * width] = up[0, j]

    normed, _ = normalize(tok[...].astype(F32))
    y = (normed * (1.0 + modes[1:2, :]) + modes[0:1, :]).astype(BF16)
    y1[...] = y
    down = jnp.concatenate([dn[0, j] for j in range(3)], axis=0)
    lat = nt(y, down).astype(BF16)
    lat_t[...] = nt(down, y).astype(BF16)
    totals = []
    for j in range(3):
        lanes = slice(j * width, (j + 1) * width)
        u = nn(y, w[j]) + nn(lat, up_s[:, lanes]) + bias[j : j + 1, :].astype(F32)
        if j == 2:
            kv[:, width:] = u.astype(BF16)
            continue
        (pre_q, pre_k)[j][...] = u.astype(BF16)
        totals.append(row_total(u * u))
        scaled = u * gain[j : j + 1, :].astype(F32)
        for h in range(head_count):
            lanes = slice(h * HEAD_DIM, (h + 1) * HEAD_DIM)
            (raw_q, kv)[j][:, lanes] = rope(scaled[:, lanes], cos[...], sin[...]).astype(BF16)
    row = lax.broadcasted_iota(jnp.int32, totals[0].shape, 0)
    ssq[...] = jnp.where(row == 0, totals[0], jnp.where(row == 1, totals[1], ctx_ssq[...]))


def attention_kernel(groups, meta, raw_q, st, st_own, st_sib, k_own, k_sib, v_own, v_sib, *outs):
    blocks, (out, lse, kn, knt, vn, qn, vt) = outs[:groups], outs[groups:]
    count = k_own.shape[0]
    step = pl.program_id(1)

    @pl.when(step == 0)
    def _():
        for at, (k, s, v) in enumerate(((k_own, st_own, v_own), (k_sib, st_sib, v_sib))):
            rows = slice(at * count, (at + 1) * count)
            scaled = k[...].astype(F32) * s[...].T[:, 1:2]
            kn[rows, :] = scaled.astype(BF16)
            knt[:, rows] = scaled.T.astype(BF16)
            vn[rows, :] = v[...]
            vt[:, rows] = v[...].astype(F32).T.astype(BF16)

    q = (raw_q[...].astype(F32) * (st[...].T[:, 0:1] * (SCALE * LOG2E))).astype(BF16)
    qn[...] = q
    scores = nt(kn[...], q)
    highest = jnp.max(scores, axis=0, keepdims=True)
    e = jnp.exp2(scores - highest)
    total = jnp.sum(e, axis=0, keepdims=True)
    mixed = (nn(vt[...], e.astype(BF16)) / total).T.astype(BF16)
    out[...] = mixed
    for r in range(groups):

        @pl.when(step == r)
        def _(r=r):
            blocks[r][...] = mixed

    lse[...] = jnp.broadcast_to(highest + jnp.log2(total), lse.shape)


def attention_back_kernel(groups, first, meta, qn, st, st_own, st_sib, kn, knt, vn, out, lse, *rest):
    grads, rest = rest[:groups], rest[groups:]
    if not first:
        stat_in, cross_in = rest[:2]
        rest = rest[2:]
    dq, dkv_own, dkv_sib, stat, cross, dk_acc, dv_acc, g_s = rest
    count = kn.shape[0] // 2
    size = qn.shape[0]
    step = pl.program_id(0)

    @pl.when(step == 0)
    def _():
        dk_acc[...] = jnp.zeros_like(dk_acc)
        dv_acc[...] = jnp.zeros_like(dv_acc)
        stat[...] = jnp.zeros_like(stat) if first else stat_in[...]
        cross[...] = jnp.zeros_like(cross) if first else cross_in[...]

    for r in range(groups):

        @pl.when(step == r)
        def _(r=r):
            g_s[...] = grads[r][...]

    q = qn[...]
    g = g_s[...]
    delta = row_total(g.astype(F32) * out[...].astype(F32))[0:1, :]
    p = jnp.exp2(nt(kn[...], q) - lse[0:1, :])
    dv_acc[...] += nn(p.astype(BF16), g)
    ds = (p * (nt(vn[...], g) - delta)).astype(BF16)
    dk_acc[...] += nn(ds, q)
    dqs = nn(knt[...], ds).T * SCALE
    dq[...] = dqs
    lanes = pl.ds(pl.multiple_of(lax.rem(meta[AT_T] + step, groups) * size, size), size)
    total = row_total(dqs * q.astype(F32)) / (st[0:1, :] * (SCALE * LOG2E))
    stat[:, lanes] += jnp.where(lax.broadcasted_iota(jnp.int32, total.shape, 0) == 0, total, 0.0)

    @pl.when(step == pl.num_programs(0) - 1)
    def _():
        for at, (s, dkv, sums) in enumerate(((st_own, dkv_own, stat), (st_sib, dkv_sib, cross))):
            rows = slice(at * count, (at + 1) * count)
            dk = dk_acc[rows, :] * (1.0 / LOG2E)
            dkv[:, :HEAD_DIM] = dk.astype(dkv.dtype)
            dkv[:, HEAD_DIM:] = dv_acc[rows, :].astype(dkv.dtype)
            all_k = row_total(dk * kn[rows, :].astype(F32)) / s[1:2, :]
            sums[...] += jnp.where(lax.broadcasted_iota(jnp.int32, all_k.shape, 0) == 1, all_k, 0.0)


def qkv_back_kernel(head_count, call, meta, *refs):
    n = head_count
    dq, dkv, dkv_in = (refs[j * n : (j + 1) * n] for j in range(3))
    refs = refs[3 * n :]
    pre_q, pre_k, st, st_back, gain_in, cos, sin, w, up_in, dn_in, tok, vec, y1, lat_t, dx1 = refs[:15]
    packed_in = refs[15] if call else None
    part, packed, up, w_s, sem = refs[-5:]
    step = pl.program_id(0)
    fetch = pltpu.make_async_copy(w, w_s, sem)

    @pl.when(step == 0)
    def _():
        fetch.start()
        packed[...] = packed_in[...] if call else jnp.zeros_like(packed)

    inverse, cubed = st[...].T, st_back[...].T
    c, s = cos[...], sin[...]
    width = n * HEAD_DIM
    rank = up_in.shape[2]
    d = tok.shape[1]
    gain = gain_in[...].astype(F32)
    up[...] = jnp.zeros_like(up)
    for j in range(3):
        up[j * rank : (j + 1) * rank, j * width : (j + 1) * width] = up_in[0, j]
    dn = jnp.concatenate([dn_in[0, j] for j in range(3)], axis=0)
    dk = [a[:, :HEAD_DIM] + b[:, :HEAD_DIM].astype(F32) for a, b in zip(dkv, dkv_in)]
    dv = [a[:, HEAD_DIM:] + b[:, HEAD_DIM:].astype(F32) for a, b in zip(dkv, dkv_in)]
    grads = [
        jnp.concatenate([rope_back(ref[...], c, s) for ref in dq], axis=1),
        jnp.concatenate([rope_back(a, c, s) for a in dk], axis=1),
        jnp.concatenate(dv, axis=1).astype(BF16),
    ]
    for j, pre in enumerate((pre_q, pre_k)):
        grads[j] = (
            inverse[:, j : j + 1] * gain[j : j + 1, :] * grads[j] - pre[...].astype(F32) * cubed[:, j : j + 1]
        ).astype(BF16)
    joined = jnp.concatenate(grads, axis=1)
    d_lat = nt(joined, up[...]).astype(BF16)
    d_lat_t = nt(up[...], joined).astype(BF16)
    total = nn(d_lat, dn)

    @pl.when(step == 0)
    def _():
        fetch.wait()

    for j in range(3):
        total = total + nt(grads[j], w_s[j])
    normed, inverse = normalize(tok[...].astype(F32))
    back = normalize_back(normed, inverse, total * vec[M1 : M1 + 1, :])
    own = (meta[AT_T] == call * pl.num_programs(0) + step).astype(F32)
    part[...] = (back + dx1[...] * own).astype(part.dtype)
    g_dn = nn(d_lat_t, y1[...])
    for j in range(3):
        rows = slice(j * rank, (j + 1) * rank)
        g_up = nn(lat_t[rows, :], grads[j])
        for start, g in ((j * d, g_dn[rows, :]), (3 * d + j * width, g_up)):
            lanes = slice(start, start + g.shape[1])
            packed[:, lanes] += g


def context_kernel(groups, meta, ctx, w, up, dn, bias, gain, up_q, down_row, pre, low, ssq, lat_t):
    key = meta[AT_S] == 0
    c = ctx[...]
    count = c.shape[0]
    rank, width = up.shape[2:]
    lat = nt(c, dn[0, 0]).astype(BF16)
    lat_t[...] = nt(dn[0, 0], c).astype(BF16)
    b, g = bias[...].astype(F32), gain[...].astype(F32)
    u = nn(c, w[0]) + nn(lat, up[0, 0]) + jnp.where(key, b[1:2, :], b[2:3, :])
    pre[...] = u
    low[:count, :] = (u * jnp.where(key, g[1:2, :], 1.0)).astype(BF16)
    low[count : count + rank, :] = up_q[0, 0]
    low[count + rank : count + 2 * rank, :] = down_row[0, 0]
    low[count + 2 * rank : count + 3 * rank, :] = down_row[0, 1]
    row = lax.broadcasted_iota(jnp.int32, (rank, width), 0)
    low[count + 3 * rank :, :] = jnp.where(row == 0, b[0:1, :], jnp.where(row == 1, g[0:1, :], 0.0)).astype(BF16)
    total = row_total(u * u)
    share, block = count // groups, ssq.shape[1] // groups
    ssq[...] = jnp.zeros_like(ssq)
    for j in range(groups):
        ssq[:, j * block : j * block + share] = total[:, j * share : (j + 1) * share]


def context_row(groups, count, rows):
    share, block = count // groups, rows.shape[1] // groups
    return jnp.concatenate([rows[2:3, j * block : j * block + share] for j in range(groups)], axis=1)


def context_back_kernel(meta, ctx, w, up_in, dn_in, lat_t, grad, out, g_up, g_dn):
    g = grad[...]
    up, dn = up_in[0, 0], dn_in[0, 0]
    d_lat = nt(g, up).astype(BF16)
    d_lat_t = nt(up, g).astype(BF16)
    out[...] = nt(g, w[0]) + nn(d_lat, dn)
    g_up[...] = nn(lat_t[...], g)
    g_dn[...] = nn(d_lat_t, ctx[...])


def pack_kernel(meta, wo, wq, wc, out):
    rows, width = wo.shape[0], wq.shape[2]
    out[:rows, :] = wo[...]
    for j in range(out.shape[1] // width):
        out[rows : 2 * rows, j * width : (j + 1) * width] = wq[0, j * rows : (j + 1) * rows, :]
    out[2 * rows :, :] = wc[...]


def stack_kernel(meta, *refs):
    for j, ref in enumerate(refs[:-1]):
        refs[-1][j] = ref[...]


def start_copies(meta, plan, refs, targets, sems, own):
    copies = [[] for _ in targets]
    at = 0
    for source, weight, first, rows, slot, inner, size in plan:
        target = targets[weight]
        width = target.shape[2]
        sides = refs[source].shape[2] // width
        for j in range(sides):
            start = pl.multiple_of(meta[slot] * (size * sides) + (j * size + inner), 16)
            copies[weight].append(
                pltpu.make_async_copy(
                    refs[source].at[:, pl.ds(first, rows), pl.ds(j * width, width)],
                    target.at[pl.ds(target.shape[0] - refs[source].shape[0], refs[source].shape[0]), pl.ds(start, rows), :],
                    sems.at[at],
                )
            )
            at += 1
    for weight, shard in own.items():
        copies[weight].append(pltpu.make_async_copy(shard, targets[weight].at[0], sems.at[at]))
        at += 1
    for weight in copies:
        for copy in weight:
            copy.start()
    return copies


def finish(copies):
    for copy in copies:
        copy.wait()


def cross_kernel(groups, head_count, plan, meta, *refs):
    n = groups * head_count
    os_in, refs = refs[:groups], refs[groups:]
    tok, vec, up, dn3 = refs[:4]
    ctx_own, ctx_sib, refs = refs[4 : 4 + groups], refs[4 + groups : 4 + 2 * groups], refs[4 + 2 * groups :]
    st_own, st_sib, wo_own, wq_own, wc_own = refs[:5]
    k = 1 + max(entry[0] for entry in plan)
    sources, refs = refs[5 : 5 + k], refs[5 + k :]
    y2, x2, x1, y3, qn, qc, oc, os_all, lse, lats = refs[:10]
    wo, wq, wc, sems = refs[10:]
    copies = start_copies(meta, plan, sources, (wo, wq, wc), sems, {0: wo_own, 2: wc_own})
    full = lambda weight: weight[...].reshape(weight.shape[0] * weight.shape[1], weight.shape[2])
    dn3 = dn3[0, 0]
    rank = dn3.shape[0]
    ctx_len = ctx_own[0].shape[0] - 4 * rank
    small = jnp.concatenate([ctx_own[r][ctx_len:, :] for r in range(groups)], axis=1)
    first = meta[AT_S] == 0
    key_row = context_row(groups, ctx_len, jnp.where(first, st_own[...], st_sib[...]))
    ctx_inverse = jnp.broadcast_to(key_row, (8, ctx_len)).T[:, 0:1]
    width = head_count * HEAD_DIM
    for r in range(groups):
        os_all[:, r * width : (r + 1) * width] = os_in[r][...]
    os_v = os_all[...]
    down0, down1 = small[rank : 2 * rank, :], small[2 * rank : 3 * rank, :]
    lat = nt(os_v, down0).astype(BF16)
    lats[0:rank, :] = nt(down0, os_v).astype(BF16)
    total = nn(lat, up[0, 0])
    finish(copies[0])
    total = total + nn(os_v, full(wo))
    x1_v = tok[...].astype(F32) + (total + vec[B0 : B0 + 1, :]) * vec[M2 : M2 + 1, :]
    x1[...] = x1_v
    normed, _ = normalize(x1_v)
    y3_v = (normed * vec[CG : CG + 1, :] + vec[CB : CB + 1, :]).astype(BF16)
    y3[...] = y3_v
    lat = nt(y3_v, dn3).astype(BF16)
    lats[2 * rank : 3 * rank, :] = nt(dn3, y3_v).astype(BF16)
    finish(copies[1])
    q = nn(lat, small[0:rank, :]) + small[3 * rank : 3 * rank + 1, :].astype(F32)
    q = q + jnp.concatenate([nn(y3_v, wq[r - 1] if r else wq_own[0]) for r in range(groups)], axis=1)
    qc[...] = q
    inverse = lax.rsqrt(mean(q * q) + EPS)
    gain = small[3 * rank + 1 : 3 * rank + 2, :].astype(F32)
    qn[...] = (q * (inverse * (SCALE * LOG2E)) * gain).astype(BF16)
    for j in range(n):
        r, lanes = j // head_count, slice((j % head_count) * HEAD_DIM, (j % head_count + 1) * HEAD_DIM)
        a, b = ctx_own[r][:ctx_len, lanes], ctx_sib[r][:ctx_len, lanes]
        keys, values = jnp.where(first, a, b), jnp.where(first, b, a)
        keys = (keys.astype(F32) * ctx_inverse).astype(BF16)
        scores = nt(keys, qn[:, j * HEAD_DIM : (j + 1) * HEAD_DIM])
        highest = jnp.max(scores, axis=0, keepdims=True)
        e = jnp.exp2(scores - highest)
        sums = jnp.sum(e, axis=0, keepdims=True)
        mixed = nn(values.astype(F32).T.astype(BF16), e.astype(BF16)) / sums
        oc[:, j * HEAD_DIM : (j + 1) * HEAD_DIM] = mixed.T.astype(BF16)
        lse[j : j + 1, :] = highest + jnp.log2(sums)
    oc_v = oc[...]
    lat = nt(oc_v, down1).astype(BF16)
    lats[rank : 2 * rank, :] = nt(down1, oc_v).astype(BF16)
    total = nn(lat, up[0, 1])
    finish(copies[2])
    total = total + nn(oc_v, full(wc))
    x2_v = x1_v + total + vec[B1 : B1 + 1, :]
    x2[...] = x2_v
    normed, _ = normalize(x2_v)
    y2[...] = (normed * vec[M4 : M4 + 1, :] + vec[M3 : M3 + 1, :]).astype(BF16)


def cross_back_kernel(groups, head_count, plan, meta, *refs):
    n = groups * head_count
    dy_own, dy_in, og, x2, x1, y3, qn, qc, oc, os_all, lse, lats, vec, up, dn3 = refs[:15]
    ctx_own, ctx_sib, refs = refs[15 : 15 + groups], refs[15 + groups : 15 + 2 * groups], refs[15 + 2 * groups :]
    st_own, st_sib, wo_own, wq_own, wc_own = refs[:5]
    k = 1 + max(entry[0] for entry in plan)
    sources, refs = refs[5 : 5 + k], refs[5 + k :]
    dos_first, dos_rest, refs = refs[:groups], refs[groups : 2 * groups], refs[2 * groups :]
    dx1, g_own, g_oth, g_up, g_split, g_dn, wo, wq, wc, dq_s, sems = refs
    copies = start_copies(meta, plan, sources, (wo, wq, wc), sems, {0: wo_own, 2: wc_own})
    full = lambda weight: weight[...].reshape(weight.shape[0] * weight.shape[1], weight.shape[2])
    dn3 = dn3[0, 0]
    rank = dn3.shape[0]
    ctx_len = ctx_own[0].shape[0] - 4 * rank
    small = jnp.concatenate([ctx_own[r][ctx_len:, :] for r in range(groups)], axis=1)
    first = meta[AT_S] == 0
    key_row = context_row(groups, ctx_len, jnp.where(first, st_own[...], st_sib[...]))
    ctx_inverse = jnp.broadcast_to(key_row, (8, ctx_len)).T[:, 0:1]
    width = head_count * HEAD_DIM
    down0, down1 = small[rank : 2 * rank, :], small[2 * rank : 3 * rank, :]
    normed, inverse = normalize(x2[...])
    dn = (dy_own[...] + dy_in[...].astype(F32)) * vec[M4 : M4 + 1, :]
    dx2 = og[...].astype(F32) + normalize_back(normed, inverse, dn)
    grad = dx2.astype(BF16)
    d_lat = nt(grad, up[0, 1]).astype(BF16)
    d_lat_t = nt(up[0, 1], grad).astype(BF16)
    oc_v = oc[...]
    g_up[rank : 2 * rank, :] = nn(lats[rank : 2 * rank, :], grad)
    split = nn(d_lat_t, oc_v)
    for r in range(groups):
        g_split[r, 2 * rank : 3 * rank, :] = split[:, r * width : (r + 1) * width]
    finish(copies[2])
    d_oc = nn(d_lat, down1) + nt(grad, full(wc))
    d_oc = d_oc.astype(BF16)
    for j in range(n):
        r, lanes = j // head_count, slice((j % head_count) * HEAD_DIM, (j % head_count + 1) * HEAD_DIM)
        head = slice(j * HEAD_DIM, (j + 1) * HEAD_DIM)
        a, b = ctx_own[r][:ctx_len, lanes], ctx_sib[r][:ctx_len, lanes]
        keys, values = jnp.where(first, a, b), jnp.where(first, b, a)
        keys = (keys.astype(F32) * ctx_inverse).astype(BF16)
        q, g = qn[:, head], d_oc[:, head]
        delta = row_total(g.astype(F32) * oc_v[:, head].astype(F32))[0:1, :]
        p = jnp.exp2(nt(keys, q) - lse[j : j + 1, :])
        dv = nn(p.astype(BF16), g)
        ds = (p * (nt(values, g) - delta)).astype(BF16)
        dk = nn(ds, q) * (1.0 / LOG2E)
        dq_s[:, head] = nn(keys.astype(F32).T.astype(BF16), ds).T * SCALE
        g_own[r, :, lanes] = jnp.where(first, dk, dv).astype(BF16)
        g_oth[r, :, lanes] = jnp.where(first, dv, dk).astype(BF16)
    q = qc[...]
    inverse = lax.rsqrt(mean(q * q) + EPS)
    gain = small[3 * rank + 1 : 3 * rank + 2, :].astype(F32)
    scaled = dq_s[...] * gain
    stat = mean(scaled * q)
    dqc = (inverse * scaled - q * (inverse * inverse * inverse * stat)).astype(BF16)
    up_q = small[0:rank, :]
    d_lat = nt(dqc, up_q).astype(BF16)
    d_lat_t = nt(up_q, dqc).astype(BF16)
    split = nn(lats[2 * rank : 3 * rank, :], dqc)
    for r in range(groups):
        g_split[r, 0:rank, :] = split[:, r * width : (r + 1) * width]
    g_dn[...] = nn(d_lat_t, y3[...])
    dy3 = nn(d_lat, dn3)
    finish(copies[1])
    for r in range(groups):
        part = dqc[:, r * width : (r + 1) * width]
        dy3 = dy3 + nt(part, wq[r - 1] if r else wq_own[0])
    normed, inverse = normalize(x1[...])
    dx1_v = dx2 + normalize_back(normed, inverse, dy3 * vec[CG : CG + 1, :])
    dx1[...] = dx1_v
    grad = (dx1_v * vec[M2 : M2 + 1, :]).astype(BF16)
    d_lat = nt(grad, up[0, 0]).astype(BF16)
    d_lat_t = nt(up[0, 0], grad).astype(BF16)
    g_up[0:rank, :] = nn(lats[0:rank, :], grad)
    split = nn(d_lat_t, os_all[...])
    for r in range(groups):
        g_split[r, rank : 2 * rank, :] = split[:, r * width : (r + 1) * width]
    finish(copies[0])
    d_os = nn(d_lat, down0) + nt(grad, full(wo))
    for r in range(groups):
        block = d_os[:, r * width : (r + 1) * width]
        dos_first[r][...] = block[:, :HEAD_DIM].astype(BF16)
        dos_rest[r][...] = block[:, HEAD_DIM:].astype(BF16)


def feed_kernel(tiles, first, meta, *refs):
    y2, og, vec, bias, dn1, up1, dn2, up2, w1_h, w2_h = refs[:10]
    if first:
        x2 = refs[10]
    else:
        acc = refs[10:14]
    refs = refs[11:] if first else refs[15:]
    dn1, up1, dn2, up2 = dn1.at[0], up1.at[0], dn2.at[0], up2.at[0]
    out, dy, g_up1, g_dn1, g_up2, g_dn2, w1, w2, sems = refs
    copies = []
    for at, (start, size) in enumerate(tiles):
        rows = pl.ds(start, size)
        pair = [
            pltpu.make_async_copy(h.at[rows, :], v.at[rows, :], sems.at[j, at])
            for j, (h, v) in enumerate(((w1_h, w1), (w2_h, w2)))
        ]
        for copy in pair:
            copy.start()
        copies.append(pair)
    y = y2[...]
    dff = (og[...].astype(F32) * vec[M5 : M5 + 1, :]).astype(BF16)
    lat, lat_t = both_ways(nt(y, dn1[...]))
    drl, drl_t = both_ways(nt(dff, up2[...]))
    part = grad = rl = d_lat = 0.0
    for (start, size), pair in zip(tiles, copies):
        cols = slice(start, start + size)
        finish(pair)
        h = nt(y, w1[cols, :]) + nn(lat, up1[:, cols]) + bias[:, cols]
        du = nt(dff, w2[cols, :]) + nn(drl, dn2[:, cols])
        sq = h * h
        t = jnp.tanh(GELU_C * h * (1.0 + 0.044715 * sq))
        act = (0.5 * h * (1.0 + t)).astype(BF16)
        slope = 0.5 * (1.0 + t) + (0.5 * GELU_C) * h * (1.0 - t * t) * (1.0 + (3.0 * 0.044715) * sq)
        dh = (du * slope).astype(BF16)
        part = part + nn(act, w2[cols, :])
        grad = grad + nn(dh, w1[cols, :])
        rl = rl + nt(act, dn2[:, cols])
        d_lat = d_lat + nt(dh, up1[:, cols])
        new_up1, new_dn2 = nn(lat_t, dh), nn(drl_t, act)
        g_up1[:, cols] = new_up1 if first else new_up1 + acc[0][:, cols]
        g_dn2[:, cols] = new_dn2 if first else new_dn2 + acc[3][:, cols]
    rl, rl_t = both_ways(rl)
    d_lat, d_lat_t = both_ways(d_lat)
    part = part + nn(rl, up2[...])
    grad = grad + nn(d_lat, dn1[...])
    new_dn1, new_up2 = nn(d_lat_t, y), nn(rl_t, dff)
    g_dn1[...] = new_dn1 if first else new_dn1 + acc[1][...]
    g_up2[...] = new_up2 if first else new_up2 + acc[2][...]
    part = part * vec[M5 : M5 + 1, :]
    if first:
        part = part + x2[...] + vec[B2 : B2 + 1, :] * vec[M5 : M5 + 1, :]
    out[...] = part.astype(out.dtype)
    dy[...] = grad.astype(dy.dtype)


def shift(count, step):
    return [(a, (a + step) % count) for a in range(count)]


def flip(count, step):
    return [(a, a ^ step) for a in range(count)]


def powers(count):
    return [1 << j for j in range(count.bit_length() - 1)]


def send(values, axis, pairs):
    return jax.tree.map(lambda v: lax.ppermute(v, axis, pairs), values)


def ring_pieces(own, axis):
    count = lax.axis_size(axis)
    pieces = [own]
    for _ in range(count - 1):
        pieces.append(send(pieces[-1], axis, shift(count, 1)))
    return pieces


def ring_total(parts, axis):
    count = lax.axis_size(axis)
    moving = parts[1]
    for r in range(2, count):
        moving = send(moving, axis, shift(count, 1))
        moving = (moving.astype(F32) + parts[r].astype(F32)).astype(BF16)
    return parts[0], send(moving, axis, shift(count, 1))


def gather_direct(own, axis):
    count = lax.axis_size(axis)
    return [own] + [send(own, axis, shift(count, r)) for r in range(1, count)]


def scatter_direct(parts, axis):
    count = lax.axis_size(axis)
    return parts[0].astype(F32) + sum(
        send(parts[r].astype(BF16), axis, shift(count, -r)).astype(F32) for r in range(1, count)
    )


def gather_flipped(own, axis):
    count = lax.axis_size(axis)
    return [own] + [send(own, axis, flip(count, j)) for j in range(1, count)]


def total_flipped(own, axis):
    terms = [v.astype(F32) for v in gather_flipped(own, axis)]
    while len(terms) > 1:
        terms = [terms[j] + terms[j + 1] for j in range(0, len(terms), 2)]
    return terms[0]


def halves(values, axis):
    half = values.shape[0] // 2
    low, high = values[:half], values[half:]
    upper = lax.axis_index(axis) == 1
    return jnp.where(upper, high, low), jnp.where(upper, low, high)


def pair_scatter(values):
    kept, sent = halves(values, "seq")
    return kept + send(sent.astype(BF16), "seq", flip(2, 1)).astype(F32)


def pair_gather(values, dim):
    other = send(values, "seq", flip(2, 1))
    upper = lax.axis_index("seq") == 1
    return jnp.concatenate([jnp.where(upper, other, values), jnp.where(upper, values, other)], axis=dim)


def place_blocks(blocks, axis):
    size = blocks[0].shape[0]
    out = jnp.zeros((size * len(blocks),) + blocks[0].shape[1:], blocks[0].dtype)
    index = lax.axis_index(axis)
    for j, block in enumerate(blocks):
        out = lax.dynamic_update_slice_in_dim(out, block, (index ^ j) * size, 0)
    return out


def total_twice(values, axis):
    for step in powers(lax.axis_size(axis)):
        values = values + send(values, axis, flip(lax.axis_size(axis), step))
    return values


class Chains:
    def __init__(self):
        self.chains, self.values, self.results = [], [], {}

    def add(self, chain):
        self.chains.append(chain)
        self.values.append(None)
        return len(self.chains) - 1

    def start(self, at):
        self.advance(at)

    def advance(self, at):
        try:
            self.values[at] = self.chains[at].send(self.values[at])
        except StopIteration as end:
            self.results[at] = end.value

    def step(self, skip=()):
        for at in range(len(self.chains)):
            if at not in self.results and at not in skip:
                self.advance(at)

    def live(self):
        return len(self.results) < len(self.chains)

    def done(self, at):
        return at in self.results

    def result(self, at):
        return self.results[at]

    def arrived(self):
        live = [self.values[at] for at in range(len(self.chains)) if at not in self.results]
        return jax.tree.leaves(live)

    def put(self, leaves):
        places = [at for at in range(len(self.chains)) if at not in self.results]
        structure = jax.tree.structure([self.values[at] for at in places])
        for at, value in zip(places, jax.tree.unflatten(structure, leaves)):
            self.values[at] = value


def seal(*values):
    return list(lax.optimization_barrier(values)) if values else []


def ring_steps(parts, axis):
    count = lax.axis_size(axis)
    moving = parts[1].astype(BF16)
    for r in range(2, count + 1):
        moving = yield send(moving, axis, shift(count, 1))
        if r < count:
            moving = (moving.astype(F32) + parts[r].astype(F32)).astype(BF16)
    return parts[0].astype(F32) + moving.astype(F32)


def line_kernel(shape, meta, *refs):
    inward, across, outward, both = shape
    inner = (meta[AT_T] == 1) | (meta[AT_T] == 2)
    count = (inward or outward) + inward + 2 * across + outward + both
    ins, outs = list(refs[:count]), list(refs[count:])
    add = lambda a, b: (a[...].astype(F32) + b[...].astype(F32)).astype(BF16)
    if inward or outward:
        first = ins.pop(0)
    if inward:
        outs.pop(0)[...] = add(ins.pop(0), first)
    if across:
        total = add(ins.pop(0), ins.pop(0))
        outs.pop(0)[...] = jnp.where(inner, total, ins.pop(0)[...]) if both else total
    if outward:
        outs.pop(0)[...] = jnp.where(inner, ins.pop(0)[...], first[...])


class Line:
    def __init__(self, meta, size):
        self.meta, self.size = meta, size
        self.parts, self.targets, self.outs = [], [], {}
        self.acc, self.total, self.at, self.moving = {}, {}, 0, []

    def add(self, array, block, target, out_block):
        self.parts.append((array, block))
        self.targets.append((target, out_block))

    def start(self):
        array, block = self.parts[self.at] if self.at < len(self.parts) else (None, None)
        inward, outward = array is not None, self.at - 2 in self.total
        pairs = [(0, 1), (3, 2)] * inward + [(1, 0), (2, 3)] * outward
        if inward and outward:
            mine = self.total[self.at - 2]
        elif inward:
            mine = array if array.shape[0] == self.size else array[block * self.size : (block + 1) * self.size]
        else:
            mine = self.total.get(self.at - 2)
        self.moving = [send(mine, "tensor", pairs)] if pairs else []
        across = self.at - 1 in self.acc
        if across:
            self.moving.append(send(self.acc[self.at - 1], "tensor", [(1, 2), (2, 1)]))
        self.shape = (inward, across, outward)

    def advance(self, moving):
        inward, across, outward = self.shape
        moving, at = list(moving), self.at
        first = moving.pop(0) if inward or outward else None
        second = moving.pop(0) if across else None
        both = across and at + 1 < len(self.parts)
        grid = 2
        rows = lambda block: pl.BlockSpec((self.size // grid, width), lambda b, m: (block * grid + b, 0))
        width = (second if first is None else first).shape[1]
        kind = sds((self.size, width), BF16)
        ins, outs, aliases = [], [], None
        if first is not None:
            ins.append((first, rows(0)))
        if inward:
            array, block = self.parts[at]
            ins.append((array, rows(block)))
            outs.append((kind, rows(0)))
        if across:
            ins += [(self.acc[at - 1], rows(0)), (second, rows(0))]
            outs.append((kind, rows(0)))
        if both:
            array, block = self.parts[at + 1]
            ins.append((array, rows(block)))
        if outward:
            ins.append((self.total[at - 2], rows(0)))
        count = len(ins)
        if outward:
            target, block = self.targets[at - 2]
            length = self.size * sum(t == target for t, _ in self.targets)
            outs.append((sds((length, width), BF16), rows(block)))
            if target in self.outs:
                ins.append((self.outs[target], pl.BlockSpec(memory_space=pl.ANY)))
                aliases = {count + 1: len(outs) - 1}

        def body(meta, *refs):
            line_kernel((inward, across, outward, both), meta, *refs[:count], *refs[len(ins) :])

        results = list(run_kernel(body, self.meta, ins, outs, grid=(grid,), us=3, aliases=aliases))
        if inward:
            self.acc[at] = results.pop(0)
        if across:
            self.total[at - 1] = results.pop(0)
        if outward:
            self.outs[self.targets[at - 2][0]] = results.pop(0)
        self.at, self.moving = at + 1, []
        if self.live():
            self.start()

    def live(self):
        return self.at < len(self.parts) + 2


def total_steps(value, axis):
    for step in powers(lax.axis_size(axis)):
        value = value + (yield send(value, axis, flip(lax.axis_size(axis), step)))
    return value


def adapter_steps(value, shared):
    groups, dp = lax.axis_size("tensor"), lax.axis_size("dp")
    pair, upper = flip(2, 1), lax.axis_index("seq") == 1
    kept, sent = halves(value, "seq")
    other = yield send(sent.astype(BF16), "seq", pair)
    value = kept + other.astype(F32)
    own, rest = value[:, :shared].astype(BF16), value[:, shared:].astype(BF16)
    for step in powers(groups):
        other = yield send(own, "tensor", flip(groups, step))
        own = (own.astype(F32) + other.astype(F32)).astype(BF16)
    value = jnp.concatenate([own, rest], axis=1)[None]
    for step in powers(dp):
        other = yield send(value, "dp", flip(dp, step))
        value = jnp.concatenate([value, other])
    other = yield send(value, "seq", pair)
    return jnp.concatenate([jnp.where(upper, other, value), jnp.where(upper, value, other)], axis=1)


def context_grad_steps(value):
    groups, dp = lax.axis_size("tensor"), lax.axis_size("dp")
    at_dp = lax.axis_index("dp")
    pair, second = flip(2, 1), lax.axis_index("seq") == 1
    kept, sent = halves(value, "seq")
    other = yield send(sent.astype(BF16), "seq", pair)
    value = kept + other.astype(F32)
    rows = value.shape[0] // dp
    parts = [lax.dynamic_slice_in_dim(value, (at_dp ^ j) * rows, rows, 0) for j in range(dp)]
    others = yield tuple(send(parts[j].astype(BF16), "dp", flip(dp, j)) for j in range(1, dp))
    value = (parts[0] + sum(other.astype(F32) for other in others)).astype(BF16)
    for step in powers(groups):
        other = yield send(value, "tensor", flip(groups, step))
        value = (value.astype(F32) + other.astype(F32)).astype(BF16)
    for step in powers(dp):
        other = yield send(value, "dp", flip(dp, step))
        upper = (at_dp & step) != 0
        value = jnp.concatenate([jnp.where(upper, other, value), jnp.where(upper, value, other)])
    other = yield send(value, "seq", pair)
    return jnp.concatenate([jnp.where(second, other, value), jnp.where(second, value, other)])


def weight_share():
    return 4 if lax.axis_size("dp") == 4 else 1


def weight_plan(rows, count):
    share, seq = weight_share(), lax.axis_size("seq")
    d, s = lax.axis_index("dp"), lax.axis_index("seq")
    slots = [(s ^ a) * share + ((d ^ b) if share > 1 else 0) for a in range(seq) for b in range(share)]
    total = rows * count
    cut = far_cut(total)
    half = [(0, 0, total, 0)]
    if share > 1:
        half += [(1, 0, total, 1), (2, 0, total, 2), (3, 0, cut, 3), (4, cut, total - cut, 3)]
    spans = half + [(len(half) + a, b, c, share + e) for a, b, c, e in half]
    plan = []
    for source, start, size, slot in spans:
        for weight in range(count):
            low, high = max(start, weight * rows), min(start + size, (weight + 1) * rows)
            if low < high:
                plan.append((source, weight, low - start, high - low, SLOTS + slot, low - weight * rows, rows))
    return plan, slots


def far_cut(total):
    return (total // 2 + 15) // 16 * 16


def rope_tables(grid_pos):
    sixth = HEAD_DIM // 6
    counts = [(HEAD_DIM - 4 * sixth) // 2, sixth, sixth]
    table = np.zeros((3, HEAD_DIM), np.float32)
    lane = 0
    for component, count in enumerate(counts):
        for pair in range(count):
            table[component, lane : lane + 2] = 10000.0 ** (-pair / count)
            lane += 2
    positions = grid_pos.astype(F32)
    angles = sum(positions[c][:, None] * table[c][None, :] for c in range(3))
    sign = np.where(np.arange(HEAD_DIM) % 2 == 0, -1.0, 1.0).astype(np.float32)
    return jnp.cos(angles), jnp.sin(angles) * sign[None, :]


def select_slot(table, index):
    return lax.dynamic_index_in_dim(table, index, 0, keepdims=False)


def spread(gradients, indices, slot_count):
    hits = (jnp.arange(slot_count)[:, None] == indices[None, :]).astype(F32)
    out = 0.0
    for latent in range(gradients.shape[0]):
        shape = (slot_count,) + (1,) * (gradients.ndim - 1)
        out = out + hits[:, latent].reshape(shape) * gradients[latent].astype(F32)[None]
    return out


def eight_rows(rows):
    return jnp.concatenate([jnp.stack(rows), jnp.zeros((8 - len(rows), rows[0].shape[0]), F32)])


def per_device(
    tokens,
    positions,
    time_emb,
    modulation,
    context,
    adapter_index,
    self_qkv,
    self_bias,
    self_gain,
    self_out,
    cross_qkv,
    cross_bias,
    cross_gain,
    cross_out,
    cross_norm_gain,
    cross_norm_bias,
    ffn_in,
    ffn_bias,
    ffn_out,
    out_bias,
    col_down,
    col_up,
    ffn1_down,
    ffn1_up,
    row_down,
    row_up,
    ffn2_down,
    ffn2_up,
    out_grad,
):
    groups = lax.axis_size("tensor")
    seq = lax.axis_size("seq")
    i, s = lax.axis_index("tensor"), lax.axis_index("seq")
    tl, d = tokens.shape[1:]
    tc = tl // groups
    ctx_len = context.shape[0]
    width = self_qkv.shape[2]
    hc = width // HEAD_DIM
    ff = ffn_in.shape[1]
    slots, rank = col_down.shape[0], col_down.shape[3]
    share = weight_share()
    slice_rows = width // (share * seq)
    plan, slot_list = weight_plan(slice_rows, 3)
    part_at = s * share + (lax.axis_index("dp") if share > 1 else 0)
    meta = jnp.stack([jnp.asarray(v, jnp.int32) for v in [i, s, adapter_index[0], part_at] + slot_list])
    tok, og = tokens[0], out_grad[0]
    block = pl.BlockSpec
    hbm = pl.BlockSpec(memory_space=pl.ANY)
    pair = flip(seq, 1)

    def table(array, *place, rows=1):
        if not place:
            return (array, block((1,) + array.shape[1:], lambda *a: (a[-1][ADAPTER],) + (0,) * (array.ndim - 1)))
        return (
            array,
            block(
                (1, rows) + array.shape[2:],
                lambda *a: (a[-1][ADAPTER], place[0](a[-1]) if callable(place[0]) else place[0], 0, 0),
            ),
        )

    col_dn, row_dn = jnp.swapaxes(col_down, 2, 3), jnp.swapaxes(row_down, 2, 3)
    feed_tables = [
        table(jnp.swapaxes(ffn1_down, 1, 2)),
        table(ffn1_up),
        table(jnp.swapaxes(ffn2_down, 1, 2)),
        table(ffn2_up),
    ]

    shard_at = lambda b, m: (m[PART], 0)
    (slices,) = run_kernel(
        pack_kernel,
        meta,
        [
            (self_out, block((slice_rows, d), shard_at)),
            (cross_qkv, block((1, slice_rows * groups, width), lambda b, m: (0, m[PART], 0))),
            (cross_out, block((slice_rows, d), shard_at)),
        ],
        [(sds((3 * slice_rows, d), BF16), whole((3 * slice_rows, d)))],
        us=1.5,
    )
    by_group = gather_direct(slices, "tensor")[1:]

    is_key = s == 0
    ctx_w = (cross_qkv, block((1, d, width), lambda b, m: (1 + m[AT_S], 0, 0)))
    ctx_up, ctx_dn = table(col_up, lambda m: 4 + m[AT_S]), table(col_dn, lambda m: 4 + m[AT_S])
    low_rows = ctx_len + 4 * rank
    ctx_pre, ctx_low, ctx_ssq, ctx_lat_t = run_kernel(
        functools.partial(context_kernel, groups),
        meta,
        [
            (context, whole(context.shape)),
            ctx_w,
            ctx_up,
            ctx_dn,
            (cross_bias, whole(cross_bias.shape)),
            (cross_gain, whole(cross_gain.shape)),
            table(col_up, 3),
            table(row_dn, 0, rows=2),
        ],
        [
            (sds((ctx_len, width), F32), whole((ctx_len, width))),
            (sds((low_rows, width), BF16), whole((low_rows, width))),
            (sds((8, tl), F32), whole((8, tl))),
            (sds((rank, ctx_len), BF16), whole((rank, ctx_len))),
        ],
        us=6,
        after=[slices],
    )
    cos, sin = rope_tables(positions[:, 0, :])
    rows_d = block((tc, d), lambda b, m: (b, 0))
    rows_w = block((tc, width), lambda b, m: (b, 0))
    rows_h = block((tc, HEAD_DIM), lambda b, m: (b, 0))
    lanes_8 = block((8, tc), lambda b, m: (0, b))
    self_tables = [table(col_up, 0, rows=3), table(col_dn, 0, rows=3)]
    y1, lat_t, pre_q, pre_k, raw_q, kv, ssq, vec = run_kernel(
        functools.partial(qkv_kernel, hc),
        meta,
        [
            (tok, rows_d),
            (modulation, whole(modulation.shape)),
            (time_emb[0], whole(modulation.shape)),
            (out_bias, whole(out_bias.shape)),
            (cross_norm_gain[None], whole((1, d))),
            (cross_norm_bias[None], whole((1, d))),
            (self_qkv, whole(self_qkv.shape)),
        ]
        + self_tables
        + [
            (self_bias, whole(self_bias.shape)),
            (self_gain, whole(self_gain.shape)),
            (cos, rows_h),
            (sin, rows_h),
            (ctx_ssq, lanes_8),
        ],
        [
            (sds((tl, d), BF16), rows_d),
            (sds((3 * rank, tl), BF16), block((3 * rank, tc), lambda b, m: (0, b))),
            (sds((tl, width), BF16), rows_w),
            (sds((tl, width), BF16), rows_w),
            (sds((tl, width), BF16), rows_w),
            (sds((tl, 2 * width), BF16), block((tc, 2 * width), lambda b, m: (b, 0))),
            (sds((8, tl), F32), lanes_8),
            (sds((16, d), F32), whole((16, d))),
        ],
        grid=(groups,),
        scratch=[pltpu.VMEM((3 * rank, 3 * width), BF16)],
        us=15,
    )
    kv_sib = send(kv, "seq", pair)
    *first_steps, last_step = powers(groups)
    for step in first_steps:
        ssq = ssq + send(ssq, "tensor", flip(groups, step))
    ssq, *by_group = seal(ssq, *by_group)
    (by_group,) = run_kernel(
        stack_kernel,
        meta,
        [(a, whole(a.shape)) for a in by_group],
        [(sds((groups - 1,) + slices.shape, BF16), whole((groups - 1,) + slices.shape))],
        us=2,
    )
    ssq, by_group = seal(ssq, by_group)
    along = [send(by_group, "dp", flip(share, 1)), send(by_group, "dp", flip(share, 2))] if share > 1 else []
    st_own = lax.rsqrt((ssq + send(ssq, "tensor", flip(groups, last_step))) / d + EPS)
    st_sib = send(st_own, "seq", pair)
    by_group_sib = send(by_group, "seq", pair)
    st_sib, by_group_sib, kv_sib = seal(st_sib, by_group_sib, kv_sib)
    ctx_low, _ = seal(ctx_low, st_own)
    ctx_pieces = gather_direct(ctx_low, "tensor")

    all_8 = whole((8, tl))
    turned = lambda r, m: lax.rem(m[AT_T] + r, groups)
    kv_at = lambda lane: block((tl, HEAD_DIM), lambda h, r, m: (0, lane + h))
    own_rows = block((tc, HEAD_DIM), lambda h, r, m: (0, h))
    *blocks, mixed, lses, kn, knt, vn, qn_self = run_kernel(
        functools.partial(attention_kernel, groups),
        meta,
        [
            (raw_q, block((tc, HEAD_DIM), lambda h, r, m: (turned(r, m), h))),
            (st_own, block((8, tc), lambda h, r, m: (0, turned(r, m)))),
            (st_own, all_8),
            (st_sib, all_8),
            (kv, kv_at(0)),
            (kv_sib, kv_at(0)),
            (kv, kv_at(hc)),
            (kv_sib, kv_at(hc)),
        ],
        [(sds((tc, width), BF16), own_rows)] * groups
        + [
            (sds((tl, width), BF16), block((tc, HEAD_DIM), lambda h, r, m: (r, h))),
            (sds((8 * hc, tl), F32), block((8, tc), lambda h, r, m: (h, r))),
            (sds((2 * tl, width), BF16), block((2 * tl, HEAD_DIM), lambda h, r, m: (0, h))),
            (sds((width, 2 * tl), BF16), block((HEAD_DIM, 2 * tl), lambda h, r, m: (h, 0))),
            (sds((2 * tl, width), BF16), block((2 * tl, HEAD_DIM), lambda h, r, m: (0, h))),
            (sds((tl, width), BF16), block((tc, HEAD_DIM), lambda h, r, m: (r, h))),
        ],
        grid=(hc, groups),
        scratch=[pltpu.VMEM((HEAD_DIM, 2 * tl), BF16)],
        us=25,
        after=[by_group],
    )
    tied = seal(*blocks, *along, *ctx_pieces[1:])
    blocks, along, ctx_pieces[1:] = tied[:groups], tied[groups : groups + len(along)], tied[groups + len(along) :]
    os_pieces = [send(a, "tensor", shift(groups, r)) if r else a for r, a in enumerate(blocks)]
    weight_parts = [by_group] + along
    if share > 1:
        middle = far_cut(by_group.shape[1])
        weight_parts += [
            send(along[1][:, :middle], "dp", flip(share, 1)),
            send(along[0][:, middle:], "dp", flip(share, 2)),
        ]
    tied = seal(*os_pieces[1:], *along, *ctx_pieces)
    os_pieces[1:], tied = tied[: groups - 1], tied[groups - 1 :]
    weight_parts[1 : 1 + len(along)], ctx_pieces = tied[: len(along)], tied[len(along) :]
    weight_parts = weight_parts + [by_group_sib] + [send(p, "seq", pair) for p in weight_parts[1:]]
    ctx_sib = [send(p, "seq", pair) for p in ctx_pieces]

    vspec = whole(vec.shape)
    own_block = block((tc, d), lambda b, m: (m[AT_T], 0))
    weight_scratch = [
        pltpu.VMEM((groups, width, d), BF16),
        pltpu.VMEM((groups - 1, d, width), BF16),
        pltpu.VMEM((groups, width, d), BF16),
    ]
    sems = pltpu.SemaphoreType.DMA((len(plan) * groups + 2,))
    shared = [
        table(row_up),
        table(col_dn, 3),
        *[(p, whole(p.shape)) for p in ctx_pieces + ctx_sib],
        (st_own, all_8),
        (st_sib, all_8),
        (self_out, hbm),
        (cross_qkv, block((1, d, width), lambda b, m: (0, 0, 0))),
        (cross_out, hbm),
    ] + [(p, hbm) for p in weight_parts]
    whole_of = lambda shape, dtype: (sds(shape, dtype), whole(shape))
    y2, x2, x1, y3, qn, qc, oc, os_all, lse_c, lats = run_kernel(
        functools.partial(cross_kernel, groups, hc, plan),
        meta,
        [(p, whole(p.shape)) for p in os_pieces] + [(tok, own_block), (vec, vspec)] + shared,
        [
            whole_of((tc, d), BF16),
            whole_of((tc, d), F32),
            whole_of((tc, d), F32),
            whole_of((tc, d), BF16),
            whole_of((tc, d), BF16),
            whole_of((tc, d), F32),
            whole_of((tc, d), BF16),
            whole_of((tc, d), BF16),
            whole_of((16, tc), F32),
            whole_of((3 * rank, tc), BF16),
        ],
        scratch=weight_scratch + [sems],
        us=20,
    )

    tiles = [(0, min(256, ff))] + [(a, min(1024, ff - a)) for a in range(256, ff, 1024)]
    w1t = ffn_in.T
    y2_pieces = ring_pieces(y2, "tensor")
    feed_bias = ffn_bias.astype(F32)[None]
    feed_out, dys, acc = None, [], None
    for r in range(groups):
        place = block((tc, d), lambda b, m, r=r: (lax.rem(m[AT_T] + groups - r, groups), 0))
        ins = [(y2_pieces[r], whole((tc, d))), (og, place), (vec, vspec), (feed_bias, whole(feed_bias.shape))]
        ins += feed_tables + [(w1t, hbm), (ffn_out, hbm)]
        if r == 0:
            ins += [(x2, whole((tc, d)))]
        else:
            ins += [(a, whole(a.shape)) for a in acc] + [(feed_out, hbm)]
        feed_out, dy, *acc = run_kernel(
            functools.partial(feed_kernel, tiles, r == 0),
            meta,
            ins,
            [(sds((tl, d), BF16), place), whole_of((tc, d), F32 if r == 0 else BF16)]
            + [whole_of((rank, n), F32) for n in (ff, d, d, ff)],
            scratch=[pltpu.VMEM((ff, d), BF16), pltpu.VMEM((ff, d), BF16), pltpu.SemaphoreType.DMA((2, len(tiles)))],
            us=18,
            aliases={15: 0} if r else None,
        )
        dys.append(dy)
    g_up1, g_dn1, g_up2, g_dn2 = acc

    dy_own, dy_in = ring_total(dys, "tensor")
    feed_first = [feed_out[r * tc : (r + 1) * tc] for r in range(2)]
    feed_out, dy_in, *feed_first = seal(feed_out, dy_in, *feed_first)
    line = Line(meta, tc) if groups == 4 else None
    if line:
        for r in range(groups):
            line.add(*((feed_first[r], 0) if r < 2 else (feed_out, r)), "output", r)
        line.start()
    else:
        result = lax.psum(feed_out, "tensor")
    *dos, dx1, g_own, g_oth, g_rup, g_split, g_cqdn = run_kernel(
        functools.partial(cross_back_kernel, groups, hc, plan),
        meta,
        [(dy_own, whole((tc, d))), (dy_in, whole((tc, d))), (og, own_block)]
        + [(a, whole(a.shape)) for a in (x2, x1, y3, qn, qc, oc, os_all, lse_c, lats)]
        + [(vec, vspec)]
        + shared,
        [whole_of((tc, HEAD_DIM), BF16)] * groups
        + [whole_of((tc, width - HEAD_DIM), BF16)] * groups
        + [
            whole_of((tc, d), F32),
            whole_of((groups, ctx_len, width), BF16),
            whole_of((groups, ctx_len, width), BF16),
            whole_of((2 * rank, d), F32),
            whole_of((groups, 3 * rank, width), F32),
            whole_of((rank, d), F32),
        ],
        scratch=weight_scratch + [pltpu.VMEM((tc, d), F32), sems],
        us=26,
    )

    back_shift = lambda arrays: [send(a, "tensor", shift(groups, -r)) if r else a for r, a in enumerate(arrays)]
    moving = lambda: line.moving if line else []
    chains = Chains()
    dos[0], g_oth, g_cqdn, *arrived_line = seal(dos[0], g_oth, g_cqdn, *moving())
    dos_first = back_shift(dos[:groups])
    packed = jnp.concatenate([g_cqdn, g_dn1, g_rup[:rank], g_rup[rank:], g_up2, g_up1, g_dn2], axis=1)
    early_at = chains.add(adapter_steps(packed, 5 * d))
    g_oth = send(g_oth, "seq", pair)
    chains.step()
    g_oth, *dos_first = seal(g_oth, *dos_first)
    to_group = jnp.concatenate([g_own.astype(F32) + g_oth.astype(F32), g_split], axis=1)
    dos_rest = back_shift(dos[groups:])
    group_at = chains.add(ring_steps([to_group[r] for r in range(groups)], "tensor"))
    chains.step()

    back, dkv_in = [], []
    for h in range(hc):
        grads = dos_first if h == 0 else dos_rest
        lane = 0 if h == 0 else h - 1
        if h:
            if h == 1:
                tied = seal(*dos_rest, *chains.arrived(), back[-1][0], back[-1][2])
                dos_rest = tied[: len(dos_rest)]
                chains.put(tied[len(dos_rest) : -2])
                chains.step()
                if line:
                    line.advance(arrived_line)
            else:
                tied = seal(back[-1][0], back[-1][2])
            dkv_in.append(send(tied[-1], "seq", pair))
            grads = dos_rest
        back.append(
            run_kernel(
                functools.partial(attention_back_kernel, groups, h == 0),
                meta,
                [
                    (qn_self, block((tc, HEAD_DIM), lambda r, m, h=h: (r, h))),
                    (st_own, block((8, tc), lambda r, m: (0, turned(r, m)))),
                    (st_own, all_8),
                    (st_sib, all_8),
                    (kn, block((2 * tl, HEAD_DIM), lambda r, m, h=h: (0, h))),
                    (knt, block((HEAD_DIM, 2 * tl), lambda r, m, h=h: (h, 0))),
                    (vn, block((2 * tl, HEAD_DIM), lambda r, m, h=h: (0, h))),
                    (mixed, block((tc, HEAD_DIM), lambda r, m, h=h: (r, h))),
                    (lses, block((8, tc), lambda r, m, h=h: (h, r))),
                ]
                + [(g, block((tc, HEAD_DIM), lambda r, m, lane=lane: (0, lane))) for g in grads]
                + ([(a, all_8) for a in back[-1][3:]] if h else []),
                [
                    (sds((tl, HEAD_DIM), F32), block((tc, HEAD_DIM), lambda r, m: (turned(r, m), 0))),
                    whole_of((tl, 2 * HEAD_DIM), F32),
                    whole_of((tl, 2 * HEAD_DIM), BF16),
                    whole_of((8, tl), F32),
                    whole_of((8, tl), F32),
                ],
                grid=(groups,),
                scratch=[
                    pltpu.VMEM((2 * tl, HEAD_DIM), F32),
                    pltpu.VMEM((2 * tl, HEAD_DIM), F32),
                    pltpu.VMEM((tc, HEAD_DIM), BF16),
                ],
                us=12.5,
                after=list(tied[-2:-1]) if h else [],
            )
        )
    dq, dkv, dkv_out = zip(*[b[:3] for b in back])
    stat, cross = back[-1][3:]
    last_dkv = dkv_out[-1]
    stat, cross, last_dkv, *tied = seal(stat, cross, last_dkv, *chains.arrived(), *moving())
    count = len(chains.arrived())
    chains.put(tied[:count])
    arrived_line = tied[count:]
    dkv_in.append(send(last_dkv, "seq", pair))
    stat = stat + send(cross, "seq", pair)
    chains.step([group_at])
    for step in powers(groups):
        (other,) = seal(send(stat, "tensor", flip(groups, step)))
        stat = stat + other
    st_back = st_own * st_own * st_own * stat / d
    st_back, *tied = seal(st_back, *chains.arrived())
    chains.put(tied)
    chains.step()
    if line:
        line.advance(arrived_line)

    q_parts, late = [], None
    calls = 2
    for call in range(calls):
        steps = groups // calls
        in_d = block((tc, d), lambda b, m, c=call * steps: (c + b, 0))
        in_w = block((tc, width), lambda b, m, c=call * steps: (c + b, 0))
        in_h = block((tc, HEAD_DIM), lambda b, m, c=call * steps: (c + b, 0))
        in_2h = block((tc, 2 * HEAD_DIM), lambda b, m, c=call * steps: (c + b, 0))
        in_8 = block((8, tc), lambda b, m, c=call * steps: (0, c + b))
        size = (rank, 3 * (d + width))
        part, late = run_kernel(
            functools.partial(qkv_back_kernel, hc, call),
            meta,
            [(a, in_h) for a in dq]
            + [(a, in_2h) for a in list(dkv) + dkv_in]
            + [
                (pre_q, in_w),
                (pre_k, in_w),
                (st_own, in_8),
                (st_back, in_8),
                (self_gain, whole(self_gain.shape)),
                (cos, in_h),
                (sin, in_h),
                (self_qkv, hbm),
            ]
            + self_tables
            + [
                (tok, in_d),
                (vec, vspec),
                (y1, in_d),
                (lat_t, block((3 * rank, tc), lambda b, m, c=call * steps: (0, c + b))),
                (dx1, whole((tc, d))),
            ]
            + ([(late, whole(size))] if call else []),
            [(sds((steps * tc, d), BF16), block((tc, d), lambda b, m: (b, 0))), whole_of(size, F32)],
            grid=(steps,),
            scratch=[
                pltpu.VMEM((3 * rank, 3 * width), BF16),
                pltpu.VMEM(self_qkv.shape, BF16),
                pltpu.SemaphoreType.DMA(()),
            ],
            us=14,
        )
        q_parts.append(part)
        if line:
            for r in range(steps):
                line.add(part, r, "input_grad", call * steps + r)
        late, *tied = seal(late, *chains.arrived(), *moving())
        count = len(chains.arrived())
        chains.put(tied[:count])
        chains.step()
        if call == 0:
            to_group = chains.result(group_at)
            g_ctx, split = to_group[:ctx_len], to_group[ctx_len:]
            ctx_gain = jnp.where(is_key, cross_gain[1:2].astype(F32), 1.0)
            ctx_stat = jnp.sum(g_ctx * ctx_gain * ctx_pre, axis=1)
            stat_at = chains.add(total_steps(ctx_stat, "tensor"))
            chains.advance(stat_at)
        if line:
            line.advance(tied[count:])
    while not chains.done(stat_at):
        chains.put(seal(*chains.arrived()))
        chains.step()
    ctx_stat = chains.result(stat_at)

    ctx_inverse = jnp.concatenate([st_own[2, j * tc : j * tc + ctx_len // groups] for j in range(groups)])
    ctx_cubed = ctx_inverse * ctx_inverse * ctx_inverse * ctx_stat / d
    d_key = ctx_inverse[:, None] * ctx_gain * g_ctx - ctx_pre * ctx_cubed[:, None]
    d_ctx = jnp.where(is_key, d_key, g_ctx).astype(BF16)
    ctx_part, g_ctx_up, g_ctx_dn = run_kernel(
        context_back_kernel,
        meta,
        [
            (context, whole(context.shape)),
            ctx_w,
            ctx_up,
            ctx_dn,
            (ctx_lat_t, whole(ctx_lat_t.shape)),
            (d_ctx, whole(d_ctx.shape)),
        ],
        [whole_of((ctx_len, d), F32), whole_of((rank, width), F32), whole_of((rank, d), F32)],
        us=6,
        after=[line.acc[max(line.acc)]] if line else [],
    )

    pick = lambda g: [jnp.where(is_key, g, 0.0), jnp.where(is_key, 0.0, g)]
    late = jnp.concatenate(
        [late[:, : 3 * d]]
        + pick(g_ctx_dn)
        + [late[:, 3 * d :], split[:rank]]
        + pick(g_ctx_up)
        + [split[rank : 2 * rank], split[2 * rank :]]
        + [jnp.broadcast_to(adapter_index[0].astype(F32) / seq, (rank, HEAD_DIM))],
        axis=1,
    )
    ctx_at = chains.add(context_grad_steps(ctx_part))
    late_at = chains.add(adapter_steps(late, 5 * d))
    chains.advance(ctx_at)
    chains.advance(late_at)
    while line and line.at < len(line.parts):
        tied = seal(*chains.arrived(), *moving())
        count = len(chains.arrived())
        chains.put(tied[:count])
        chains.step()
        line.advance(tied[count:])
    while line and line.live():
        line.advance(line.moving)
    while chains.live():
        chains.put(seal(*chains.arrived()))
        chains.step()
    early, late, context_grad = chains.result(early_at), chains.result(late_at), chains.result(ctx_at).astype(F32)
    if line:
        result, input_grad = line.outs["output"], line.outs["input_grad"]
    else:
        input_grad = lax.psum(jnp.concatenate(q_parts), "tensor")

    indices = jnp.round(late[:, 0, -1].astype(F32)).astype(jnp.int32)
    early, late = spread(early, indices, slots), spread(late[:, :, :-HEAD_DIM], indices, slots)
    cut = lambda grads, start, size, count: [
        grads[:, :, start + j * size : start + (j + 1) * size] for j in range(count)
    ]
    wide, feed = cut(early, 0, d, 5), cut(early, 5 * d, ff, 2)
    wide_late, narrow = cut(late, 0, d, 5), cut(late, 5 * d, width, 8)
    swap = lambda a: jnp.swapaxes(a, -1, -2)
    return (
        result[None],
        input_grad[None],
        context_grad,
        swap(jnp.stack(wide_late[:3] + wide[:1] + wide_late[3:], axis=1)),
        jnp.stack(narrow[:6], axis=1),
        swap(wide[1]),
        feed[0],
        swap(jnp.stack(narrow[6:], axis=1)),
        jnp.stack(wide[2:4], axis=1),
        swap(feed[1]),
        wide[4],
    )


def solution(mesh):
    placed = (
        P("dp", "seq", None),
        P(None, "dp", "seq"),
        P("dp", None, None),
        P(),
        P(),
        P("dp"),
        P(None, None, "tensor"),
        P(None, "tensor"),
        P(None, "tensor"),
        P("tensor", None),
        P(None, None, "tensor"),
        P(None, "tensor"),
        P(None, "tensor"),
        P("tensor", None),
        P(),
        P(),
        P(None, "tensor"),
        P("tensor"),
        P("tensor", None),
        P(),
        P(),
        P(None, None, None, "tensor"),
        P(),
        P(None, None, "tensor"),
        P(None, None, "tensor", None),
        P(),
        P(None, "tensor", None),
        P(),
        P("dp", "seq", None),
    )
    return jax.shard_map(
        per_device,
        mesh=mesh,
        in_specs=placed,
        out_specs=(
            P("dp", "seq", None),
            P("dp", "seq", None),
            P(),
            P(),
            P(None, None, None, "tensor"),
            P(),
            P(None, None, "tensor"),
            P(None, None, "tensor", None),
            P(),
            P(None, "tensor", None),
            P(),
        ),
        check_vma=False,
    )
```
